128 devices in a mesh: graph: 32 (over z, y, core), mp: 4 (over x).
Axes of the slice: x: 4, y: 4, z: 4, core: 2. Of those that a mesh axis runs over, the one named last changes fastest.
Arguments:
- node_features: bfloat16 [65536, 512], P('graph'), may hold values from -6 to 6
- w_qkv: bfloat16 [3, 512, 512], P(None, None, 'mp'), may hold values from -0.25 to 0.25
- w_out: bfloat16 [512, 512], P('mp'), may hold values from -0.25 to 0.25
- head_scale: float32 [8], P('mp'), may hold values from 1 to 100
- norm_gain: float32 [512], replicated, may hold values from 0.1 to 1.9
- router: bfloat16 [512, 64], replicated, may hold values from -0.5 to 0.5
- w_gate: bfloat16 [64, 512, 2048], P('graph', None, 'mp'), may hold values from -0.25 to 0.25
- w_up: bfloat16 [64, 512, 2048], P('graph', None, 'mp'), may hold values from -0.25 to 0.25
- w_down: bfloat16 [64, 2048, 512], P('graph', 'mp'), may hold values from -0.25 to 0.25
- neighbor_blocks: int32 [512, 12], P('graph'), may hold values from 0 to 511, as said below
- expert_ids: int32 [65536, 1], P('graph'), may hold values from 0 to 63; in each aligned block of 2048 rows (0 to 2047, 2048 to 4095, ...) at most 96 rows name the same one
Outputs:
- attn_out: bfloat16 [65536, 512], P('graph', 'mp')
- layer_out: bfloat16 [65536, 512], P('graph', 'mp')
The draws below stay inside these ranges and needn't reach their ends.
Inputs may be any that keep to these rules, and one draw needn't show every extreme that they name: `neighbor_blocks`: row b lists distinct blocks: b itself, 3 other blocks of the same index of graph (blocks of part p are p * 16 to p * 16 + 15), then 8 blocks of other parts. Among all rows of one part, at most 2 distinct blocks come from any one other part, and every part reaches 2 from some other part. `expert_ids`: among the rows of one index of graph, at most 96 name one expert, a bound that some block reaches.
All inputs are finite; a program needn't handle non-finite values.
Results may differ from the reference program's by a relative error of at most 0.012.
The reference program's roundings to bfloat16 on the way count: a program that leaves them out, or rounds other values in their place, can miss the bound.
Values may be sent and summed in bfloat16 or wider, within the bound.
No kernel may reach another device: no remote copies, remote signals or barrier semaphores. Data moves between devices by JAX's collectives and lax.ppermute only.
A program may use at most 128 MiB of HBM per device.

```python
import math
import jax
import jax.numpy as jnp
import numpy as np
from jax import lax

HEADS = 8
HEAD_DIM = 64
D = 512
FF = 2048
EXPERTS = 64
ROWS_BLK = 128
BLK_DEV = 16
LOCALS = 3
HALO_REF = 8
NBR = 12
NODE_DEV = 2048
BLOCKS = 512
TOKENS = 65536
CAP_E = 96


def draw_head_scale(key, part):
    key = jax.random.fold_in(key, 7)
    spread = jax.random.uniform(key, (HEADS,), jnp.float32)
    return jnp.exp(spread * jnp.log(8.0))


def draw_neighbor_blocks(key, part):
    key = jax.random.fold_in(key, 11)
    parts = BLOCKS // BLK_DEV
    peers = parts - 1
    key_extra, key_first, key_step, key_local = jax.random.split(key, 4)
    extra = jax.random.randint(key_extra, (parts, peers), 0, 2).astype(jnp.int32)
    extra = extra.at[:, 0].set(1)
    first = jax.random.randint(key_first, (parts, peers), 0, BLK_DEV).astype(jnp.int32)
    stride = jax.random.randint(key_step, (parts, peers), 1, BLK_DEV).astype(jnp.int32)
    second = (first + stride) % BLK_DEV
    device = jnp.arange(parts, dtype=jnp.int32)[:, None]
    owner = (device + 1 + jnp.arange(peers, dtype=jnp.int32)[None, :]) % parts
    listed = jnp.stack([owner * BLK_DEV + first, owner * BLK_DEV + second], axis=-1).reshape(parts, 2 * peers)
    valid = jnp.stack([jnp.ones_like(extra), extra], axis=-1).reshape(parts, 2 * peers)
    ranked = jnp.cumsum(valid, axis=1) - valid
    number = jnp.sum(valid, axis=1)
    target = jnp.where(valid == 1, ranked, 2 * peers)
    compact = jnp.zeros((parts, 2 * peers + 1), jnp.int32).at[device, target].set(listed)
    spots = jnp.arange(BLK_DEV, dtype=jnp.int32)[:, None] * HALO_REF + jnp.arange(HALO_REF, dtype=jnp.int32)[None, :]
    spots = spots[None, :, :] % number[:, None, None]
    remote = compact[jnp.arange(parts, dtype=jnp.int32)[:, None, None], spots]
    local_keys = jax.random.split(key_local, parts * BLK_DEV)
    shifts = jax.vmap(lambda sub: jax.random.permutation(sub, BLK_DEV - 1)[:LOCALS])(local_keys)
    shifts = shifts.astype(jnp.int32).reshape(parts, BLK_DEV, LOCALS)
    within = jnp.arange(BLK_DEV, dtype=jnp.int32)[None, :, None]
    others = (within + 1 + shifts) % BLK_DEV + device[:, :, None] * BLK_DEV
    itself = device * BLK_DEV + jnp.arange(BLK_DEV, dtype=jnp.int32)[None, :]
    rows = jnp.concatenate([itself[:, :, None], others, remote], axis=-1)
    return rows.reshape(BLOCKS, NBR).astype(jnp.int32)


def level_of(own_key, shape, cuts, least, high):
    loudness, own = 1.0, jax.random.fold_in(own_key, 6)
    for dim, blocks in cuts:
        steps = jnp.exp(jax.random.uniform(jax.random.fold_in(own, dim), (blocks,), jnp.float32, least / len(cuts), high / len(cuts)))
        loudness = loudness * jnp.repeat(steps, shape[dim] // blocks).reshape([-1 if axis == dim else 1 for axis in range(len(shape))])
    return loudness


def routed_block(rng, own, number, rows, amount, top, reach, skew):
    sequence = jax.random.permutation(rng, amount)
    crowded, common = shares(amount, rows * top, reach, skew, True), shares(amount, rows * top, reach, skew, False)
    places = jnp.arange(amount)

    def named(lengths, rotation):
        used = int((lengths > 0).sum())
        fixed = max(1, used // 4)
        moved = fixed + (places - fixed + rotation * (used - fixed)) % max(1, amount - fixed)
        return jnp.zeros((amount,), jnp.int32).at[sequence[jnp.where(places < fixed, places, moved)]].set(jnp.asarray(lengths, jnp.int32))

    lengths = jnp.where(number % 4 == 0, named(crowded, number // 4), named(common, number - number // 4 - 1))
    mixed = jax.random.permutation(jax.random.fold_in(own, 3), amount)
    source_of, taker = mixed[0:amount // 2 * 2:2], mixed[1:amount // 2 * 2:2]
    margin = jnp.minimum(lengths[source_of] - 1, reach - lengths[taker]) // 2
    margin = jnp.where((source_of == sequence[0]) | (taker == sequence[0]) | (lengths[taker] == 0), 0, jnp.maximum(margin, 0))
    moved = jax.random.randint(jax.random.fold_in(own, 4), (amount // 2,), 0, 1 << 20) % (margin + 1)
    lengths = lengths.at[source_of].add(-moved).at[taker].add(moved)
    members = jnp.searchsorted(jnp.cumsum(lengths), jnp.arange(rows * top), side="right").astype(jnp.int32)
    table = members.reshape(top, rows).T
    table = table[jax.random.permutation(jax.random.fold_in(own, 1), rows)]
    rotation = jax.random.randint(jax.random.fold_in(own, 2), (rows, 1), 0, top)
    return jnp.take_along_axis(table, (jnp.arange(top)[None, :] + rotation) % top, axis=1)


def shares(amount, total, limit, lean, full):
    portions = [(1 << 20) // math.isqrt(rank ** lean) + 1 for rank in range(1, amount + 1)]
    largest = limit if full else min(limit, max(-(-total // amount), total * portions[0] // sum(portions)))
    least = 1 if total - largest >= amount - 1 else 0
    given, spare = [largest] + [least] * (amount - 1), total - largest - least * (amount - 1)
    while spare > 0:
        free = [i for i in range(1, amount) if given[i] < largest] or [i for i in range(1, amount) if given[i] < limit]
        whole, budget = sum([portions[i] for i in free]), spare
        for i in free:
            addition = min(limit - given[i], max(1, budget * portions[i] // whole), spare)
            given[i] = given[i] + addition
            spare = spare - addition
    return np.array(given)


def gaussian(rng, shape, deviation, most, cuts=(), held_as=jnp.bfloat16):
    array = deviation * jax.random.normal(rng, shape, jnp.float32)
    if cuts:
        array = array * level_of(rng, shape, cuts, -0.22, 0.18)
    return jnp.clip(array, -most, most).astype(held_as)


def setup_inputs(seed: int = 0) -> dict:
    splits = jax.random.split(jax.random.key(seed), 12)
    node_features = gaussian(splits[0], (TOKENS, D), 1.0, 6.0, ((0, 32),))
    w_qkv = gaussian(splits[1], (3, D, D), D ** -0.5, 0.25, ((2, 4),))
    w_out = gaussian(splits[2], (D, D), D ** -0.5, 0.25, ((0, 4),))
    head_scale = draw_head_scale(jax.random.fold_in(splits[11], 71), 0)
    norm_gain = jnp.clip(1.0 + 0.18 * jax.random.normal(splits[4], (D,), jnp.float32), 0.1, 1.9)
    router = gaussian(splits[5], (D, EXPERTS), (D // 4) ** -0.5, 0.5)
    w_gate = gaussian(splits[6], (EXPERTS, D, FF), D ** -0.5, 0.25, ((0, 32), (2, 4)))
    w_up = gaussian(splits[7], (EXPERTS, D, FF), D ** -0.5, 0.25, ((0, 32), (2, 4)))
    w_down = gaussian(splits[8], (EXPERTS, FF, D), (FF // 4) ** -0.5, 0.25, ((0, 32), (1, 4)))
    neighbor_blocks = draw_neighbor_blocks(jax.random.fold_in(splits[11], 71), 0)
    expert_ids_keys = jax.random.split(jax.random.fold_in(splits[10], 1), TOKENS // NODE_DEV)
    expert_ids_turns = jax.random.permutation(jax.random.fold_in(splits[10], 3), TOKENS // NODE_DEV)
    expert_ids = jax.vmap(lambda own, number: routed_block(jax.random.fold_in(splits[10], 2), own, number, NODE_DEV, EXPERTS, 1, CAP_E, 2))(expert_ids_keys, expert_ids_turns).reshape((TOKENS, 1))
    return dict(node_features=node_features, w_qkv=w_qkv, w_out=w_out, head_scale=head_scale, norm_gain=norm_gain, router=router, w_gate=w_gate, w_up=w_up, w_down=w_down, neighbor_blocks=neighbor_blocks, expert_ids=expert_ids)


slab_rows = 256

def unit_rms(values):
    return values * lax.rsqrt(lax.optimization_barrier(jnp.mean(values * values, axis=-1, keepdims=True)) + 1e-06)

def reference(node_features, w_qkv, w_out, head_scale, norm_gain, router, w_gate, w_up, w_down, neighbor_blocks, expert_ids):
    count = node_features.shape[0]
    query = jnp.dot(node_features, w_qkv[0], preferred_element_type=jnp.float32).reshape(count, HEADS, HEAD_DIM)
    keys = jnp.dot(node_features, w_qkv[1], preferred_element_type=jnp.float32).reshape(count, HEADS, HEAD_DIM)
    values = jnp.dot(node_features, w_qkv[2], preferred_element_type=jnp.float32)
    scaled = (unit_rms(query) * (head_scale / math.sqrt(HEAD_DIM))[None, :, None]).astype(jnp.bfloat16)
    key_unit = unit_rms(keys).astype(jnp.bfloat16)
    value_rows = values.astype(jnp.bfloat16)
    query_blocks = scaled.reshape(BLOCKS, ROWS_BLK, HEADS, HEAD_DIM)
    key_blocks = key_unit.reshape(BLOCKS, ROWS_BLK, HEADS, HEAD_DIM)
    value_blocks = value_rows.reshape(BLOCKS, ROWS_BLK, HEADS, HEAD_DIM)

    def one_block(block):
        listed = neighbor_blocks[block]
        near_keys = key_blocks[listed].reshape(NBR * ROWS_BLK, HEADS, HEAD_DIM).astype(jnp.float32)
        near_values = value_blocks[listed].reshape(NBR * ROWS_BLK, HEADS, HEAD_DIM).astype(jnp.float32)
        scores = jnp.einsum('qhd,khd->hqk', query_blocks[block].astype(jnp.float32), near_keys)
        largest = lax.optimization_barrier(jnp.max(scores, axis=-1, keepdims=True))
        expo = jnp.exp(scores - largest)
        weights = (expo / lax.optimization_barrier(jnp.sum(expo, axis=-1, keepdims=True))).astype(jnp.bfloat16)
        result = jnp.einsum('hqk,khd->qhd', weights.astype(jnp.float32), near_values)
        return result.astype(jnp.bfloat16)
    heads_out = lax.map(one_block, jnp.arange(BLOCKS, dtype=jnp.int32)).reshape(count, D)
    attn_sum = jnp.dot(heads_out, w_out, preferred_element_type=jnp.float32)
    mixed = node_features.astype(jnp.float32) + attn_sum
    normed = (unit_rms(mixed) * norm_gain).astype(jnp.bfloat16)
    routed = expert_ids[:, 0]
    logits = jnp.dot(normed, router, preferred_element_type=jnp.float32)
    chosen = routed[:, None] == jnp.arange(EXPERTS, dtype=jnp.int32)[None, :]
    gate = jax.nn.sigmoid(lax.optimization_barrier(jnp.sum(jnp.where(chosen, logits, 0.0), axis=1)))
    order = jnp.argsort(routed, stable=True).astype(jnp.int32)
    counts = lax.optimization_barrier(jnp.sum(chosen.astype(jnp.int32), axis=0))
    starts = jnp.cumsum(counts) - counts
    slabs = (counts + slab_rows - 1) // slab_rows
    slab_end = jnp.cumsum(slabs)
    slab_start = slab_end - slabs
    sorted_rows = normed[order]
    total_slabs = count // slab_rows + EXPERTS + 1
    offsets = jnp.arange(slab_rows, dtype=jnp.int32)

    def one_slab(slab):
        expert = jnp.sum((slab_end <= slab).astype(jnp.int32))
        clipped = jnp.minimum(expert, EXPERTS - 1)
        inside = slab - slab_start[clipped]
        positions = starts[clipped] + inside * slab_rows + offsets
        live = (inside * slab_rows + offsets < counts[clipped]) & (expert < EXPERTS)
        safe = jnp.clip(positions, 0, count - 1)
        picked = sorted_rows[safe]
        gate_part = jnp.dot(picked, w_gate[clipped], preferred_element_type=jnp.float32)
        up_part = jnp.dot(picked, w_up[clipped], preferred_element_type=jnp.float32)
        hidden = (jax.nn.silu(gate_part) * up_part).astype(jnp.bfloat16)
        result = jnp.dot(hidden, w_down[clipped], preferred_element_type=jnp.float32)
        target = jnp.where(live, order[safe], count).astype(jnp.int32)
        return (result, target)
    results, targets = lax.map(one_slab, jnp.arange(total_slabs, dtype=jnp.int32))
    expert_out = jnp.zeros((count + 1, D), jnp.float32).at[targets.reshape(-1)].set(results.reshape(-1, D))[:count]
    layer_out = (mixed + gate[:, None] * expert_out).astype(jnp.bfloat16)
    return (attn_sum.astype(jnp.bfloat16), layer_out)
```

```python
import math

import jax
import jax.numpy as jnp
from jax import lax
from jax.experimental import pallas as pl
from jax.experimental.pallas import tpu as pltpu
from jax.sharding import PartitionSpec as P

HEAD_DIM = 64
ROWS_BLK = 128
LOCAL_REFS = 4
CAP_H = 2
CAP_E = 96
EPS = 1e-06
LANES = 128
VMEM_BYTES = 48 * 2**20

VMEM = pl.BlockSpec(memory_space=pltpu.VMEM)
SMEM = pl.BlockSpec(memory_space=pltpu.SMEM)
ANY = pl.BlockSpec(memory_space=pl.ANY)
F32 = jnp.float32
BF16 = jnp.bfloat16


def params():
    return pltpu.CompilerParams(vmem_limit_bytes=VMEM_BYTES)


def cost(flops, moved, transcendentals=0):
    return pl.CostEstimate(flops=flops, bytes_accessed=moved, transcendentals=transcendentals)


def head_units(values):
    low = lax.broadcasted_iota(jnp.int32, values.shape, 1) < HEAD_DIM
    squares = values * values
    first = jnp.sum(jnp.where(low, squares, 0.0), axis=1, keepdims=True)
    second = jnp.sum(jnp.where(low, 0.0, squares), axis=1, keepdims=True)
    scale = lax.rsqrt(jnp.where(low, first, second) * (1.0 / HEAD_DIM) + EPS)
    return values * scale


def qkv_kernel(x_ref, w_ref, scale_ref, q_ref, kv_ref):
    x = x_ref[...]
    rows = x.shape[0]
    query = jnp.dot(x, w_ref[0], preferred_element_type=F32)
    q_ref[...] = (head_units(query) * scale_ref[...]).astype(BF16)
    key = jnp.dot(x, w_ref[1], preferred_element_type=F32)
    value = jnp.dot(x, w_ref[2], preferred_element_type=F32)
    kv_ref[:, :, :LANES] = head_units(key).astype(BF16).reshape(rows // ROWS_BLK, ROWS_BLK, LANES)
    kv_ref[:, :, LANES:] = value.astype(BF16).reshape(rows // ROWS_BLK, ROWS_BLK, LANES)


def qkv(x, w, scale):
    rows, width = x.shape
    tile = 512
    blocks = tile // ROWS_BLK
    return pl.pallas_call(
        qkv_kernel,
        grid=(rows // tile,),
        in_specs=[
            pl.BlockSpec((tile, width), lambda i: (i, 0)),
            pl.BlockSpec((3, width, LANES), lambda i: (0, 0, 0)),
            pl.BlockSpec((1, LANES), lambda i: (0, 0)),
        ],
        out_specs=[
            pl.BlockSpec((tile, LANES), lambda i: (i, 0)),
            pl.BlockSpec((blocks, ROWS_BLK, 2 * LANES), lambda i: (i, 0, 0)),
        ],
        out_shape=[
            jax.ShapeDtypeStruct((rows, LANES), BF16),
            jax.ShapeDtypeStruct((rows // ROWS_BLK, ROWS_BLK, 2 * LANES), BF16),
        ],
        compiler_params=params(),
        cost_estimate=cost(2 * rows * width * 3 * LANES, 2 * rows * (width + 3 * LANES)),
        name="qkv",
    )(x, w, scale)


def pick_kernel(wanted_ref, kv_ref, out_ref, sems):
    count = out_ref.shape[0]
    copies = [
        pltpu.make_async_copy(kv_ref.at[wanted_ref[i]], out_ref.at[i], sems.at[i])
        for i in range(count)
    ]
    for copy in copies:
        copy.start()
    for copy in copies:
        copy.wait()


def pick_blocks(wanted, kv):
    count = wanted.shape[0]
    out = jax.ShapeDtypeStruct((count,) + kv.shape[1:], kv.dtype)
    return pl.pallas_call(
        pick_kernel,
        in_specs=[SMEM, VMEM],
        out_specs=ANY,
        out_shape=out,
        scratch_shapes=[pltpu.SemaphoreType.DMA((count,))],
        compiler_params=params(),
        cost_estimate=cost(0, 2 * out.size * 2),
        name="pick_blocks",
    )(wanted, kv)


def attention_kernel(
    near_ref, far_ref, q_ref, kv_ref, halo_ref, spot_ref, lane_ref, heads_ref, send_ref, keys, values, spread
):
    blocks = kv_ref.shape[0]
    nears, fars = near_ref.shape[1], far_ref.shape[1]
    low = lax.broadcasted_iota(jnp.int32, (ROWS_BLK, LANES), 1) < HEAD_DIM

    @pl.loop(0, blocks)
    def _(b):
        rows = pl.ds(pl.multiple_of(b * ROWS_BLK, ROWS_BLK), ROWS_BLK)
        q = q_ref[rows, :].astype(F32)
        both = jnp.concatenate([jnp.where(low, q, 0.0), jnp.where(low, 0.0, q)], axis=0).astype(BF16)
        for j in range(nears + fars):
            if j < nears:
                block = kv_ref[near_ref[b, j]]
            else:
                block = halo_ref[far_ref[b, j - nears]]
            keys[j * ROWS_BLK : (j + 1) * ROWS_BLK, :] = block[:, :LANES]
            values[j * ROWS_BLK : (j + 1) * ROWS_BLK, :] = block[:, LANES:]
        scores = lax.dot_general(
            both, keys[...], (((1,), (1,)), ((), ())), preferred_element_type=F32
        )
        largest = jnp.max(scores, axis=1, keepdims=True)
        expo = jnp.exp(scores - largest)
        total = jnp.sum(expo, axis=1, keepdims=True)
        out = jnp.dot(expo.astype(BF16), values[...], preferred_element_type=F32) / total
        heads = jnp.where(low, out[:ROWS_BLK], out[ROWS_BLK:])
        heads_ref[rows, :] = heads.astype(BF16)
        lane = lane_ref[rows, :]
        for m in range(4):
            spread[rows, m * LANES : (m + 1) * LANES] = jnp.where(lane == m, heads, 0.0).astype(BF16)

    dests, cap = send_ref.shape[0], send_ref.shape[2]
    step = 4

    @pl.loop(0, dests // step)
    def _(i):
        tile = step * cap
        spot = spot_ref[...]
        here = lax.broadcasted_iota(jnp.int32, (tile, spot.shape[1]), 0) + i * tile
        hot = jnp.where(here == spot, 1.0, 0.0).astype(BF16)
        placed = jnp.dot(hot, spread[...], preferred_element_type=F32).astype(BF16)
        for d in range(step):
            for m in range(4):
                send_ref[i * step + d, m] = placed[d * cap : (d + 1) * cap, m * LANES : (m + 1) * LANES]


def attention(near, far, q, kv, halo, spot_row, lane_col, parts, cap):
    rows = q.shape[0]
    keys = (near.shape[1] + far.shape[1]) * ROWS_BLK
    return pl.pallas_call(
        attention_kernel,
        in_specs=[SMEM, SMEM, VMEM, VMEM, VMEM, VMEM, VMEM],
        out_specs=[VMEM, VMEM],
        out_shape=[
            jax.ShapeDtypeStruct((rows, LANES), BF16),
            jax.ShapeDtypeStruct((parts, 4, cap, LANES), BF16),
        ],
        scratch_shapes=[
            pltpu.VMEM((keys, LANES), BF16),
            pltpu.VMEM((keys, LANES), BF16),
            pltpu.VMEM((rows, 4 * LANES), BF16),
        ],
        compiler_params=params(),
        cost_estimate=cost(12 * 10**9, 8 * 2**20, 2 * rows * keys),
        name="attention",
    )(near, far, q, kv, halo, spot_row, lane_col)


def place_kernel(spot_ref, x_ref, out_ref):
    dests, cap = out_ref.shape[0], out_ref.shape[1]
    step = 4

    @pl.loop(0, dests // step)
    def _(i):
        tile = step * cap
        spot = spot_ref[...]
        here = lax.broadcasted_iota(jnp.int32, (tile, spot.shape[1]), 0) + i * tile
        hot = jnp.where(here == spot, 1.0, 0.0).astype(BF16)
        placed = jnp.dot(hot, x_ref[...], preferred_element_type=F32).astype(BF16)
        for d in range(step):
            out_ref[i * step + d] = placed[d * cap : (d + 1) * cap, :]


def place_rows(spot_row, x, parts, cap):
    rows, width = x.shape
    return pl.pallas_call(
        place_kernel,
        in_specs=[VMEM, VMEM],
        out_specs=VMEM,
        out_shape=jax.ShapeDtypeStruct((parts, cap, width), BF16),
        compiler_params=params(),
        cost_estimate=cost(2 * parts * cap * rows * width, 4 * 2**20),
        name="place_rows",
    )(spot_row, x)


def experts_kernel(
    me_ref, h_ref, x_ref, gain_ref, route_ref, w0_ref, w1_ref, w2_ref, w3_ref, out_ref
):
    me = me_ref[0]
    parts, cap, width = x_ref.shape
    tile = parts * cap
    quarters = (w0_ref, w1_ref, w2_ref, w3_ref)
    total = None
    for k, w in enumerate(quarters):
        piece = h_ref[:, me ^ k].reshape(tile, LANES)
        term = jnp.dot(piece, w[3 * width :, :], preferred_element_type=F32)
        total = term if total is None else total + term
    mixed = x_ref[...].reshape(tile, width).astype(F32) + total
    mean = jnp.mean(mixed * mixed, axis=1, keepdims=True)
    normed = (mixed * lax.rsqrt(mean + EPS) * gain_ref[...]).astype(BF16)
    logit = jnp.sum(normed.astype(F32) * route_ref[...], axis=1, keepdims=True)
    gate = 1.0 / (1.0 + jnp.exp(-logit))
    result = None
    for w in quarters:
        left = jnp.dot(normed, w[:width, :], preferred_element_type=F32)
        right = jnp.dot(normed, w[width : 2 * width, :], preferred_element_type=F32)
        half = 0.5 * left
        hidden = ((half + half * jnp.tanh(half)) * right).astype(BF16)
        term = jnp.dot(hidden, w[2 * width : 3 * width, :], preferred_element_type=F32)
        result = term if result is None else result + term
    result = (gate * result).astype(BF16).reshape(parts, cap, width)
    for m in range(4):
        out_ref[:, m] = result[:, :, m * LANES : (m + 1) * LANES]


def experts(me, heads, x, gain, route, weights):
    parts, cap, width = x.shape
    step = 8
    whole = pl.BlockSpec(weights[0].shape, lambda i: (0, 0))
    row = pl.BlockSpec((1, width), lambda i: (0, 0))
    return pl.pallas_call(
        experts_kernel,
        grid=(parts // step,),
        in_specs=[
            SMEM,
            pl.BlockSpec((step, 4, cap, LANES), lambda i: (i, 0, 0, 0)),
            pl.BlockSpec((step, cap, width), lambda i: (i, 0, 0)),
            row,
            row,
            whole,
            whole,
            whole,
            whole,
        ],
        out_specs=pl.BlockSpec((step, 4, cap, LANES), lambda i: (i, 0, 0, 0)),
        out_shape=jax.ShapeDtypeStruct((parts, 4, cap, LANES), BF16),
        compiler_params=params(),
        cost_estimate=cost(2 * parts * cap * width * (12 * width + width), 12 * 2**20),
        name="experts",
    )(me, heads, x, gain, route, *weights)


def columns_kernel(
    me_ref, h0_ref, h1_ref, h2_ref, h3_ref, w0_ref, w1_ref, w2_ref, w3_ref, x_ref, attn_ref, mixed_ref
):
    columns = pl.ds(pl.multiple_of(me_ref[0] * LANES, LANES), LANES)
    total = None
    for h, w in zip((h0_ref, h1_ref, h2_ref, h3_ref), (w0_ref, w1_ref, w2_ref, w3_ref)):
        term = jnp.dot(h[...], w[:, columns], preferred_element_type=F32)
        total = term if total is None else total + term
    attn_ref[...] = total.astype(BF16)
    mixed_ref[...] = x_ref[:, columns].astype(F32) + total


def attention_columns(me, heads, weights, x):
    rows, width = x.shape
    last = weights[0].shape[0] // LANES - 1
    out = pl.BlockSpec((rows, LANES), lambda i: (0, 0))
    return pl.pallas_call(
        columns_kernel,
        grid=(1,),
        in_specs=[SMEM]
        + [out] * 4
        + [pl.BlockSpec((LANES, width), lambda i: (last, 0))] * 4
        + [pl.BlockSpec((rows, width), lambda i: (0, 0))],
        out_specs=[out, out],
        out_shape=[
            jax.ShapeDtypeStruct((rows, LANES), BF16),
            jax.ShapeDtypeStruct((rows, LANES), F32),
        ],
        compiler_params=params(),
        cost_estimate=cost(2 * rows * width * LANES, 8 * 2**20),
        name="attention_columns",
    )(me, *heads, *weights, x)


def combine_kernel(spot_ref, lane_ref, back_ref, mixed_ref, out_ref, slots):
    dests, cap = back_ref.shape[0], back_ref.shape[2]
    rows = out_ref.shape[0]
    for m in range(4):
        slots[:, m * LANES : (m + 1) * LANES] = back_ref[:, m].reshape(dests * cap, LANES)
    tile = 256

    @pl.loop(0, rows // tile)
    def _(i):
        here = pl.ds(pl.multiple_of(i * tile, tile), tile)
        spot = lax.broadcasted_iota(jnp.int32, (tile, dests * cap), 1)
        hot = jnp.where(spot == spot_ref[here, :], 1.0, 0.0).astype(BF16)
        found = jnp.dot(hot, slots[...], preferred_element_type=F32)
        lane = lane_ref[here, :]
        total = mixed_ref[here, :]
        for m in range(4):
            total = total + jnp.where(lane == m, found[:, m * LANES : (m + 1) * LANES], 0.0)
        out_ref[here, :] = total.astype(BF16)


def combine(spot_col, lane_col, back, mixed):
    rows = mixed.shape[0]
    slots = back.shape[0] * back.shape[2]
    return pl.pallas_call(
        combine_kernel,
        in_specs=[VMEM] * 4,
        out_specs=VMEM,
        out_shape=jax.ShapeDtypeStruct((rows, LANES), BF16),
        scratch_shapes=[pltpu.VMEM((slots, 4 * LANES), BF16)],
        compiler_params=params(),
        cost_estimate=cost(2 * rows * slots * 4 * LANES, 4 * 2**20),
        name="combine",
    )(spot_col, lane_col, back, mixed)


def swap(array, change):
    return lax.ppermute(array, "mp", [(i, i ^ change) for i in range(4)])


def exchange(array, axes):
    return lax.all_to_all(array, axes, split_axis=0, concat_axis=0, tiled=True)


def on_device(
    node_features,
    w_qkv,
    w_out,
    head_scale,
    norm_gain,
    router,
    w_gate,
    w_up,
    w_down,
    neighbor_blocks,
    expert_ids,
):
    parts = lax.axis_size("graph")
    part = lax.axis_index("graph")
    me = lax.axis_index("mp")
    rows, width = node_features.shape
    blocks = rows // ROWS_BLK
    half_cap = CAP_E // 2

    far = neighbor_blocks[:, LOCAL_REFS:]
    names = jnp.arange(parts * blocks, dtype=jnp.int32).reshape(parts, blocks)
    wanted = jnp.any(far.reshape(-1)[:, None, None] == names[None], axis=0)
    inside = jnp.arange(blocks, dtype=jnp.int32)[None, :]
    first = jnp.min(jnp.where(wanted, inside, blocks - 1), axis=1)
    last = jnp.max(jnp.where(wanted, inside, 0), axis=1)
    requests = jnp.stack([first, last], axis=1)
    incoming = exchange(requests.reshape(parts, 1, CAP_H), "graph").reshape(-1)
    bases = jnp.arange(parts, dtype=jnp.int32)[:, None] * blocks
    pool = (bases + requests).reshape(-1)
    slots = jnp.arange(pool.shape[0], dtype=jnp.int32)
    far_slots = jnp.max(jnp.where(far[:, :, None] == pool[None, None, :], slots[None, None, :], 0), axis=2)
    near_slots = neighbor_blocks[:, :LOCAL_REFS] - part * blocks

    scale = jnp.repeat(head_scale / math.sqrt(HEAD_DIM), HEAD_DIM)[None, :]
    q, kv = qkv(node_features, w_qkv, scale)
    halo = exchange(pick_blocks(incoming, kv), "graph")

    routed = expert_ids[:, 0]
    experts_all = router.shape[1]
    chosen = routed[:, None] == jnp.arange(experts_all, dtype=jnp.int32)[None, :]
    row_ids = jnp.arange(rows, dtype=jnp.int32)
    earlier = (row_ids[:, None] > row_ids[None, :]).astype(BF16)
    before = jnp.dot(earlier, chosen.astype(BF16), preferred_element_type=F32)
    rank = jnp.sum(jnp.where(chosen, before, 0.0), axis=1).astype(jnp.int32)
    second = (rank >= half_cap).astype(jnp.int32)
    lane = (routed % 2) * 2 + second
    spot = (routed // 2) * half_cap + rank - second * half_cap
    spot_row, spot_col, lane_col = spot[None, :], spot[:, None], lane[:, None]
    mine_row = jnp.where(lane == me, spot, -1)[None, :]
    x_there = exchange(place_rows(mine_row, node_features, parts, half_cap), "graph")

    which = me // 2
    kept, given = [
        jnp.concatenate(
            [lax.dynamic_index_in_dim(w, i, 0, keepdims=False) for w in (w_gate, w_up, w_down)] + [w_out],
            axis=0,
        )
        for i in (which, 1 - which)
    ]
    weights = [kept, swap(kept, 1), swap(given, 2), swap(given, 3)]
    route = lax.dynamic_index_in_dim(router, 2 * part + which, 1, keepdims=False).astype(F32)[None, :]
    me_ref = me[None].astype(jnp.int32)

    heads, send = attention(
        near_slots, far_slots, q, kv, halo, spot_row, lane_col, parts, half_cap
    )
    heads_there = exchange(send.reshape(parts * 4, half_cap, LANES), ("graph", "mp"))
    all_heads = [heads] + [swap(heads, k) for k in (1, 2, 3)]
    attn_out, mixed = attention_columns(me_ref, all_heads, weights, node_features)

    produced = experts(
        me_ref,
        heads_there.reshape(parts, 4, half_cap, LANES),
        x_there,
        norm_gain[None, :],
        route,
        weights,
    )
    back = exchange(produced.reshape(parts * 4, half_cap, LANES), ("graph", "mp"))
    layer_out = combine(spot_col, lane_col, back.reshape(parts, 4, half_cap, LANES), mixed)
    return (attn_out, layer_out)


def solution(mesh):
    placed = (
        P("graph", None),
        P(None, None, "mp"),
        P("mp", None),
        P("mp"),
        P(),
        P(),
        P("graph", None, "mp"),
        P("graph", None, "mp"),
        P("graph", "mp", None),
        P("graph", None),
        P("graph", None),
    )
    return jax.shard_map(
        on_device,
        mesh=mesh,
        in_specs=placed,
        out_specs=(P("graph", "mp"), P("graph", "mp")),
        check_vma=False,
    )
```

```python
import math

import jax
import jax.numpy as jnp
from jax import lax
from jax.experimental import pallas as pl
from jax.experimental.pallas import tpu as pltpu
from jax.sharding import PartitionSpec as P

HEAD_DIM = 64
ROWS_BLK = 128
LOCAL_REFS = 4
CAP_H = 2
CAP_E = 96
EPS = 1e-06
LANES = 128

VMEM = pl.BlockSpec(memory_space=pltpu.VMEM)
SMEM = pl.BlockSpec(memory_space=pltpu.SMEM)
ANY = pl.BlockSpec(memory_space=pl.ANY)
HBM = pl.BlockSpec(memory_space=pltpu.HBM)
F32 = jnp.float32
BF16 = jnp.bfloat16


def params(mebibytes):
    return pltpu.CompilerParams(vmem_limit_bytes=mebibytes * 2**20)


def cost(flops, moved, transcendentals=0):
    return pl.CostEstimate(flops=flops, bytes_accessed=moved, transcendentals=transcendentals)


def head_units(values):
    low = lax.broadcasted_iota(jnp.int32, values.shape, 1) < HEAD_DIM
    squares = values * values
    first = jnp.sum(jnp.where(low, squares, 0.0), axis=1, keepdims=True)
    second = jnp.sum(jnp.where(low, 0.0, squares), axis=1, keepdims=True)
    scale = lax.rsqrt(jnp.where(low, first, second) * (1.0 / HEAD_DIM) + EPS)
    return values * scale


def qkv_kernel(x_ref, w_ref, scale_ref, _, q_ref, kv_ref):
    x = x_ref[...]
    rows = x.shape[0]
    query = jnp.dot(x, w_ref[0], preferred_element_type=F32)
    low = lax.broadcasted_iota(jnp.int32, (1, LANES), 1) < HEAD_DIM
    scale = jnp.where(low, scale_ref[0], scale_ref[1]) * (1.0 / math.sqrt(HEAD_DIM))
    q_ref[...] = (head_units(query) * scale).astype(BF16)
    key = jnp.dot(x, w_ref[1], preferred_element_type=F32)
    value = jnp.dot(x, w_ref[2], preferred_element_type=F32)
    kv_ref[:, :, :LANES] = head_units(key).astype(BF16).reshape(rows // ROWS_BLK, ROWS_BLK, LANES)
    kv_ref[:, :, LANES:] = value.astype(BF16).reshape(rows // ROWS_BLK, ROWS_BLK, LANES)


def qkv(x, w, scale, after):
    rows, width = x.shape
    tile = 512
    blocks = tile // ROWS_BLK
    return pl.pallas_call(
        qkv_kernel,
        grid=(rows // tile,),
        in_specs=[
            pl.BlockSpec((tile, width), lambda i: (i, 0)),
            pl.BlockSpec((3, width, LANES), lambda i: (0, 0, 0)),
            SMEM,
            ANY,
        ],
        out_specs=[
            pl.BlockSpec((tile, LANES), lambda i: (i, 0)),
            pl.BlockSpec((blocks, ROWS_BLK, 2 * LANES), lambda i: (i, 0, 0)),
        ],
        out_shape=[
            jax.ShapeDtypeStruct((rows, LANES), BF16),
            jax.ShapeDtypeStruct((rows // ROWS_BLK, ROWS_BLK, 2 * LANES), BF16),
        ],
        compiler_params=params(60),
        cost_estimate=cost(2 * rows * width * 3 * LANES, 2 * rows * (width + 3 * LANES)),
        name="qkv",
    )(x, w, scale, after)


def split_kernel(me_ref, gate_ref, up_ref, down_ref, out_w_ref, kept_ref, given_ref, sems):
    which = me_ref[0] // 2
    width = gate_ref.shape[1]
    copies = []
    for target, index in ((kept_ref, which), (given_ref, 1 - which)):
        for i, source in enumerate((gate_ref, up_ref, down_ref)):
            copies.append((source.at[index], target.at[pl.ds(i * width, width)]))
        copies.append((out_w_ref, target.at[pl.ds(3 * width, LANES)]))
    copies = [pltpu.make_async_copy(a, b, sems.at[i]) for i, (a, b) in enumerate(copies)]
    for copy in copies:
        copy.start()
    for copy in copies:
        copy.wait()


def split_weights(me, gate, up, down, out_w):
    width = gate.shape[1]
    out = jax.ShapeDtypeStruct((3 * width + LANES, width), BF16)
    return pl.pallas_call(
        split_kernel,
        in_specs=[SMEM] + [HBM] * 4,
        out_specs=[HBM, HBM],
        out_shape=[out, out],
        scratch_shapes=[pltpu.SemaphoreType.DMA((8,))],
        compiler_params=params(60),
        cost_estimate=cost(0, 4 * out.size * 2),
        name="split_weights",
    )(me, gate, up, down, out_w)


def pick_kernel(wanted_ref, kv_ref, out_ref, sems):
    count = out_ref.shape[0]
    copies = [
        pltpu.make_async_copy(
            kv_ref.at[wanted_ref[i // CAP_H, 0, i % CAP_H]], out_ref.at[i], sems.at[i]
        )
        for i in range(count)
    ]
    for copy in copies:
        copy.start()
    for copy in copies:
        copy.wait()


def pick_blocks(wanted, kv):
    count = wanted.size
    out = jax.ShapeDtypeStruct((count,) + kv.shape[1:], kv.dtype)
    return pl.pallas_call(
        pick_kernel,
        in_specs=[SMEM, VMEM],
        out_specs=HBM,
        out_shape=out,
        scratch_shapes=[pltpu.SemaphoreType.DMA((count,))],
        compiler_params=params(60),
        cost_estimate=cost(0, 2 * out.size * 2),
        name="pick_blocks",
    )(wanted, kv)


def as_column(row):
    count = row.shape[1]
    shape = (count, count)
    same = lax.broadcasted_iota(jnp.int32, shape, 0) == lax.broadcasted_iota(jnp.int32, shape, 1)
    return jnp.sum(jnp.where(same, row.astype(F32), 0.0), axis=1, keepdims=True)


def attention_kernel(
    near_ref, far_ref, q_ref, kv_ref, halo_ref, spot_ref, lane_ref, *rest
):
    heads_ref, send_ref, keys, values, spread = rest[-5:]
    blocks = kv_ref.shape[0]
    together = keys.shape[0]
    nears, fars = near_ref.shape[1], far_ref.shape[1]
    low = lax.broadcasted_iota(jnp.int32, (ROWS_BLK, LANES), 1) < HEAD_DIM

    @pl.loop(0, blocks // together)
    def _(i):
        at = [i * together + t for t in range(together)]
        at_rows = [pl.ds(pl.multiple_of(b * ROWS_BLK, ROWS_BLK), ROWS_BLK) for b in at]
        scores = []
        for t, (b, rows) in enumerate(zip(at, at_rows)):
            q = q_ref[rows, :].astype(F32)
            both = jnp.concatenate([jnp.where(low, q, 0.0), jnp.where(low, 0.0, q)], axis=0).astype(BF16)
            for j in range(nears + fars):
                if j < nears:
                    block = kv_ref[near_ref[b, j]]
                else:
                    block = halo_ref[far_ref[b, j - nears]]
                keys[t, j * ROWS_BLK : (j + 1) * ROWS_BLK, :] = block[:, :LANES]
                values[t, j * ROWS_BLK : (j + 1) * ROWS_BLK, :] = block[:, LANES:]
            scores.append(
                lax.dot_general(both, keys[t], (((1,), (1,)), ((), ())), preferred_element_type=F32)
            )
        for t, rows in enumerate(at_rows):
            largest = jnp.max(scores[t], axis=1, keepdims=True)
            expo = jnp.exp(scores[t] - largest)
            total = jnp.sum(expo, axis=1, keepdims=True)
            out = jnp.dot(expo.astype(BF16), values[t], preferred_element_type=F32) / total
            heads = jnp.where(low, out[:ROWS_BLK], out[ROWS_BLK:])
            heads_ref[rows, :] = heads.astype(BF16)
            lane = as_column(lane_ref[:, rows])
            for m in range(4):
                spread[rows, m * LANES : (m + 1) * LANES] = jnp.where(lane == m, heads, 0.0).astype(BF16)

    dests, cap = send_ref.shape[0], send_ref.shape[2]
    step = 4

    @pl.loop(0, dests // step)
    def _(i):
        tile = step * cap
        spot = spot_ref[...]
        here = lax.broadcasted_iota(jnp.int32, (tile, spot.shape[1]), 0) + i * tile
        hot = jnp.where(here == spot, 1.0, 0.0).astype(BF16)
        placed = jnp.dot(hot, spread[...], preferred_element_type=F32).astype(BF16)
        for d in range(step):
            for m in range(4):
                send_ref[i * step + d, m] = placed[d * cap : (d + 1) * cap, m * LANES : (m + 1) * LANES]


def attention(near, far, q, kv, halo, spot_row, lane_row, after, parts, cap, together=4):
    rows = q.shape[0]
    keys = (near.shape[1] + far.shape[1]) * ROWS_BLK
    return pl.pallas_call(
        attention_kernel,
        in_specs=[SMEM, SMEM, VMEM, VMEM, VMEM, VMEM, VMEM] + [ANY] * len(after),
        out_specs=[VMEM, VMEM],
        out_shape=[
            jax.ShapeDtypeStruct((rows, LANES), BF16),
            jax.ShapeDtypeStruct((parts, 4, cap, LANES), BF16),
        ],
        scratch_shapes=[
            pltpu.VMEM((together, keys, LANES), BF16),
            pltpu.VMEM((together, keys, LANES), BF16),
            pltpu.VMEM((rows, 4 * LANES), BF16),
        ],
        compiler_params=params(60),
        cost_estimate=cost(12 * 10**9, 8 * 2**20, 2 * rows * keys),
        name="attention",
    )(near, far, q, kv, halo, spot_row, lane_row, *after)


def place_kernel(spot_ref, x_ref, out_ref):
    dests, cap = out_ref.shape[0], out_ref.shape[1]
    step = 4

    @pl.loop(0, dests // step)
    def _(i):
        tile = step * cap
        spot = spot_ref[...]
        here = lax.broadcasted_iota(jnp.int32, (tile, spot.shape[1]), 0) + i * tile
        hot = jnp.where(here == spot, 1.0, 0.0).astype(BF16)
        placed = jnp.dot(hot, x_ref[...], preferred_element_type=F32).astype(BF16)
        for d in range(step):
            out_ref[i * step + d] = placed[d * cap : (d + 1) * cap, :]


def place_rows(spot_row, x, parts, cap):
    rows, width = x.shape
    return pl.pallas_call(
        place_kernel,
        in_specs=[VMEM, VMEM],
        out_specs=VMEM,
        out_shape=jax.ShapeDtypeStruct((parts, cap, width), BF16),
        compiler_params=params(60),
        cost_estimate=cost(2 * parts * cap * rows * width, 4 * 2**20),
        name="place_rows",
    )(spot_row, x)


def experts_kernel(me_ref, gain_ref, route_ref, h_ref, x_ref, w0_ref, w1_ref, w2_ref, w3_ref, *rest):
    out_ref, heads, features, project, quarters, results, sems = rest[-7:]
    me = me_ref[0]
    tiles, step, cap, width = features.shape
    tile = step * cap
    sources = (w0_ref, w1_ref, w2_ref, w3_ref)
    sizes = ((h_ref, heads), (x_ref, features))
    small = [
        pltpu.make_async_copy(
            w.at[pl.ds(3 * width, LANES)], project.at[pl.ds(k * LANES, LANES)], sems.at[k]
        )
        for k, w in enumerate(sources)
    ]
    large = [
        pltpu.make_async_copy(w.at[pl.ds(0, 3 * width)], quarters.at[k], sems.at[4 + k])
        for k, w in enumerate(sources)
    ]
    rows = [
        [
            pltpu.make_async_copy(source.at[pl.ds(t * step, step)], target.at[t], sems.at[8 + 2 * t + i])
            for i, (source, target) in enumerate(sizes)
        ]
        for t in range(tiles)
    ]
    outs = [
        pltpu.make_async_copy(
            results.at[t], out_ref.at[pl.ds(t * step, step)], sems.at[8 + 2 * tiles + t]
        )
        for t in range(tiles)
    ]
    for copy in rows[0] + small + large + [c for later in rows[1:] for c in later]:
        copy.start()
    for copy in small:
        copy.wait()
    for t in range(tiles):
        for copy in rows[t]:
            copy.wait()
        arrived = jnp.concatenate([heads[t, :, me ^ k].reshape(tile, LANES) for k in range(4)], axis=1)
        mixed = features[t].reshape(tile, width).astype(F32) + jnp.dot(
            arrived, project[...], preferred_element_type=F32
        )
        mean = jnp.mean(mixed * mixed, axis=1, keepdims=True)
        normed = (mixed * lax.rsqrt(mean + EPS) * gain_ref[...]).astype(BF16)
        logit = jnp.sum(normed.astype(F32) * route_ref[...], axis=1, keepdims=True)
        gate = 1.0 / (1.0 + jnp.exp(-logit))
        result = None
        for k in range(4):
            if t == 0:
                large[k].wait()
            left = jnp.dot(normed, quarters[k, :width, :], preferred_element_type=F32)
            right = jnp.dot(normed, quarters[k, width : 2 * width, :], preferred_element_type=F32)
            half = 0.5 * left
            hidden = ((half + half * jnp.tanh(half)) * right).astype(BF16)
            term = jnp.dot(hidden, quarters[k, 2 * width :, :], preferred_element_type=F32)
            result = term if result is None else result + term
        result = (gate * result).astype(BF16).reshape(step, cap, width)
        for m in range(4):
            results[t, :, m] = result[:, :, m * LANES : (m + 1) * LANES]
        outs[t].start()
    for copy in outs:
        copy.wait()


def experts(me, heads, x, gain, route, weights, after, tiles=2):
    parts, cap, width = x.shape
    step = parts // tiles
    return pl.pallas_call(
        experts_kernel,
        in_specs=[SMEM, VMEM, VMEM, HBM, HBM] + [ANY] * (4 + len(after)),
        out_specs=HBM,
        out_shape=jax.ShapeDtypeStruct((parts, 4, cap, LANES), BF16),
        scratch_shapes=[
            pltpu.VMEM((tiles, step, 4, cap, LANES), BF16),
            pltpu.VMEM((tiles, step, cap, width), BF16),
            pltpu.VMEM((width, width), BF16),
            pltpu.VMEM((4, 3 * width, width), BF16),
            pltpu.VMEM((tiles, step, 4, cap, LANES), BF16),
            pltpu.SemaphoreType.DMA((8 + 3 * tiles,)),
        ],
        compiler_params=params(59),
        cost_estimate=cost(2 * parts * cap * width * (12 * width + width), 12 * 2**20),
        name="experts",
    )(me, gain, route, heads, x, *weights, *after)


def columns_kernel(
    me_ref, h0_ref, h1_ref, h2_ref, h3_ref, w0_ref, w1_ref, w2_ref, w3_ref, x_ref, attn_ref, mixed_ref
):
    columns = pl.ds(pl.multiple_of(me_ref[0] * LANES, LANES), LANES)
    total = None
    for h, w in zip((h0_ref, h1_ref, h2_ref, h3_ref), (w0_ref, w1_ref, w2_ref, w3_ref)):
        term = jnp.dot(h[...], w[:, columns], preferred_element_type=F32)
        total = term if total is None else total + term
    attn_ref[...] = total.astype(BF16)
    mixed_ref[...] = x_ref[:, columns].astype(F32) + total


def attention_columns(me, heads, weights, x):
    rows, width = x.shape
    last = weights[0].shape[0] // LANES - 1
    out = pl.BlockSpec((rows, LANES), lambda i: (0, 0))
    return pl.pallas_call(
        columns_kernel,
        grid=(1,),
        in_specs=[SMEM]
        + [out] * 4
        + [pl.BlockSpec((LANES, width), lambda i: (last, 0))] * 4
        + [pl.BlockSpec((rows, width), lambda i: (0, 0))],
        out_specs=[out, out],
        out_shape=[
            jax.ShapeDtypeStruct((rows, LANES), BF16),
            jax.ShapeDtypeStruct((rows, LANES), F32),
        ],
        compiler_params=params(60),
        cost_estimate=cost(2 * rows * width * LANES, 8 * 2**20),
        name="attention_columns",
    )(me, *heads, *weights, x)


def combine_kernel(spot_ref, lane_ref, mixed_ref, back_ref, out_ref, slots, sems):
    dests, cap, width = slots.shape
    rows = out_ref.shape[0]
    copies = [
        pltpu.make_async_copy(
            back_ref.at[:, m], slots.at[:, :, pl.ds(m * LANES, LANES)], sems.at[m]
        )
        for m in range(4)
    ]
    for copy in copies:
        copy.start()
    for copy in copies:
        copy.wait()
    tile = 256
    names = lax.broadcasted_iota(jnp.int32, (ROWS_BLK, dests * cap), 1).astype(F32)

    @pl.loop(0, rows // tile)
    def _(i):
        pieces = [
            pl.ds(pl.multiple_of(i * tile + t * ROWS_BLK, ROWS_BLK), ROWS_BLK) for t in range(tile // ROWS_BLK)
        ]
        hot = jnp.concatenate(
            [jnp.where(names == as_column(spot_ref[:, p]), 1.0, 0.0).astype(BF16) for p in pieces], axis=0
        )
        found = jnp.dot(hot, slots[...].reshape(dests * cap, width), preferred_element_type=F32)
        for t, p in enumerate(pieces):
            lane = as_column(lane_ref[:, p])
            total = mixed_ref[p, :]
            for m in range(4):
                part = found[t * ROWS_BLK : (t + 1) * ROWS_BLK, m * LANES : (m + 1) * LANES]
                total = total + jnp.where(lane == m, part, 0.0)
            out_ref[p, :] = total.astype(BF16)


def combine(spot_row, lane_row, back, mixed):
    rows = mixed.shape[0]
    slots = back.shape[0] * back.shape[2]
    return pl.pallas_call(
        combine_kernel,
        in_specs=[VMEM] * 3 + [HBM],
        out_specs=VMEM,
        out_shape=jax.ShapeDtypeStruct((rows, LANES), BF16),
        scratch_shapes=[
            pltpu.VMEM((back.shape[0], back.shape[2], 4 * LANES), BF16),
            pltpu.SemaphoreType.DMA((4,)),
        ],
        compiler_params=params(24),
        cost_estimate=cost(2 * rows * slots * 4 * LANES, 4 * 2**20),
        name="combine",
    )(spot_row, lane_row, mixed, back)


def swap(array, change):
    return lax.ppermute(array, "mp", [(i, i ^ change) for i in range(4)])


def exchange(array, axes):
    return lax.all_to_all(array, axes, split_axis=0, concat_axis=0, tiled=True)


def on_device(
    node_features,
    w_qkv,
    w_out,
    head_scale,
    norm_gain,
    router,
    w_gate,
    w_up,
    w_down,
    neighbor_blocks,
    expert_ids,
):
    parts = lax.axis_size("graph")
    part = lax.axis_index("graph")
    me = lax.axis_index("mp")
    rows, width = node_features.shape
    blocks = rows // ROWS_BLK
    half_cap = CAP_E // 2

    far = neighbor_blocks[:, LOCAL_REFS:]
    names = jnp.arange(parts * blocks, dtype=jnp.int32).reshape(parts, blocks)
    wanted = jnp.any(far.reshape(-1)[:, None, None] == names[None], axis=0)
    inside = jnp.arange(blocks, dtype=jnp.int32)[None, :]
    first = jnp.min(jnp.where(wanted, inside, blocks - 1), axis=1)
    last = jnp.max(jnp.where(wanted, inside, 0), axis=1)
    requests = jnp.stack([first, last], axis=1)
    incoming = exchange(requests.reshape(parts, 1, CAP_H), "graph")
    bases = jnp.arange(parts, dtype=jnp.int32)[:, None] * blocks
    pool = (bases + requests).reshape(-1)
    slots = jnp.arange(pool.shape[0], dtype=jnp.int32)
    far_slots = jnp.max(jnp.where(far[:, :, None] == pool[None, None, :], slots[None, None, :], 0), axis=2)
    near_slots = neighbor_blocks[:, :LOCAL_REFS] - part * blocks

    which = me // 2
    me_ref = me[None].astype(jnp.int32)
    kept, given = split_weights(me_ref, w_gate, w_up, w_down, w_out)
    weights = [kept, swap(kept, 1), swap(given, 2), swap(given, 3)]

    q, kv = qkv(node_features, w_qkv, head_scale, kept)
    halo = exchange(pick_blocks(incoming, kv), "graph")

    routed = expert_ids[:, 0]
    experts_all = router.shape[1]
    chosen = routed[:, None] == jnp.arange(experts_all, dtype=jnp.int32)[None, :]
    row_ids = jnp.arange(rows, dtype=jnp.int32)
    earlier = (row_ids[:, None] > row_ids[None, :]).astype(BF16)
    before = jnp.dot(earlier, chosen.astype(BF16), preferred_element_type=F32)
    rank = jnp.sum(jnp.where(chosen, before, 0.0), axis=1).astype(jnp.int32)
    second = (rank >= half_cap).astype(jnp.int32)
    lane = (routed % 2) * 2 + second
    spot = (routed // 2) * half_cap + rank - second * half_cap
    spot_row, lane_row = spot[None, :], lane[None, :]
    mine_row = jnp.where(lane == me, spot, -1)[None, :]
    x_there = exchange(place_rows(mine_row, node_features, parts, half_cap), "graph")

    route = lax.dynamic_index_in_dim(router, 2 * part + which, 1, keepdims=False).astype(F32)[None, :]
    heads, send = attention(
        near_slots, far_slots, q, kv, halo, spot_row, lane_row, weights[1:2], parts, half_cap
    )
    send, x_there, weights[2:] = lax.optimization_barrier((send, x_there, weights[2:]))
    heads_there = exchange(send.reshape(parts * 4, half_cap, LANES), ("graph", "mp"))
    all_heads = [heads] + [swap(heads, k) for k in (1, 2, 3)]
    attn_out, mixed = attention_columns(me_ref, all_heads, weights, node_features)

    produced = experts(
        me_ref,
        heads_there.reshape(parts, 4, half_cap, LANES),
        x_there,
        norm_gain[None, :],
        route,
        weights,
        all_heads[1:],
    )
    back = exchange(produced.reshape(parts * 4, half_cap, LANES), ("graph", "mp"))
    layer_out = combine(spot_row, lane_row, back.reshape(parts, 4, half_cap, LANES), mixed)
    return (attn_out, layer_out)


def solution(mesh):
    placed = (
        P("graph", None),
        P(None, None, "mp"),
        P("mp", None),
        P("mp"),
        P(),
        P(),
        P("graph", None, "mp"),
        P("graph", None, "mp"),
        P("graph", "mp", None),
        P("graph", None),
        P("graph", None),
    )
    return jax.shard_map(
        on_device,
        mesh=mesh,
        in_specs=placed,
        out_specs=(P("graph", "mp"), P("graph", "mp")),
        check_vma=False,
    )
```

```python
import math

import jax
import jax.numpy as jnp
from jax import lax
from jax.experimental import pallas as pl
from jax.experimental.pallas import tpu as pltpu
from jax.sharding import PartitionSpec as P

HEAD_DIM = 64
ROWS_BLK = 128
LOCAL_REFS = 4
CAP_H = 2
CAP_E = 96
EPS = 1e-06
LANES = 128

VMEM = pl.BlockSpec(memory_space=pltpu.VMEM)
SMEM = pl.BlockSpec(memory_space=pltpu.SMEM)
ANY = pl.BlockSpec(memory_space=pl.ANY)
HBM = pl.BlockSpec(memory_space=pltpu.HBM)
F32 = jnp.float32
BF16 = jnp.bfloat16


def params(mebibytes):
    return pltpu.CompilerParams(vmem_limit_bytes=mebibytes * 2**20)


def cost(flops, moved, transcendentals=0):
    return pl.CostEstimate(flops=flops, bytes_accessed=moved, transcendentals=transcendentals)


def head_units(values):
    low = lax.broadcasted_iota(jnp.int32, values.shape, 1) < HEAD_DIM
    squares = values * values
    first = jnp.sum(jnp.where(low, squares, 0.0), axis=1, keepdims=True)
    second = jnp.sum(jnp.where(low, 0.0, squares), axis=1, keepdims=True)
    scale = lax.rsqrt(jnp.where(low, first, second) * (1.0 / HEAD_DIM) + EPS)
    return values * scale


def qkv_kernel(x_ref, w_ref, scale_ref, _, q_ref, kv_ref):
    x = x_ref[...]
    rows = x.shape[0]
    query = jnp.dot(x, w_ref[0], preferred_element_type=F32)
    low = lax.broadcasted_iota(jnp.int32, (1, LANES), 1) < HEAD_DIM
    scale = jnp.where(low, scale_ref[0], scale_ref[1]) * (1.0 / math.sqrt(HEAD_DIM))
    q_ref[...] = (head_units(query) * scale).astype(BF16)
    key = jnp.dot(x, w_ref[1], preferred_element_type=F32)
    value = jnp.dot(x, w_ref[2], preferred_element_type=F32)
    kv_ref[:, :, :LANES] = head_units(key).astype(BF16).reshape(rows // ROWS_BLK, ROWS_BLK, LANES)
    kv_ref[:, :, LANES:] = value.astype(BF16).reshape(rows // ROWS_BLK, ROWS_BLK, LANES)


def qkv(x, w, scale, after):
    rows, width = x.shape
    tile = 512
    blocks = tile // ROWS_BLK
    return pl.pallas_call(
        qkv_kernel,
        grid=(rows // tile,),
        in_specs=[
            pl.BlockSpec((tile, width), lambda i: (i, 0)),
            pl.BlockSpec((3, width, LANES), lambda i: (0, 0, 0)),
            SMEM,
            ANY,
        ],
        out_specs=[
            pl.BlockSpec((tile, LANES), lambda i: (i, 0)),
            pl.BlockSpec((blocks, ROWS_BLK, 2 * LANES), lambda i: (i, 0, 0)),
        ],
        out_shape=[
            jax.ShapeDtypeStruct((rows, LANES), BF16),
            jax.ShapeDtypeStruct((rows // ROWS_BLK, ROWS_BLK, 2 * LANES), BF16),
        ],
        compiler_params=params(60),
        cost_estimate=cost(2 * rows * width * 3 * LANES, 2 * rows * (width + 3 * LANES)),
        name="qkv",
    )(x, w, scale, after)


def split_kernel(me_ref, gate_ref, up_ref, down_ref, out_w_ref, kept_ref, given_ref, sems):
    which = me_ref[0] // 2
    width = gate_ref.shape[1]
    copies = []
    for target, index in ((kept_ref, which), (given_ref, 1 - which)):
        for i, source in enumerate((gate_ref, up_ref, down_ref)):
            copies.append((source.at[index], target.at[pl.ds(i * width, width)]))
        copies.append((out_w_ref, target.at[pl.ds(3 * width, LANES)]))
    copies = [pltpu.make_async_copy(a, b, sems.at[i]) for i, (a, b) in enumerate(copies)]
    for copy in copies:
        copy.start()
    for copy in copies:
        copy.wait()


def split_weights(me, gate, up, down, out_w):
    width = gate.shape[1]
    out = jax.ShapeDtypeStruct((3 * width + LANES, width), BF16)
    return pl.pallas_call(
        split_kernel,
        in_specs=[SMEM] + [VMEM] * 4,
        out_specs=[HBM, HBM],
        out_shape=[out, out],
        scratch_shapes=[pltpu.SemaphoreType.DMA((8,))],
        compiler_params=params(60),
        cost_estimate=cost(0, 4 * out.size * 2),
        name="split_weights",
    )(me, gate, up, down, out_w)


def pick_kernel(wanted_ref, kv_ref, out_ref, sems):
    count = out_ref.shape[0]
    copies = [
        pltpu.make_async_copy(
            kv_ref.at[wanted_ref[i // CAP_H, 0, i % CAP_H]], out_ref.at[i], sems.at[i]
        )
        for i in range(count)
    ]
    for copy in copies:
        copy.start()
    for copy in copies:
        copy.wait()


def pick_blocks(wanted, kv):
    count = wanted.size
    out = jax.ShapeDtypeStruct((count,) + kv.shape[1:], kv.dtype)
    return pl.pallas_call(
        pick_kernel,
        in_specs=[SMEM, VMEM],
        out_specs=HBM,
        out_shape=out,
        scratch_shapes=[pltpu.SemaphoreType.DMA((count,))],
        compiler_params=params(60),
        cost_estimate=cost(0, 2 * out.size * 2),
        name="pick_blocks",
    )(wanted, kv)


def as_column(row):
    count = row.shape[1]
    shape = (count, count)
    same = lax.broadcasted_iota(jnp.int32, shape, 0) == lax.broadcasted_iota(jnp.int32, shape, 1)
    return jnp.sum(jnp.where(same, row.astype(F32), 0.0), axis=1, keepdims=True)


def attention_kernel(
    near_ref, far_ref, q_ref, kv_ref, halo_ref, spot_ref, lane_ref, *rest
):
    heads_ref, send_ref, keys, values, spread = rest[-5:]
    blocks = kv_ref.shape[0]
    together = keys.shape[0]
    nears, fars = near_ref.shape[1], far_ref.shape[1]
    low = lax.broadcasted_iota(jnp.int32, (ROWS_BLK, LANES), 1) < HEAD_DIM

    @pl.loop(0, blocks // together)
    def _(i):
        at = [i * together + t for t in range(together)]
        at_rows = [pl.ds(pl.multiple_of(b * ROWS_BLK, ROWS_BLK), ROWS_BLK) for b in at]
        scores = []
        for t, (b, rows) in enumerate(zip(at, at_rows)):
            q = q_ref[rows, :].astype(F32)
            both = jnp.concatenate([jnp.where(low, q, 0.0), jnp.where(low, 0.0, q)], axis=0).astype(BF16)
            for j in range(nears + fars):
                if j < nears:
                    block = kv_ref[near_ref[b, j]]
                else:
                    block = halo_ref[far_ref[b, j - nears]]
                keys[t, j * ROWS_BLK : (j + 1) * ROWS_BLK, :] = block[:, :LANES]
                values[t, j * ROWS_BLK : (j + 1) * ROWS_BLK, :] = block[:, LANES:]
            scores.append(
                lax.dot_general(both, keys[t], (((1,), (1,)), ((), ())), preferred_element_type=F32)
            )
        for t, rows in enumerate(at_rows):
            largest = jnp.max(scores[t], axis=1, keepdims=True)
            expo = jnp.exp(scores[t] - largest)
            total = jnp.sum(expo, axis=1, keepdims=True)
            out = jnp.dot(expo.astype(BF16), values[t], preferred_element_type=F32) / total
            heads = jnp.where(low, out[:ROWS_BLK], out[ROWS_BLK:])
            heads_ref[rows, :] = heads.astype(BF16)
            lane = as_column(lane_ref[:, rows])
            for m in range(4):
                spread[rows, m * LANES : (m + 1) * LANES] = jnp.where(lane == m, heads, 0.0).astype(BF16)

    dests, cap = send_ref.shape[0], send_ref.shape[2]
    step = 4

    @pl.loop(0, dests // step)
    def _(i):
        tile = step * cap
        spot = spot_ref[...]
        here = lax.broadcasted_iota(jnp.int32, (tile, spot.shape[1]), 0) + i * tile
        hot = jnp.where(here == spot, 1.0, 0.0).astype(BF16)
        placed = jnp.dot(hot, spread[...], preferred_element_type=F32).astype(BF16)
        for d in range(step):
            for m in range(4):
                send_ref[i * step + d, m] = placed[d * cap : (d + 1) * cap, m * LANES : (m + 1) * LANES]


def attention(near, far, q, kv, halo, spot_row, lane_row, after, parts, cap, together=4):
    rows = q.shape[0]
    keys = (near.shape[1] + far.shape[1]) * ROWS_BLK
    return pl.pallas_call(
        attention_kernel,
        in_specs=[SMEM, SMEM, VMEM, VMEM, VMEM, VMEM, VMEM] + [ANY] * len(after),
        out_specs=[VMEM, VMEM],
        out_shape=[
            jax.ShapeDtypeStruct((rows, LANES), BF16),
            jax.ShapeDtypeStruct((parts, 4, cap, LANES), BF16),
        ],
        scratch_shapes=[
            pltpu.VMEM((together, keys, LANES), BF16),
            pltpu.VMEM((together, keys, LANES), BF16),
            pltpu.VMEM((rows, 4 * LANES), BF16),
        ],
        compiler_params=params(60),
        cost_estimate=cost(12 * 10**9, 8 * 2**20, 2 * rows * keys),
        name="attention",
    )(near, far, q, kv, halo, spot_row, lane_row, *after)


def place_kernel(spot_ref, x_ref, *rest):
    out_ref = rest[-1]
    dests, cap = out_ref.shape[0], out_ref.shape[1]
    step = 4

    @pl.loop(0, dests // step)
    def _(i):
        tile = step * cap
        spot = spot_ref[...]
        here = lax.broadcasted_iota(jnp.int32, (tile, spot.shape[1]), 0) + i * tile
        hot = jnp.where(here == spot, 1.0, 0.0).astype(BF16)
        placed = jnp.dot(hot, x_ref[...], preferred_element_type=F32).astype(BF16)
        for d in range(step):
            out_ref[i * step + d] = placed[d * cap : (d + 1) * cap, :]


def place_rows(spot_row, x, after, parts, cap):
    rows, width = x.shape
    return pl.pallas_call(
        place_kernel,
        in_specs=[VMEM, VMEM] + [ANY] * len(after),
        out_specs=VMEM,
        out_shape=jax.ShapeDtypeStruct((parts, cap, width), BF16),
        compiler_params=params(60),
        cost_estimate=cost(2 * parts * cap * rows * width, 4 * 2**20),
        name="place_rows",
    )(spot_row, x, *after)


def experts_kernel(me_ref, gain_ref, route_ref, h_ref, x_ref, w0_ref, w1_ref, w2_ref, w3_ref, *rest):
    out_ref, heads, features, project, quarters, results, sems = rest[-7:]
    me = me_ref[0]
    tiles, step, cap, width = features.shape
    tile = step * cap
    sources = (w0_ref, w1_ref, w2_ref, w3_ref)
    sizes = ((h_ref, heads), (x_ref, features))
    small = [
        pltpu.make_async_copy(
            w.at[pl.ds(3 * width, LANES)], project.at[pl.ds(k * LANES, LANES)], sems.at[k]
        )
        for k, w in enumerate(sources)
    ]
    large = [
        pltpu.make_async_copy(w.at[pl.ds(0, 3 * width)], quarters.at[k], sems.at[4 + k])
        for k, w in enumerate(sources)
    ]
    rows = [
        [
            pltpu.make_async_copy(source.at[pl.ds(t * step, step)], target.at[t], sems.at[8 + 2 * t + i])
            for i, (source, target) in enumerate(sizes)
        ]
        for t in range(tiles)
    ]
    outs = [
        pltpu.make_async_copy(
            results.at[t], out_ref.at[pl.ds(t * step, step)], sems.at[8 + 2 * tiles + t]
        )
        for t in range(tiles)
    ]
    for copy in rows[0] + small + large + [c for later in rows[1:] for c in later]:
        copy.start()
    for copy in small:
        copy.wait()
    for t in range(tiles):
        for copy in rows[t]:
            copy.wait()
        arrived = jnp.concatenate([heads[t, :, me ^ k].reshape(tile, LANES) for k in range(4)], axis=1)
        mixed = features[t].reshape(tile, width).astype(F32) + jnp.dot(
            arrived, project[...], preferred_element_type=F32
        )
        mean = jnp.mean(mixed * mixed, axis=1, keepdims=True)
        normed = (mixed * lax.rsqrt(mean + EPS) * gain_ref[...]).astype(BF16)
        logit = jnp.sum(normed.astype(F32) * route_ref[...], axis=1, keepdims=True)
        gate = 1.0 / (1.0 + jnp.exp(-logit))
        result = None
        for k in range(4):
            if t == 0:
                large[k].wait()
            left = jnp.dot(normed, quarters[k, :width, :], preferred_element_type=F32)
            right = jnp.dot(normed, quarters[k, width : 2 * width, :], preferred_element_type=F32)
            half = 0.5 * left
            hidden = ((half + half * jnp.tanh(half)) * right).astype(BF16)
            term = jnp.dot(hidden, quarters[k, 2 * width :, :], preferred_element_type=F32)
            result = term if result is None else result + term
        result = (gate * result).astype(BF16).reshape(step, cap, width)
        for m in range(4):
            results[t, :, m] = result[:, :, m * LANES : (m + 1) * LANES]
        outs[t].start()
    for copy in outs:
        copy.wait()


def experts(me, heads, x, gain, route, weights, after, tiles=2):
    parts, cap, width = x.shape
    step = parts // tiles
    return pl.pallas_call(
        experts_kernel,
        in_specs=[SMEM, VMEM, VMEM, HBM, HBM] + [ANY] * (4 + len(after)),
        out_specs=HBM,
        out_shape=jax.ShapeDtypeStruct((parts, 4, cap, LANES), BF16),
        scratch_shapes=[
            pltpu.VMEM((tiles, step, 4, cap, LANES), BF16),
            pltpu.VMEM((tiles, step, cap, width), BF16),
            pltpu.VMEM((width, width), BF16),
            pltpu.VMEM((4, 3 * width, width), BF16),
            pltpu.VMEM((tiles, step, 4, cap, LANES), BF16),
            pltpu.SemaphoreType.DMA((8 + 3 * tiles,)),
        ],
        compiler_params=params(59),
        cost_estimate=cost(2 * parts * cap * width * (12 * width + width), 12 * 2**20),
        name="experts",
    )(me, gain, route, heads, x, *weights, *after)


def columns_kernel(
    me_ref, h0_ref, h1_ref, h3_ref, top_ref, bottom_ref, w0_ref, w1_ref, w2_ref, w3_ref, x_ref, attn_ref, mixed_ref
):
    columns = pl.ds(pl.multiple_of(me_ref[0] * LANES, LANES), LANES)
    half = top_ref.shape[0]
    for start, h2_ref in ((0, top_ref), (half, bottom_ref)):
        rows = slice(start, start + half)
        pieces = [h0_ref[rows, :], h1_ref[rows, :], h2_ref[...], h3_ref[rows, :]]
        weights = [w[:, columns] for w in (w0_ref, w1_ref, w2_ref, w3_ref)]
        total = jnp.dot(
            jnp.concatenate(pieces, axis=1), jnp.concatenate(weights, axis=0), preferred_element_type=F32
        )
        attn_ref[rows, :] = total.astype(BF16)
        mixed_ref[rows, :] = x_ref[rows, columns].astype(F32) + total


def attention_columns(me, heads, by_one, by_three, relayed, weights, x):
    rows, width = x.shape
    last = weights[0].shape[0] // LANES - 1
    out = pl.BlockSpec((rows, LANES), lambda i: (0, 0))
    half = pl.BlockSpec((rows // 2, LANES), lambda i: (0, 0))
    return pl.pallas_call(
        columns_kernel,
        grid=(1,),
        in_specs=[SMEM]
        + [out] * 3
        + [half] * 2
        + [pl.BlockSpec((LANES, width), lambda i: (last, 0))] * 4
        + [pl.BlockSpec((rows, width), lambda i: (0, 0))],
        out_specs=[out, out],
        out_shape=[
            jax.ShapeDtypeStruct((rows, LANES), BF16),
            jax.ShapeDtypeStruct((rows, LANES), F32),
        ],
        compiler_params=params(60),
        cost_estimate=cost(2 * rows * width * LANES, 8 * 2**20),
        name="attention_columns",
    )(me, heads, by_one, by_three, *relayed, *weights, x)


def combine_kernel(spot_ref, lane_ref, mixed_hbm, back_ref, out_ref, slots, mixed_ref, sems):
    dests, cap, width = slots.shape
    rows = out_ref.shape[0]
    copies = [
        pltpu.make_async_copy(
            back_ref.at[:, m], slots.at[:, :, pl.ds(m * LANES, LANES)], sems.at[m]
        )
        for m in range(4)
    ]
    copies.append(pltpu.make_async_copy(mixed_hbm, mixed_ref, sems.at[4]))
    for copy in copies:
        copy.start()
    for copy in copies:
        copy.wait()
    tile = 256
    names = lax.broadcasted_iota(jnp.int32, (ROWS_BLK, dests * cap), 1).astype(F32)

    @pl.loop(0, rows // tile)
    def _(i):
        pieces = [
            pl.ds(pl.multiple_of(i * tile + t * ROWS_BLK, ROWS_BLK), ROWS_BLK) for t in range(tile // ROWS_BLK)
        ]
        hot = jnp.concatenate(
            [jnp.where(names == as_column(spot_ref[:, p]), 1.0, 0.0).astype(BF16) for p in pieces], axis=0
        )
        found = jnp.dot(hot, slots[...].reshape(dests * cap, width), preferred_element_type=F32)
        for t, p in enumerate(pieces):
            lane = as_column(lane_ref[:, p])
            total = mixed_ref[p, :]
            for m in range(4):
                part = found[t * ROWS_BLK : (t + 1) * ROWS_BLK, m * LANES : (m + 1) * LANES]
                total = total + jnp.where(lane == m, part, 0.0)
            out_ref[p, :] = total.astype(BF16)


def combine(spot_row, lane_row, back, mixed):
    rows = mixed.shape[0]
    slots = back.shape[0] * back.shape[2]
    return pl.pallas_call(
        combine_kernel,
        in_specs=[VMEM] * 2 + [HBM] * 2,
        out_specs=VMEM,
        out_shape=jax.ShapeDtypeStruct((rows, LANES), BF16),
        scratch_shapes=[
            pltpu.VMEM((back.shape[0], back.shape[2], 4 * LANES), BF16),
            pltpu.VMEM((rows, LANES), F32),
            pltpu.SemaphoreType.DMA((5,)),
        ],
        compiler_params=params(24),
        cost_estimate=cost(2 * rows * slots * 4 * LANES, 4 * 2**20),
        name="combine",
    )(spot_row, lane_row, mixed, back)


def swap(array, change):
    return lax.ppermute(array, "mp", [(i, i ^ change) for i in range(4)])


def exchange(array, axes):
    return lax.all_to_all(array, axes, split_axis=0, concat_axis=0, tiled=True)


def on_device(
    node_features,
    w_qkv,
    w_out,
    head_scale,
    norm_gain,
    router,
    w_gate,
    w_up,
    w_down,
    neighbor_blocks,
    expert_ids,
):
    parts = lax.axis_size("graph")
    part = lax.axis_index("graph")
    me = lax.axis_index("mp")
    rows, width = node_features.shape
    blocks = rows // ROWS_BLK
    half_cap = CAP_E // 2

    far = neighbor_blocks[:, LOCAL_REFS:]
    names = jnp.arange(parts * blocks, dtype=jnp.int32).reshape(parts, blocks)
    wanted = jnp.any(far.reshape(-1)[:, None, None] == names[None], axis=0)
    inside = jnp.arange(blocks, dtype=jnp.int32)[None, :]
    first = jnp.min(jnp.where(wanted, inside, blocks - 1), axis=1)
    last = jnp.max(jnp.where(wanted, inside, 0), axis=1)
    requests = jnp.stack([first, last], axis=1)
    incoming = exchange(requests.reshape(parts, 1, CAP_H), "graph")
    bases = jnp.arange(parts, dtype=jnp.int32)[:, None] * blocks
    pool = (bases + requests).reshape(-1)
    slots = jnp.arange(pool.shape[0], dtype=jnp.int32)
    far_slots = jnp.max(jnp.where(far[:, :, None] == pool[None, None, :], slots[None, None, :], 0), axis=2)
    near_slots = neighbor_blocks[:, :LOCAL_REFS] - part * blocks

    which = me // 2
    me_ref = me[None].astype(jnp.int32)
    kept, given = split_weights(me_ref, w_gate, w_up, w_down, w_out)
    weights = [kept, swap(kept, 1), swap(given, 2), swap(given, 3)]

    q, kv = qkv(node_features, w_qkv, head_scale, kept)
    halo = exchange(pick_blocks(incoming, kv), "graph")

    routed = expert_ids[:, 0]
    experts_all = router.shape[1]
    chosen = routed[:, None] == jnp.arange(experts_all, dtype=jnp.int32)[None, :]
    row_ids = jnp.arange(rows, dtype=jnp.int32)
    earlier = (row_ids[:, None] > row_ids[None, :]).astype(BF16)
    before = jnp.dot(earlier, chosen.astype(BF16), preferred_element_type=F32)
    rank = jnp.sum(jnp.where(chosen, before, 0.0), axis=1).astype(jnp.int32)
    second = (rank >= half_cap).astype(jnp.int32)
    lane = (routed % 2) * 2 + second
    spot = (routed // 2) * half_cap + rank - second * half_cap
    spot_row, lane_row = spot[None, :], lane[None, :]
    mine_row = jnp.where(lane == me, spot, -1)[None, :]
    x_there = exchange(place_rows(mine_row, node_features, (near_slots, far_slots), parts, half_cap), "graph")

    route = lax.dynamic_index_in_dim(router, 2 * part + which, 1, keepdims=False).astype(F32)[None, :]
    heads, send = attention(
        near_slots, far_slots, q, kv, halo, spot_row, lane_row, weights[1:2], parts, half_cap
    )
    send, x_there, weights[2:] = lax.optimization_barrier((send, x_there, weights[2:]))
    heads_there = exchange(send.reshape(parts * 4, half_cap, LANES), ("graph", "mp"))
    by_one, by_three = swap(heads, 1), swap(heads, 3)
    middle = rows // 2
    relayed = [swap(by_three[:middle], 1), swap(by_one[middle:], 3)]
    attn_out, mixed = attention_columns(
        me_ref, heads, by_one, by_three, relayed, weights, node_features
    )

    produced = experts(
        me_ref,
        heads_there.reshape(parts, 4, half_cap, LANES),
        x_there,
        norm_gain[None, :],
        route,
        weights,
        (by_one, by_three),
    )
    back = exchange(produced.reshape(parts * 4, half_cap, LANES), ("graph", "mp"))
    layer_out = combine(spot_row, lane_row, back.reshape(parts, 4, half_cap, LANES), mixed)
    return (attn_out, layer_out)


def solution(mesh):
    placed = (
        P("graph", None),
        P(None, None, "mp"),
        P("mp", None),
        P("mp"),
        P(),
        P(),
        P("graph", None, "mp"),
        P("graph", None, "mp"),
        P("graph", "mp", None),
        P("graph", None),
        P("graph", None),
    )
    return jax.shard_map(
        on_device,
        mesh=mesh,
        in_specs=placed,
        out_specs=(P("graph", "mp"), P("graph", "mp")),
        check_vma=False,
    )
```

```python
import math

import jax
import jax.numpy as jnp
from jax import lax
from jax.experimental import pallas as pl
from jax.experimental.pallas import tpu as pltpu
from jax.sharding import PartitionSpec as P

HEAD_DIM = 64
ROWS_BLK = 128
LOCAL_REFS = 4
CAP_H = 2
CAP_E = 96
EPS = 1e-06
LANES = 128

VMEM = pl.BlockSpec(memory_space=pltpu.VMEM)
SMEM = pl.BlockSpec(memory_space=pltpu.SMEM)
ANY = pl.BlockSpec(memory_space=pl.ANY)
HBM = pl.BlockSpec(memory_space=pltpu.HBM)
F32 = jnp.float32
BF16 = jnp.bfloat16


def params(mebibytes):
    return pltpu.CompilerParams(vmem_limit_bytes=mebibytes * 2**20)


def cost(flops, moved, transcendentals=0):
    return pl.CostEstimate(flops=flops, bytes_accessed=moved, transcendentals=transcendentals)


def head_units(values):
    low = lax.broadcasted_iota(jnp.int32, values.shape, 1) < HEAD_DIM
    squares = values * values
    first = jnp.sum(jnp.where(low, squares, 0.0), axis=1, keepdims=True)
    second = jnp.sum(jnp.where(low, 0.0, squares), axis=1, keepdims=True)
    scale = lax.rsqrt(jnp.where(low, first, second) * (1.0 / HEAD_DIM) + EPS)
    return values * scale


def qkv_kernel(x_ref, w_ref, scale_ref, q_ref, kv_ref):
    x = x_ref[...]
    rows = x.shape[0]
    query = jnp.dot(x, w_ref[0], preferred_element_type=F32)
    low = lax.broadcasted_iota(jnp.int32, (1, LANES), 1) < HEAD_DIM
    scale = jnp.where(low, scale_ref[0], scale_ref[1]) * (1.0 / math.sqrt(HEAD_DIM))
    q_ref[...] = (head_units(query) * scale).astype(BF16)
    key = jnp.dot(x, w_ref[1], preferred_element_type=F32)
    value = jnp.dot(x, w_ref[2], preferred_element_type=F32)
    kv_ref[:, :, :LANES] = head_units(key).astype(BF16).reshape(rows // ROWS_BLK, ROWS_BLK, LANES)
    kv_ref[:, :, LANES:] = value.astype(BF16).reshape(rows // ROWS_BLK, ROWS_BLK, LANES)


def qkv(x, w, scale):
    rows, width = x.shape
    tile = 512
    blocks = tile // ROWS_BLK
    return pl.pallas_call(
        qkv_kernel,
        grid=(rows // tile,),
        in_specs=[
            pl.BlockSpec((tile, width), lambda i: (i, 0)),
            pl.BlockSpec((3, width, LANES), lambda i: (0, 0, 0)),
            SMEM,
        ],
        out_specs=[
            pl.BlockSpec((tile, LANES), lambda i: (i, 0)),
            pl.BlockSpec((blocks, ROWS_BLK, 2 * LANES), lambda i: (i, 0, 0)),
        ],
        out_shape=[
            jax.ShapeDtypeStruct((rows, LANES), BF16),
            jax.ShapeDtypeStruct((rows // ROWS_BLK, ROWS_BLK, 2 * LANES), BF16),
        ],
        compiler_params=params(60),
        cost_estimate=cost(2 * rows * width * 3 * LANES, 2 * rows * (width + 3 * LANES)),
        name="qkv",
    )(x, w, scale)


def requests_kernel(near_ref, out_ref):
    parts = out_ref.shape[0]
    rows, listed = near_ref.shape
    shape = (parts, rows)
    inside = lax.broadcasted_iota(jnp.int32, shape, 1)
    names = lax.broadcasted_iota(jnp.int32, shape, 0) * rows + inside
    wanted = jnp.zeros(shape, jnp.int32)
    for i in range(rows):
        for j in range(LOCAL_REFS, listed):
            wanted = jnp.where(names == near_ref[i, j], 1, wanted)
    first = jnp.min(jnp.where(wanted == 1, inside, rows - 1), axis=1, keepdims=True)
    last = jnp.max(jnp.where(wanted == 1, inside, 0), axis=1, keepdims=True)
    lane = lax.broadcasted_iota(jnp.int32, (parts, CAP_H), 1)
    out_ref[...] = jnp.where(lane == 0, first, last)


def make_requests(neighbor_blocks, parts):
    return pl.pallas_call(
        requests_kernel,
        in_specs=[SMEM],
        out_specs=VMEM,
        out_shape=jax.ShapeDtypeStruct((parts, CAP_H), jnp.int32),
        compiler_params=params(60),
        name="make_requests",
    )(neighbor_blocks)


def split_kernel(me_ref, gate_ref, up_ref, down_ref, out_w_ref, _, kept_ref, given_ref, sems):
    which = me_ref[0] // 2
    width = gate_ref.shape[1]
    copies = []
    for target, index in ((kept_ref, which), (given_ref, 1 - which)):
        for i, source in enumerate((gate_ref, up_ref, down_ref)):
            copies.append((source.at[index], target.at[pl.ds(i * width, width)]))
        copies.append((out_w_ref, target.at[pl.ds(3 * width, LANES)]))
    copies = [pltpu.make_async_copy(a, b, sems.at[i]) for i, (a, b) in enumerate(copies)]
    for copy in copies:
        copy.start()
    for copy in copies:
        copy.wait()


def split_weights(me, gate, up, down, out_w, after):
    width = gate.shape[1]
    out = jax.ShapeDtypeStruct((3 * width + LANES, width), BF16)
    return pl.pallas_call(
        split_kernel,
        in_specs=[SMEM] + [VMEM] * 4 + [ANY],
        out_specs=[HBM, HBM],
        out_shape=[out, out],
        scratch_shapes=[pltpu.SemaphoreType.DMA((8,))],
        compiler_params=params(60),
        cost_estimate=cost(0, 4 * out.size * 2),
        name="split_weights",
    )(me, gate, up, down, out_w, after)


def pick_kernel(wanted_ref, kv_ref, out_ref, sems):
    count = out_ref.shape[0]
    copies = [
        pltpu.make_async_copy(
            kv_ref.at[wanted_ref[i // CAP_H, 0, i % CAP_H]], out_ref.at[i], sems.at[i]
        )
        for i in range(count)
    ]
    for copy in copies:
        copy.start()
    for copy in copies:
        copy.wait()


def pick_blocks(wanted, kv):
    count = wanted.size
    out = jax.ShapeDtypeStruct((count,) + kv.shape[1:], kv.dtype)
    return pl.pallas_call(
        pick_kernel,
        in_specs=[SMEM, VMEM],
        out_specs=HBM,
        out_shape=out,
        scratch_shapes=[pltpu.SemaphoreType.DMA((count,))],
        compiler_params=params(60),
        cost_estimate=cost(0, 2 * out.size * 2),
        name="pick_blocks",
    )(wanted, kv)


def as_column(row):
    count = row.shape[1]
    shape = (count, count)
    same = lax.broadcasted_iota(jnp.int32, shape, 0) == lax.broadcasted_iota(jnp.int32, shape, 1)
    return jnp.sum(jnp.where(same, row.astype(F32), 0.0), axis=1, keepdims=True)


def attention_kernel(
    near_ref, asked_ref, q_ref, kv_ref, halo_ref, spot_ref, lane_ref, *rest
):
    heads_ref, send_ref, keys, values, spread = rest[-5:]
    blocks = kv_ref.shape[0]
    together = keys.shape[0]
    listed = near_ref.shape[1]
    low = lax.broadcasted_iota(jnp.int32, (ROWS_BLK, LANES), 1) < HEAD_DIM

    @pl.loop(0, blocks // together)
    def _(i):
        at = [i * together + t for t in range(together)]
        at_rows = [pl.ds(pl.multiple_of(b * ROWS_BLK, ROWS_BLK), ROWS_BLK) for b in at]
        scores = []
        for t, (b, rows) in enumerate(zip(at, at_rows)):
            q = q_ref[rows, :].astype(F32)
            both = jnp.concatenate([jnp.where(low, q, 0.0), jnp.where(low, 0.0, q)], axis=0).astype(BF16)
            for j in range(listed):
                name = near_ref[b, j]
                owner = name // blocks
                inside = name - owner * blocks
                if j < LOCAL_REFS:
                    block = kv_ref[inside]
                else:
                    second = (inside != asked_ref[owner, 0]).astype(jnp.int32)
                    block = halo_ref[owner * CAP_H + second]
                keys[t, j * ROWS_BLK : (j + 1) * ROWS_BLK, :] = block[:, :LANES]
                values[t, j * ROWS_BLK : (j + 1) * ROWS_BLK, :] = block[:, LANES:]
            scores.append(
                lax.dot_general(both, keys[t], (((1,), (1,)), ((), ())), preferred_element_type=F32)
            )
        for t, rows in enumerate(at_rows):
            largest = jnp.max(scores[t], axis=1, keepdims=True)
            expo = jnp.exp(scores[t] - largest)
            total = jnp.sum(expo, axis=1, keepdims=True)
            out = jnp.dot(expo.astype(BF16), values[t], preferred_element_type=F32) / total
            heads = jnp.where(low, out[:ROWS_BLK], out[ROWS_BLK:])
            heads_ref[rows, :] = heads.astype(BF16)
            lane = as_column(lane_ref[:, rows])
            for m in range(4):
                spread[rows, m * LANES : (m + 1) * LANES] = jnp.where(lane == m, heads, 0.0).astype(BF16)

    dests, cap = send_ref.shape[0], send_ref.shape[2]
    step = 4

    @pl.loop(0, dests // step)
    def _(i):
        tile = step * cap
        spot = spot_ref[...]
        here = lax.broadcasted_iota(jnp.int32, (tile, spot.shape[1]), 0) + i * tile
        hot = jnp.where(here == spot, 1.0, 0.0).astype(BF16)
        placed = jnp.dot(hot, spread[...], preferred_element_type=F32).astype(BF16)
        for d in range(step):
            for m in range(4):
                send_ref[i * step + d, m] = placed[d * cap : (d + 1) * cap, m * LANES : (m + 1) * LANES]


def attention(near, asked, q, kv, halo, spot_row, lane_row, after, parts, cap, together=4):
    rows = q.shape[0]
    keys = near.shape[1] * ROWS_BLK
    return pl.pallas_call(
        attention_kernel,
        in_specs=[SMEM, SMEM, VMEM, VMEM, VMEM, VMEM, VMEM] + [ANY] * len(after),
        out_specs=[VMEM, VMEM],
        out_shape=[
            jax.ShapeDtypeStruct((rows, LANES), BF16),
            jax.ShapeDtypeStruct((parts, 4, cap, LANES), BF16),
        ],
        scratch_shapes=[
            pltpu.VMEM((together, keys, LANES), BF16),
            pltpu.VMEM((together, keys, LANES), BF16),
            pltpu.VMEM((rows, 4 * LANES), BF16),
        ],
        compiler_params=params(60),
        cost_estimate=cost(12 * 10**9, 8 * 2**20, 2 * rows * keys),
        name="attention",
    )(near, asked, q, kv, halo, spot_row, lane_row, *after)


def place_kernel(spot_ref, x_ref, out_ref):
    dests, cap = out_ref.shape[0], out_ref.shape[1]
    step = 4

    @pl.loop(0, dests // step)
    def _(i):
        tile = step * cap
        spot = spot_ref[...]
        here = lax.broadcasted_iota(jnp.int32, (tile, spot.shape[1]), 0) + i * tile
        hot = jnp.where(here == spot, 1.0, 0.0).astype(BF16)
        placed = jnp.dot(hot, x_ref[...], preferred_element_type=F32).astype(BF16)
        for d in range(step):
            out_ref[i * step + d] = placed[d * cap : (d + 1) * cap, :]


def place_rows(spot_row, x, parts, cap):
    rows, width = x.shape
    return pl.pallas_call(
        place_kernel,
        in_specs=[VMEM, VMEM],
        out_specs=VMEM,
        out_shape=jax.ShapeDtypeStruct((parts, cap, width), BF16),
        compiler_params=params(60),
        cost_estimate=cost(2 * parts * cap * rows * width, 4 * 2**20),
        name="place_rows",
    )(spot_row, x)


def experts_kernel(me_ref, gain_ref, route_ref, h_ref, x_ref, w0_ref, w1_ref, w2_ref, w3_ref, *rest):
    out_ref, heads, features, project, quarters, results, sems = rest[-7:]
    me = me_ref[0]
    tiles, step, cap, width = features.shape
    tile = step * cap
    sources = (w0_ref, w1_ref, w2_ref, w3_ref)
    sizes = ((h_ref, heads), (x_ref, features))
    small = [
        pltpu.make_async_copy(
            w.at[pl.ds(3 * width, LANES)], project.at[pl.ds(k * LANES, LANES)], sems.at[k]
        )
        for k, w in enumerate(sources)
    ]
    large = [
        pltpu.make_async_copy(w.at[pl.ds(0, 3 * width)], quarters.at[k], sems.at[4 + k])
        for k, w in enumerate(sources)
    ]
    rows = [
        [
            pltpu.make_async_copy(source.at[pl.ds(t * step, step)], target.at[t], sems.at[8 + 2 * t + i])
            for i, (source, target) in enumerate(sizes)
        ]
        for t in range(tiles)
    ]
    outs = [
        pltpu.make_async_copy(
            results.at[t], out_ref.at[pl.ds(t * step, step)], sems.at[8 + 2 * tiles + t]
        )
        for t in range(tiles)
    ]
    for copy in rows[0] + small + large + [c for later in rows[1:] for c in later]:
        copy.start()
    for copy in small:
        copy.wait()
    for t in range(tiles):
        for copy in rows[t]:
            copy.wait()
        arrived = jnp.concatenate([heads[t, :, me ^ k].reshape(tile, LANES) for k in range(4)], axis=1)
        mixed = features[t].reshape(tile, width).astype(F32) + jnp.dot(
            arrived, project[...], preferred_element_type=F32
        )
        mean = jnp.mean(mixed * mixed, axis=1, keepdims=True)
        normed = (mixed * lax.rsqrt(mean + EPS) * gain_ref[...]).astype(BF16)
        logit = jnp.sum(normed.astype(F32) * route_ref[...], axis=1, keepdims=True)
        gate = 1.0 / (1.0 + jnp.exp(-logit))
        result = None
        for k in range(4):
            if t == 0:
                large[k].wait()
            left = jnp.dot(normed, quarters[k, :width, :], preferred_element_type=F32)
            right = jnp.dot(normed, quarters[k, width : 2 * width, :], preferred_element_type=F32)
            half = 0.5 * left
            hidden = ((half + half * jnp.tanh(half)) * right).astype(BF16)
            term = jnp.dot(hidden, quarters[k, 2 * width :, :], preferred_element_type=F32)
            result = term if result is None else result + term
        result = (gate * result).astype(BF16).reshape(step, cap, width)
        for m in range(4):
            results[t, :, m] = result[:, :, m * LANES : (m + 1) * LANES]
        outs[t].start()
    for copy in outs:
        copy.wait()


def experts(me, heads, x, gain, route, weights, after, tiles=2):
    parts, cap, width = x.shape
    step = parts // tiles
    return pl.pallas_call(
        experts_kernel,
        in_specs=[SMEM, VMEM, VMEM, HBM, HBM] + [ANY] * (4 + len(after)),
        out_specs=HBM,
        out_shape=jax.ShapeDtypeStruct((parts, 4, cap, LANES), BF16),
        scratch_shapes=[
            pltpu.VMEM((tiles, step, 4, cap, LANES), BF16),
            pltpu.VMEM((tiles, step, cap, width), BF16),
            pltpu.VMEM((width, width), BF16),
            pltpu.VMEM((4, 3 * width, width), BF16),
            pltpu.VMEM((tiles, step, 4, cap, LANES), BF16),
            pltpu.SemaphoreType.DMA((8 + 3 * tiles,)),
        ],
        compiler_params=params(58),
        cost_estimate=cost(2 * parts * cap * width * (12 * width + width), 12 * 2**20),
        name="experts",
    )(me, gain, route, heads, x, *weights, *after)


def columns_kernel(
    me_ref, h0_ref, h1_ref, h3_ref, top_ref, bottom_ref, w0_ref, w1_ref, w2_ref, w3_ref, x_ref, attn_ref, mixed_ref
):
    columns = pl.ds(pl.multiple_of(me_ref[0] * LANES, LANES), LANES)
    half = top_ref.shape[0]
    for start, h2_ref in ((0, top_ref), (half, bottom_ref)):
        rows = slice(start, start + half)
        pieces = [h0_ref[rows, :], h1_ref[rows, :], h2_ref[...], h3_ref[rows, :]]
        weights = [w[:, columns] for w in (w0_ref, w1_ref, w2_ref, w3_ref)]
        total = jnp.dot(
            jnp.concatenate(pieces, axis=1), jnp.concatenate(weights, axis=0), preferred_element_type=F32
        )
        attn_ref[rows, :] = total.astype(BF16)
        mixed_ref[rows, :] = x_ref[rows, columns].astype(F32) + total


def attention_columns(me, heads, by_one, by_three, relayed, weights, x):
    rows, width = x.shape
    last = weights[0].shape[0] // LANES - 1
    out = pl.BlockSpec((rows, LANES), lambda i: (0, 0))
    half = pl.BlockSpec((rows // 2, LANES), lambda i: (0, 0))
    return pl.pallas_call(
        columns_kernel,
        grid=(1,),
        in_specs=[SMEM]
        + [out] * 3
        + [half] * 2
        + [pl.BlockSpec((LANES, width), lambda i: (last, 0))] * 4
        + [pl.BlockSpec((rows, width), lambda i: (0, 0))],
        out_specs=[out, out],
        out_shape=[
            jax.ShapeDtypeStruct((rows, LANES), BF16),
            jax.ShapeDtypeStruct((rows, LANES), F32),
        ],
        compiler_params=params(60),
        cost_estimate=cost(2 * rows * width * LANES, 8 * 2**20),
        name="attention_columns",
    )(me, heads, by_one, by_three, *relayed, *weights, x)


def combine_kernel(spot_ref, lane_ref, mixed_hbm, back_ref, out_ref, slots, mixed_ref, sems):
    dests, cap, width = slots.shape
    rows = out_ref.shape[0]
    copies = [
        pltpu.make_async_copy(
            back_ref.at[:, m], slots.at[:, :, pl.ds(m * LANES, LANES)], sems.at[m]
        )
        for m in range(4)
    ]
    copies.append(pltpu.make_async_copy(mixed_hbm, mixed_ref, sems.at[4]))
    for copy in copies:
        copy.start()
    for copy in copies:
        copy.wait()
    tile = 256
    names = lax.broadcasted_iota(jnp.int32, (ROWS_BLK, dests * cap), 1).astype(F32)

    @pl.loop(0, rows // tile)
    def _(i):
        pieces = [
            pl.ds(pl.multiple_of(i * tile + t * ROWS_BLK, ROWS_BLK), ROWS_BLK) for t in range(tile // ROWS_BLK)
        ]
        hot = jnp.concatenate(
            [jnp.where(names == as_column(spot_ref[:, p]), 1.0, 0.0).astype(BF16) for p in pieces], axis=0
        )
        found = jnp.dot(hot, slots[...].reshape(dests * cap, width), preferred_element_type=F32)
        for t, p in enumerate(pieces):
            lane = as_column(lane_ref[:, p])
            total = mixed_ref[p, :]
            for m in range(4):
                part = found[t * ROWS_BLK : (t + 1) * ROWS_BLK, m * LANES : (m + 1) * LANES]
                total = total + jnp.where(lane == m, part, 0.0)
            out_ref[p, :] = total.astype(BF16)


def combine(spot_row, lane_row, back, mixed):
    rows = mixed.shape[0]
    slots = back.shape[0] * back.shape[2]
    return pl.pallas_call(
        combine_kernel,
        in_specs=[VMEM] * 2 + [HBM] * 2,
        out_specs=VMEM,
        out_shape=jax.ShapeDtypeStruct((rows, LANES), BF16),
        scratch_shapes=[
            pltpu.VMEM((back.shape[0], back.shape[2], 4 * LANES), BF16),
            pltpu.VMEM((rows, LANES), F32),
            pltpu.SemaphoreType.DMA((5,)),
        ],
        compiler_params=params(24),
        cost_estimate=cost(2 * rows * slots * 4 * LANES, 4 * 2**20),
        name="combine",
    )(spot_row, lane_row, mixed, back)


def swap(array, change):
    return lax.ppermute(array, "mp", [(i, i ^ change) for i in range(4)])


def exchange(array, axes):
    return lax.all_to_all(array, axes, split_axis=0, concat_axis=0, tiled=True)


def on_device(
    node_features,
    w_qkv,
    w_out,
    head_scale,
    norm_gain,
    router,
    w_gate,
    w_up,
    w_down,
    neighbor_blocks,
    expert_ids,
):
    parts = lax.axis_size("graph")
    part = lax.axis_index("graph")
    me = lax.axis_index("mp")
    rows, width = node_features.shape
    half_cap = CAP_E // 2

    requests = make_requests(neighbor_blocks, parts)
    incoming = exchange(requests.reshape(parts, 1, CAP_H), "graph")
    q, kv = qkv(node_features, w_qkv, head_scale)
    outgoing = pick_blocks(incoming, kv)
    halo = exchange(outgoing, "graph")

    which = me // 2
    me_ref = me[None].astype(jnp.int32)
    kept, given = split_weights(me_ref, w_gate, w_up, w_down, w_out, outgoing)
    weights = [kept, swap(kept, 1), swap(given, 2), swap(given, 3)]

    routed = expert_ids[:, 0]
    experts_all = router.shape[1]
    chosen = routed[:, None] == jnp.arange(experts_all, dtype=jnp.int32)[None, :]
    row_ids = jnp.arange(rows, dtype=jnp.int32)
    earlier = (row_ids[:, None] > row_ids[None, :]).astype(BF16)
    before = jnp.dot(earlier, chosen.astype(BF16), preferred_element_type=F32)
    rank = jnp.sum(jnp.where(chosen, before, 0.0), axis=1).astype(jnp.int32)
    second = (rank >= half_cap).astype(jnp.int32)
    lane = (routed % 2) * 2 + second
    spot = (routed // 2) * half_cap + rank - second * half_cap
    spot_row, lane_row = spot[None, :], lane[None, :]
    mine_row = jnp.where(lane == me, spot, -1)[None, :]
    x_there = exchange(place_rows(mine_row, node_features, parts, half_cap), "graph")

    route = lax.dynamic_index_in_dim(router, 2 * part + which, 1, keepdims=False).astype(F32)[None, :]
    heads, send = attention(
        neighbor_blocks, requests, q, kv, halo, spot_row, lane_row, weights[1:2], parts, half_cap
    )
    send, x_there, weights[2:] = lax.optimization_barrier((send, x_there, weights[2:]))
    heads_there = exchange(send.reshape(parts * 4, half_cap, LANES), ("graph", "mp"))
    heads, heads_there = lax.optimization_barrier((heads, heads_there))
    by_one, by_three = swap(heads, 1), swap(heads, 3)
    produced = experts(
        me_ref,
        heads_there.reshape(parts, 4, half_cap, LANES),
        x_there,
        norm_gain[None, :],
        route,
        weights,
        (),
    )
    produced, by_one, by_three = lax.optimization_barrier((produced, by_one, by_three))
    middle = rows // 2
    relayed = [swap(by_three[:middle], 1), swap(by_one[middle:], 3)]
    attn_out, mixed = attention_columns(
        me_ref, heads, by_one, by_three, relayed, weights, node_features
    )
    back = exchange(produced.reshape(parts * 4, half_cap, LANES), ("graph", "mp"))
    layer_out = combine(spot_row, lane_row, back.reshape(parts, 4, half_cap, LANES), mixed)
    return (attn_out, layer_out)


def solution(mesh):
    placed = (
        P("graph", None),
        P(None, None, "mp"),
        P("mp", None),
        P("mp"),
        P(),
        P(),
        P("graph", None, "mp"),
        P("graph", None, "mp"),
        P("graph", "mp", None),
        P("graph", None),
        P("graph", None),
    )
    return jax.shard_map(
        on_device,
        mesh=mesh,
        in_specs=placed,
        out_specs=(P("graph", "mp"), P("graph", "mp")),
        check_vma=False,
    )
```

```python
import math

import jax
import jax.numpy as jnp
from jax import lax
from jax.experimental import pallas as pl
from jax.experimental.pallas import tpu as pltpu
from jax.sharding import PartitionSpec as P

HEAD_DIM = 64
ROWS_BLK = 128
LOCAL_REFS = 4
CAP_H = 2
CAP_E = 96
EPS = 1e-06
LANES = 128

VMEM = pl.BlockSpec(memory_space=pltpu.VMEM)
SMEM = pl.BlockSpec(memory_space=pltpu.SMEM)
ANY = pl.BlockSpec(memory_space=pl.ANY)
HBM = pl.BlockSpec(memory_space=pltpu.HBM)
F32 = jnp.float32
BF16 = jnp.bfloat16


def params(mebibytes):
    return pltpu.CompilerParams(vmem_limit_bytes=mebibytes * 2**20)


def cost(flops, moved, transcendentals=0):
    return pl.CostEstimate(flops=flops, bytes_accessed=moved, transcendentals=transcendentals)


def head_units(values):
    low = lax.broadcasted_iota(jnp.int32, values.shape, 1) < HEAD_DIM
    squares = values * values
    first = jnp.sum(jnp.where(low, squares, 0.0), axis=1, keepdims=True)
    second = jnp.sum(jnp.where(low, 0.0, squares), axis=1, keepdims=True)
    scale = lax.rsqrt(jnp.where(low, first, second) * (1.0 / HEAD_DIM) + EPS)
    return values * scale


def qkv_kernel(x_ref, w_ref, scale_ref, q_ref, kv_ref):
    x = x_ref[...]
    rows = x.shape[0]
    query = jnp.dot(x, w_ref[0], preferred_element_type=F32)
    low = lax.broadcasted_iota(jnp.int32, (1, LANES), 1) < HEAD_DIM
    scale = jnp.where(low, scale_ref[0], scale_ref[1]) * (1.0 / math.sqrt(HEAD_DIM))
    q_ref[...] = (head_units(query) * scale).astype(BF16)
    key = jnp.dot(x, w_ref[1], preferred_element_type=F32)
    value = jnp.dot(x, w_ref[2], preferred_element_type=F32)
    kv_ref[:, :, :LANES] = head_units(key).astype(BF16).reshape(rows // ROWS_BLK, ROWS_BLK, LANES)
    kv_ref[:, :, LANES:] = value.astype(BF16).reshape(rows // ROWS_BLK, ROWS_BLK, LANES)


def qkv(x, w, scale):
    rows, width = x.shape
    tile = 512
    blocks = tile // ROWS_BLK
    return pl.pallas_call(
        qkv_kernel,
        grid=(rows // tile,),
        in_specs=[
            pl.BlockSpec((tile, width), lambda i: (i, 0)),
            pl.BlockSpec((3, width, LANES), lambda i: (0, 0, 0)),
            SMEM,
        ],
        out_specs=[
            pl.BlockSpec((tile, LANES), lambda i: (i, 0)),
            pl.BlockSpec((blocks, ROWS_BLK, 2 * LANES), lambda i: (i, 0, 0)),
        ],
        out_shape=[
            jax.ShapeDtypeStruct((rows, LANES), BF16),
            jax.ShapeDtypeStruct((rows // ROWS_BLK, ROWS_BLK, 2 * LANES), BF16),
        ],
        compiler_params=params(60),
        cost_estimate=cost(2 * rows * width * 3 * LANES, 2 * rows * (width + 3 * LANES)),
        name="qkv",
    )(x, w, scale)


def requests_kernel(near_ref, out_ref):
    parts = out_ref.shape[0]
    rows, listed = near_ref.shape
    shape = (parts, rows)
    inside = lax.broadcasted_iota(jnp.int32, shape, 1)
    names = lax.broadcasted_iota(jnp.int32, shape, 0) * rows + inside
    wanted = jnp.zeros(shape, jnp.int32)
    for i in range(rows):
        for j in range(LOCAL_REFS, listed):
            wanted = jnp.where(names == near_ref[i, j], 1, wanted)
    first = jnp.min(jnp.where(wanted == 1, inside, rows - 1), axis=1, keepdims=True)
    last = jnp.max(jnp.where(wanted == 1, inside, 0), axis=1, keepdims=True)
    lane = lax.broadcasted_iota(jnp.int32, (parts, CAP_H), 1)
    out_ref[...] = jnp.where(lane == 0, first, last)


def make_requests(neighbor_blocks, parts):
    return pl.pallas_call(
        requests_kernel,
        in_specs=[SMEM],
        out_specs=VMEM,
        out_shape=jax.ShapeDtypeStruct((parts, CAP_H), jnp.int32),
        compiler_params=params(60),
        name="make_requests",
    )(neighbor_blocks)


def split_kernel(me_ref, gate_ref, up_ref, down_ref, out_w_ref, _, kept_ref, given_ref, sems):
    which = me_ref[0] // 2
    width = gate_ref.shape[1]
    copies = []
    for target, index in ((kept_ref, which), (given_ref, 1 - which)):
        for i, source in enumerate((gate_ref, up_ref, down_ref)):
            copies.append((source.at[index], target.at[pl.ds(i * width, width)]))
        copies.append((out_w_ref, target.at[pl.ds(3 * width, LANES)]))
    copies = [pltpu.make_async_copy(a, b, sems.at[i]) for i, (a, b) in enumerate(copies)]
    for copy in copies:
        copy.start()
    for copy in copies:
        copy.wait()


def split_weights(me, gate, up, down, out_w, after):
    width = gate.shape[1]
    out = jax.ShapeDtypeStruct((3 * width + LANES, width), BF16)
    return pl.pallas_call(
        split_kernel,
        in_specs=[SMEM] + [VMEM] * 4 + [ANY],
        out_specs=[HBM, HBM],
        out_shape=[out, out],
        scratch_shapes=[pltpu.SemaphoreType.DMA((8,))],
        compiler_params=params(60),
        cost_estimate=cost(0, 4 * out.size * 2),
        name="split_weights",
    )(me, gate, up, down, out_w, after)


def pick_kernel(wanted_ref, kv_ref, out_ref, sems):
    count = out_ref.shape[0]
    copies = [
        pltpu.make_async_copy(
            kv_ref.at[wanted_ref[i // CAP_H, 0, i % CAP_H]], out_ref.at[i], sems.at[i]
        )
        for i in range(count)
    ]
    for copy in copies:
        copy.start()
    for copy in copies:
        copy.wait()


def pick_blocks(wanted, kv):
    count = wanted.size
    out = jax.ShapeDtypeStruct((count,) + kv.shape[1:], kv.dtype)
    return pl.pallas_call(
        pick_kernel,
        in_specs=[SMEM, VMEM],
        out_specs=HBM,
        out_shape=out,
        scratch_shapes=[pltpu.SemaphoreType.DMA((count,))],
        compiler_params=params(60),
        cost_estimate=cost(0, 2 * out.size * 2),
        name="pick_blocks",
    )(wanted, kv)


def as_column(row):
    count = row.shape[1]
    shape = (count, count)
    same = lax.broadcasted_iota(jnp.int32, shape, 0) == lax.broadcasted_iota(jnp.int32, shape, 1)
    return jnp.sum(jnp.where(same, row.astype(F32), 0.0), axis=1, keepdims=True)


def attention_kernel(
    near_ref, asked_ref, q_ref, kv_ref, halo_ref, spot_ref, lane_ref, *rest
):
    heads_ref, send_ref, keys, values, spread = rest[-5:]
    blocks = kv_ref.shape[0]
    together = keys.shape[0]
    listed = near_ref.shape[1]
    low = lax.broadcasted_iota(jnp.int32, (ROWS_BLK, LANES), 1) < HEAD_DIM

    @pl.loop(0, blocks // together)
    def _(i):
        at = [i * together + t for t in range(together)]
        at_rows = [pl.ds(pl.multiple_of(b * ROWS_BLK, ROWS_BLK), ROWS_BLK) for b in at]
        scores = []
        for t, (b, rows) in enumerate(zip(at, at_rows)):
            q = q_ref[rows, :].astype(F32)
            both = jnp.concatenate([jnp.where(low, q, 0.0), jnp.where(low, 0.0, q)], axis=0).astype(BF16)
            for j in range(listed):
                name = near_ref[b, j]
                owner = name // blocks
                inside = name - owner * blocks
                if j < LOCAL_REFS:
                    block = kv_ref[inside]
                else:
                    second = (inside != asked_ref[owner, 0]).astype(jnp.int32)
                    block = halo_ref[owner * CAP_H + second]
                keys[t, j * ROWS_BLK : (j + 1) * ROWS_BLK, :] = block[:, :LANES]
                values[t, j * ROWS_BLK : (j + 1) * ROWS_BLK, :] = block[:, LANES:]
            scores.append(
                lax.dot_general(both, keys[t], (((1,), (1,)), ((), ())), preferred_element_type=F32)
            )
        for t, rows in enumerate(at_rows):
            largest = jnp.max(scores[t], axis=1, keepdims=True)
            expo = jnp.exp(scores[t] - largest)
            total = jnp.sum(expo, axis=1, keepdims=True)
            out = jnp.dot(expo.astype(BF16), values[t], preferred_element_type=F32) / total
            heads = jnp.where(low, out[:ROWS_BLK], out[ROWS_BLK:])
            heads_ref[rows, :] = heads.astype(BF16)
            lane = as_column(lane_ref[:, rows])
            for m in range(4):
                spread[rows, m * LANES : (m + 1) * LANES] = jnp.where(lane == m, heads, 0.0).astype(BF16)

    dests, cap = send_ref.shape[0], send_ref.shape[2]
    step = 4

    @pl.loop(0, dests // step)
    def _(i):
        tile = step * cap
        spot = spot_ref[...]
        here = lax.broadcasted_iota(jnp.int32, (tile, spot.shape[1]), 0) + i * tile
        hot = jnp.where(here == spot, 1.0, 0.0).astype(BF16)
        placed = jnp.dot(hot, spread[...], preferred_element_type=F32).astype(BF16)
        for d in range(step):
            for m in range(4):
                send_ref[i * step + d, m] = placed[d * cap : (d + 1) * cap, m * LANES : (m + 1) * LANES]


def attention(near, asked, q, kv, halo, spot_row, lane_row, after, parts, cap, together=4):
    rows = q.shape[0]
    keys = near.shape[1] * ROWS_BLK
    return pl.pallas_call(
        attention_kernel,
        in_specs=[SMEM, SMEM, VMEM, VMEM, VMEM, VMEM, VMEM] + [ANY] * len(after),
        out_specs=[VMEM, VMEM],
        out_shape=[
            jax.ShapeDtypeStruct((rows, LANES), BF16),
            jax.ShapeDtypeStruct((parts, 4, cap, LANES), BF16),
        ],
        scratch_shapes=[
            pltpu.VMEM((together, keys, LANES), BF16),
            pltpu.VMEM((together, keys, LANES), BF16),
            pltpu.VMEM((rows, 4 * LANES), BF16),
        ],
        compiler_params=params(60),
        cost_estimate=cost(12 * 10**9, 8 * 2**20, 2 * rows * keys),
        name="attention",
    )(near, asked, q, kv, halo, spot_row, lane_row, *after)


def place_kernel(spot_ref, x_ref, out_ref):
    dests, cap = out_ref.shape[0], out_ref.shape[1]
    step = 4

    @pl.loop(0, dests // step)
    def _(i):
        tile = step * cap
        spot = spot_ref[...]
        here = lax.broadcasted_iota(jnp.int32, (tile, spot.shape[1]), 0) + i * tile
        hot = jnp.where(here == spot, 1.0, 0.0).astype(BF16)
        placed = jnp.dot(hot, x_ref[...], preferred_element_type=F32).astype(BF16)
        for d in range(step):
            out_ref[i * step + d] = placed[d * cap : (d + 1) * cap, :]


def place_rows(spot_row, x, parts, cap):
    rows, width = x.shape
    return pl.pallas_call(
        place_kernel,
        in_specs=[VMEM, VMEM],
        out_specs=VMEM,
        out_shape=jax.ShapeDtypeStruct((parts, cap, width), BF16),
        compiler_params=params(60),
        cost_estimate=cost(2 * parts * cap * rows * width, 4 * 2**20),
        name="place_rows",
    )(spot_row, x)


def experts_kernel(me_ref, gain_ref, route_ref, h_ref, x_ref, w0_ref, w1_ref, w2_ref, w3_ref, *rest):
    out_ref, heads, features, project, quarters, results, sems = rest[-7:]
    me = me_ref[0]
    tiles, step, cap, width = features.shape
    tile = step * cap
    sources = (w0_ref, w1_ref, w2_ref, w3_ref)
    sizes = ((h_ref, heads), (x_ref, features))
    small = [
        pltpu.make_async_copy(
            w.at[pl.ds(3 * width, LANES)], project.at[pl.ds(k * LANES, LANES)], sems.at[k]
        )
        for k, w in enumerate(sources)
    ]
    large = [
        pltpu.make_async_copy(w.at[pl.ds(0, 3 * width)], quarters.at[k], sems.at[4 + k])
        for k, w in enumerate(sources)
    ]
    rows = [
        [
            pltpu.make_async_copy(source.at[pl.ds(t * step, step)], target.at[t], sems.at[8 + 2 * t + i])
            for i, (source, target) in enumerate(sizes)
        ]
        for t in range(tiles)
    ]
    outs = [
        pltpu.make_async_copy(
            results.at[t], out_ref.at[pl.ds(t * step, step)], sems.at[8 + 2 * tiles + t]
        )
        for t in range(tiles)
    ]
    for copy in rows[0] + small + large + [c for later in rows[1:] for c in later]:
        copy.start()
    for copy in small:
        copy.wait()
    for t in range(tiles):
        for copy in rows[t]:
            copy.wait()
        arrived = jnp.concatenate([heads[t, :, me ^ k].reshape(tile, LANES) for k in range(4)], axis=1)
        mixed = features[t].reshape(tile, width).astype(F32) + jnp.dot(
            arrived, project[...], preferred_element_type=F32
        )
        mean = jnp.mean(mixed * mixed, axis=1, keepdims=True)
        normed = (mixed * lax.rsqrt(mean + EPS) * gain_ref[...]).astype(BF16)
        logit = jnp.sum(normed.astype(F32) * route_ref[...], axis=1, keepdims=True)
        gate = 1.0 / (1.0 + jnp.exp(-logit))
        result = None
        for k in range(4):
            if t == 0:
                large[k].wait()
            left = jnp.dot(normed, quarters[k, :width, :], preferred_element_type=F32)
            right = jnp.dot(normed, quarters[k, width : 2 * width, :], preferred_element_type=F32)
            half = 0.5 * left
            hidden = ((half + half * jnp.tanh(half)) * right).astype(BF16)
            term = jnp.dot(hidden, quarters[k, 2 * width :, :], preferred_element_type=F32)
            result = term if result is None else result + term
        result = (gate * result).astype(BF16).reshape(step, cap, width)
        for m in range(4):
            results[t, :, m] = result[:, :, m * LANES : (m + 1) * LANES]
        outs[t].start()
    for copy in outs:
        copy.wait()


def experts(me, heads, x, gain, route, weights, after, tiles=2):
    parts, cap, width = x.shape
    step = parts // tiles
    return pl.pallas_call(
        experts_kernel,
        in_specs=[SMEM, VMEM, VMEM, HBM, HBM] + [ANY] * (4 + len(after)),
        out_specs=HBM,
        out_shape=jax.ShapeDtypeStruct((parts, 4, cap, LANES), BF16),
        scratch_shapes=[
            pltpu.VMEM((tiles, step, 4, cap, LANES), BF16),
            pltpu.VMEM((tiles, step, cap, width), BF16),
            pltpu.VMEM((width, width), BF16),
            pltpu.VMEM((4, 3 * width, width), BF16),
            pltpu.VMEM((tiles, step, 4, cap, LANES), BF16),
            pltpu.SemaphoreType.DMA((8 + 3 * tiles,)),
        ],
        compiler_params=params(58),
        cost_estimate=cost(2 * parts * cap * width * (12 * width + width), 12 * 2**20),
        name="experts",
    )(me, gain, route, heads, x, *weights, *after)


def columns_kernel(
    me_ref, h0_ref, h1_ref, h3_ref, top_ref, bottom_ref, w0_ref, w1_ref, w2_ref, w3_ref, x_ref, attn_ref, mixed_ref
):
    columns = pl.ds(pl.multiple_of(me_ref[0] * LANES, LANES), LANES)
    half = top_ref.shape[0]
    for start, h2_ref in ((0, top_ref), (half, bottom_ref)):
        rows = slice(start, start + half)
        pieces = [h0_ref[rows, :], h1_ref[rows, :], h2_ref[...], h3_ref[rows, :]]
        weights = [w[:, columns] for w in (w0_ref, w1_ref, w2_ref, w3_ref)]
        total = jnp.dot(
            jnp.concatenate(pieces, axis=1), jnp.concatenate(weights, axis=0), preferred_element_type=F32
        )
        attn_ref[rows, :] = total.astype(BF16)
        mixed_ref[rows, :] = x_ref[rows, columns].astype(F32) + total


def attention_columns(me, heads, by_one, by_three, relayed, weights, x):
    rows, width = x.shape
    last = weights[0].shape[0] // LANES - 1
    out = pl.BlockSpec((rows, LANES), lambda i: (0, 0))
    half = pl.BlockSpec((rows // 2, LANES), lambda i: (0, 0))
    return pl.pallas_call(
        columns_kernel,
        grid=(1,),
        in_specs=[SMEM]
        + [out] * 3
        + [half] * 2
        + [pl.BlockSpec((LANES, width), lambda i: (last, 0))] * 4
        + [pl.BlockSpec((rows, width), lambda i: (0, 0))],
        out_specs=[out, out],
        out_shape=[
            jax.ShapeDtypeStruct((rows, LANES), BF16),
            jax.ShapeDtypeStruct((rows, LANES), F32),
        ],
        compiler_params=params(60),
        cost_estimate=cost(2 * rows * width * LANES, 8 * 2**20),
        name="attention_columns",
    )(me, heads, by_one, by_three, *relayed, *weights, x)


def combine_kernel(spot_ref, lane_ref, mixed_hbm, back_ref, out_ref, slots, mixed_ref, sems):
    dests, cap, width = slots.shape
    rows = out_ref.shape[0]
    copies = [
        pltpu.make_async_copy(
            back_ref.at[:, m], slots.at[:, :, pl.ds(m * LANES, LANES)], sems.at[m]
        )
        for m in range(4)
    ]
    copies.append(pltpu.make_async_copy(mixed_hbm, mixed_ref, sems.at[4]))
    for copy in copies:
        copy.start()
    for copy in copies:
        copy.wait()
    tile = 256
    names = lax.broadcasted_iota(jnp.int32, (ROWS_BLK, dests * cap), 1).astype(F32)

    @pl.loop(0, rows // tile)
    def _(i):
        pieces = [
            pl.ds(pl.multiple_of(i * tile + t * ROWS_BLK, ROWS_BLK), ROWS_BLK) for t in range(tile // ROWS_BLK)
        ]
        hot = jnp.concatenate(
            [jnp.where(names == as_column(spot_ref[:, p]), 1.0, 0.0).astype(BF16) for p in pieces], axis=0
        )
        found = jnp.dot(hot, slots[...].reshape(dests * cap, width), preferred_element_type=F32)
        for t, p in enumerate(pieces):
            lane = as_column(lane_ref[:, p])
            total = mixed_ref[p, :]
            for m in range(4):
                part = found[t * ROWS_BLK : (t + 1) * ROWS_BLK, m * LANES : (m + 1) * LANES]
                total = total + jnp.where(lane == m, part, 0.0)
            out_ref[p, :] = total.astype(BF16)


def combine(spot_row, lane_row, back, mixed):
    rows = mixed.shape[0]
    slots = back.shape[0] * back.shape[2]
    return pl.pallas_call(
        combine_kernel,
        in_specs=[VMEM] * 2 + [HBM] * 2,
        out_specs=VMEM,
        out_shape=jax.ShapeDtypeStruct((rows, LANES), BF16),
        scratch_shapes=[
            pltpu.VMEM((back.shape[0], back.shape[2], 4 * LANES), BF16),
            pltpu.VMEM((rows, LANES), F32),
            pltpu.SemaphoreType.DMA((5,)),
        ],
        compiler_params=params(24),
        cost_estimate=cost(2 * rows * slots * 4 * LANES, 4 * 2**20),
        name="combine",
    )(spot_row, lane_row, mixed, back)


def swap(array, change):
    return lax.ppermute(array, "mp", [(i, i ^ change) for i in range(4)])


def exchange(array, axes):
    return lax.all_to_all(array, axes, split_axis=0, concat_axis=0, tiled=True)


def on_device(
    node_features,
    w_qkv,
    w_out,
    head_scale,
    norm_gain,
    router,
    w_gate,
    w_up,
    w_down,
    neighbor_blocks,
    expert_ids,
):
    parts = lax.axis_size("graph")
    part = lax.axis_index("graph")
    me = lax.axis_index("mp")
    rows, width = node_features.shape
    half_cap = CAP_E // 2

    requests = make_requests(neighbor_blocks, parts)
    incoming = exchange(requests.reshape(parts, 1, CAP_H), "graph")
    q, kv = qkv(node_features, w_qkv, head_scale)
    outgoing = pick_blocks(incoming, kv)
    halo = exchange(outgoing, "graph")

    which = me // 2
    me_ref = me[None].astype(jnp.int32)
    kept, given = split_weights(me_ref, w_gate, w_up, w_down, w_out, outgoing)
    weights = [kept, swap(kept, 1), swap(given, 2), swap(given, 3)]

    routed = expert_ids[:, 0]
    experts_all = router.shape[1]
    chosen = routed[:, None] == jnp.arange(experts_all, dtype=jnp.int32)[None, :]
    row_ids = jnp.arange(rows, dtype=jnp.int32)
    earlier = (row_ids[:, None] > row_ids[None, :]).astype(BF16)
    before = jnp.dot(earlier, chosen.astype(BF16), preferred_element_type=F32)
    rank = jnp.sum(jnp.where(chosen, before, 0.0), axis=1).astype(jnp.int32)
    second = (rank >= half_cap).astype(jnp.int32)
    lane = (routed % 2) * 2 + second
    spot = (routed // 2) * half_cap + rank - second * half_cap
    spot_row, lane_row = spot[None, :], lane[None, :]
    mine_row = jnp.where(lane == me, spot, -1)[None, :]
    x_there = exchange(place_rows(mine_row, node_features, parts, half_cap), "graph")

    route = lax.dynamic_index_in_dim(router, 2 * part + which, 1, keepdims=False).astype(F32)[None, :]
    heads, send = attention(
        neighbor_blocks, requests, q, kv, halo, spot_row, lane_row, weights[1:2], parts, half_cap
    )
    send, x_there, weights[3] = lax.optimization_barrier((send, x_there, weights[3]))
    heads_there = exchange(send.reshape(parts * 4, half_cap, LANES), ("graph", "mp"))
    heads, heads_there = lax.optimization_barrier((heads, heads_there))
    by_one, by_three = swap(heads, 1), swap(heads, 3)
    produced = experts(
        me_ref,
        heads_there.reshape(parts, 4, half_cap, LANES),
        x_there,
        norm_gain[None, :],
        route,
        weights,
        (),
    )
    produced, by_one, by_three = lax.optimization_barrier((produced, by_one, by_three))
    middle = rows // 2
    relayed = [swap(by_three[:middle], 1), swap(by_one[middle:], 3)]
    attn_out, mixed = attention_columns(
        me_ref, heads, by_one, by_three, relayed, weights, node_features
    )
    back = exchange(produced.reshape(parts * 4, half_cap, LANES), ("graph", "mp"))
    layer_out = combine(spot_row, lane_row, back.reshape(parts, 4, half_cap, LANES), mixed)
    return (attn_out, layer_out)


def solution(mesh):
    placed = (
        P("graph", None),
        P(None, None, "mp"),
        P("mp", None),
        P("mp"),
        P(),
        P(),
        P("graph", None, "mp"),
        P("graph", None, "mp"),
        P("graph", "mp", None),
        P("graph", None),
        P("graph", None),
    )
    return jax.shard_map(
        on_device,
        mesh=mesh,
        in_specs=placed,
        out_specs=(P("graph", "mp"), P("graph", "mp")),
        check_vma=False,
    )
```

```python
import math

import jax
import jax.numpy as jnp
from jax import lax
from jax.experimental import pallas as pl
from jax.experimental.pallas import tpu as pltpu
from jax.sharding import PartitionSpec as P

HEAD_DIM = 64
ROWS_BLK = 128
LOCAL_REFS = 4
CAP_H = 2
CAP_E = 96
EPS = 1e-06
LANES = 128

VMEM = pl.BlockSpec(memory_space=pltpu.VMEM)
SMEM = pl.BlockSpec(memory_space=pltpu.SMEM)
ANY = pl.BlockSpec(memory_space=pl.ANY)
HBM = pl.BlockSpec(memory_space=pltpu.HBM)
F32 = jnp.float32
BF16 = jnp.bfloat16


def params(mebibytes):
    return pltpu.CompilerParams(vmem_limit_bytes=mebibytes * 2**20)


def cost(flops, moved, transcendentals=0):
    return pl.CostEstimate(flops=flops, bytes_accessed=moved, transcendentals=transcendentals)


def head_units(values):
    low = lax.broadcasted_iota(jnp.int32, values.shape, 1) < HEAD_DIM
    squares = values * values
    first = jnp.sum(jnp.where(low, squares, 0.0), axis=1, keepdims=True)
    second = jnp.sum(jnp.where(low, 0.0, squares), axis=1, keepdims=True)
    scale = lax.rsqrt(jnp.where(low, first, second) * (1.0 / HEAD_DIM) + EPS)
    return values * scale


def qkv_kernel(x_ref, w_ref, scale_ref, q_ref, kv_ref):
    x = x_ref[...]
    rows = x.shape[0]
    query = jnp.dot(x, w_ref[0], preferred_element_type=F32)
    low = lax.broadcasted_iota(jnp.int32, (1, LANES), 1) < HEAD_DIM
    scale = jnp.where(low, scale_ref[0], scale_ref[1]) * (1.0 / math.sqrt(HEAD_DIM))
    q_ref[...] = (head_units(query) * scale).astype(BF16)
    key = jnp.dot(x, w_ref[1], preferred_element_type=F32)
    value = jnp.dot(x, w_ref[2], preferred_element_type=F32)
    kv_ref[:, :, :LANES] = head_units(key).astype(BF16).reshape(rows // ROWS_BLK, ROWS_BLK, LANES)
    kv_ref[:, :, LANES:] = value.astype(BF16).reshape(rows // ROWS_BLK, ROWS_BLK, LANES)


def qkv(x, w, scale):
    rows, width = x.shape
    tile = 1024
    blocks = tile // ROWS_BLK
    return pl.pallas_call(
        qkv_kernel,
        grid=(rows // tile,),
        in_specs=[
            pl.BlockSpec((tile, width), lambda i: (i, 0)),
            pl.BlockSpec((3, width, LANES), lambda i: (0, 0, 0)),
            SMEM,
        ],
        out_specs=[
            pl.BlockSpec((tile, LANES), lambda i: (i, 0)),
            pl.BlockSpec((blocks, ROWS_BLK, 2 * LANES), lambda i: (i, 0, 0)),
        ],
        out_shape=[
            jax.ShapeDtypeStruct((rows, LANES), BF16),
            jax.ShapeDtypeStruct((rows // ROWS_BLK, ROWS_BLK, 2 * LANES), BF16),
        ],
        compiler_params=params(60),
        cost_estimate=cost(2 * rows * width * 3 * LANES, 2 * rows * (width + 3 * LANES)),
        name="qkv",
    )(x, w, scale)


def requests_kernel(near_ref, out_ref):
    parts = out_ref.shape[0]
    rows, listed = near_ref.shape
    shape = (parts, rows)
    inside = lax.broadcasted_iota(jnp.int32, shape, 1)
    names = lax.broadcasted_iota(jnp.int32, shape, 0) * rows + inside
    wanted = jnp.zeros(shape, jnp.int32)
    for i in range(rows):
        for j in range(LOCAL_REFS, listed):
            wanted = jnp.where(names == near_ref[i, j], 1, wanted)
    first = jnp.min(jnp.where(wanted == 1, inside, rows - 1), axis=1, keepdims=True)
    last = jnp.max(jnp.where(wanted == 1, inside, 0), axis=1, keepdims=True)
    lane = lax.broadcasted_iota(jnp.int32, (parts, CAP_H), 1)
    out_ref[...] = jnp.where(lane == 0, first, last)


def make_requests(neighbor_blocks, parts):
    return pl.pallas_call(
        requests_kernel,
        in_specs=[SMEM],
        out_specs=VMEM,
        out_shape=jax.ShapeDtypeStruct((parts, CAP_H), jnp.int32),
        compiler_params=params(60),
        name="make_requests",
    )(neighbor_blocks)


def split_kernel(me_ref, gate_ref, up_ref, down_ref, out_w_ref, _, kept_ref, given_ref, sems):
    which = me_ref[0] // 2
    width = gate_ref.shape[1]
    copies = []
    for target, index in ((kept_ref, which), (given_ref, 1 - which)):
        for i, source in enumerate((gate_ref, up_ref, down_ref)):
            copies.append((source.at[index], target.at[pl.ds(i * width, width)]))
        copies.append((out_w_ref, target.at[pl.ds(3 * width, LANES)]))
    copies = [pltpu.make_async_copy(a, b, sems.at[i]) for i, (a, b) in enumerate(copies)]
    for copy in copies:
        copy.start()
    for copy in copies:
        copy.wait()


def split_weights(me, gate, up, down, out_w, after):
    width = gate.shape[1]
    out = jax.ShapeDtypeStruct((3 * width + LANES, width), BF16)
    return pl.pallas_call(
        split_kernel,
        in_specs=[SMEM] + [VMEM] * 4 + [ANY],
        out_specs=[HBM, HBM],
        out_shape=[out, out],
        scratch_shapes=[pltpu.SemaphoreType.DMA((8,))],
        compiler_params=params(60),
        cost_estimate=cost(0, 4 * out.size * 2),
        name="split_weights",
    )(me, gate, up, down, out_w, after)


def pick_kernel(wanted_ref, kv_ref, out_ref, sems):
    count = out_ref.shape[0]
    copies = [
        pltpu.make_async_copy(
            kv_ref.at[wanted_ref[i // CAP_H, 0, i % CAP_H]], out_ref.at[i], sems.at[i]
        )
        for i in range(count)
    ]
    for copy in copies:
        copy.start()
    for copy in copies:
        copy.wait()


def pick_blocks(wanted, kv):
    count = wanted.size
    out = jax.ShapeDtypeStruct((count,) + kv.shape[1:], kv.dtype)
    return pl.pallas_call(
        pick_kernel,
        in_specs=[SMEM, VMEM],
        out_specs=HBM,
        out_shape=out,
        scratch_shapes=[pltpu.SemaphoreType.DMA((count,))],
        compiler_params=params(60),
        cost_estimate=cost(0, 2 * out.size * 2),
        name="pick_blocks",
    )(wanted, kv)


def as_column(row):
    count = row.shape[1]
    shape = (count, count)
    same = lax.broadcasted_iota(jnp.int32, shape, 0) == lax.broadcasted_iota(jnp.int32, shape, 1)
    return jnp.sum(jnp.where(same, row.astype(F32), 0.0), axis=1, keepdims=True)


def attention_kernel(
    near_ref, asked_ref, q_ref, kv_ref, halo_ref, spot_ref, lane_ref, *rest
):
    heads_ref, send_ref, keys, values, spread = rest[-5:]
    blocks = kv_ref.shape[0]
    together = keys.shape[0]
    listed = near_ref.shape[1]
    low = lax.broadcasted_iota(jnp.int32, (ROWS_BLK, LANES), 1) < HEAD_DIM

    @pl.loop(0, blocks // together)
    def _(i):
        at = [i * together + t for t in range(together)]
        at_rows = [pl.ds(pl.multiple_of(b * ROWS_BLK, ROWS_BLK), ROWS_BLK) for b in at]
        scores = []
        for t, (b, rows) in enumerate(zip(at, at_rows)):
            q = q_ref[rows, :].astype(F32)
            both = jnp.concatenate([jnp.where(low, q, 0.0), jnp.where(low, 0.0, q)], axis=0).astype(BF16)
            for j in range(listed):
                name = near_ref[b, j]
                owner = name // blocks
                inside = name - owner * blocks
                if j < LOCAL_REFS:
                    block = kv_ref[inside]
                else:
                    second = (inside != asked_ref[owner, 0]).astype(jnp.int32)
                    block = halo_ref[owner * CAP_H + second]
                keys[t, j * ROWS_BLK : (j + 1) * ROWS_BLK, :] = block[:, :LANES]
                values[t, j * ROWS_BLK : (j + 1) * ROWS_BLK, :] = block[:, LANES:]
            scores.append(
                lax.dot_general(both, keys[t], (((1,), (1,)), ((), ())), preferred_element_type=F32)
            )
        for t, rows in enumerate(at_rows):
            largest = jnp.max(scores[t], axis=1, keepdims=True)
            expo = jnp.exp(scores[t] - largest)
            total = jnp.sum(expo, axis=1, keepdims=True)
            out = jnp.dot(expo.astype(BF16), values[t], preferred_element_type=F32) / total
            heads = jnp.where(low, out[:ROWS_BLK], out[ROWS_BLK:])
            heads_ref[rows, :] = heads.astype(BF16)
            lane = as_column(lane_ref[:, rows])
            for m in range(4):
                spread[rows, m * LANES : (m + 1) * LANES] = jnp.where(lane == m, heads, 0.0).astype(BF16)

    dests, cap = send_ref.shape[0], send_ref.shape[2]
    step = 4

    @pl.loop(0, dests // step)
    def _(i):
        tile = step * cap
        spot = spot_ref[...]
        here = lax.broadcasted_iota(jnp.int32, (tile, spot.shape[1]), 0) + i * tile
        hot = jnp.where(here == spot, 1.0, 0.0).astype(BF16)
        placed = jnp.dot(hot, spread[...], preferred_element_type=F32).astype(BF16)
        for d in range(step):
            for m in range(4):
                send_ref[i * step + d, m] = placed[d * cap : (d + 1) * cap, m * LANES : (m + 1) * LANES]


def attention(near, asked, q, kv, halo, spot_row, lane_row, after, parts, cap, together=4):
    rows = q.shape[0]
    keys = near.shape[1] * ROWS_BLK
    return pl.pallas_call(
        attention_kernel,
        in_specs=[SMEM, SMEM, VMEM, VMEM, VMEM, VMEM, VMEM] + [ANY] * len(after),
        out_specs=[VMEM, VMEM],
        out_shape=[
            jax.ShapeDtypeStruct((rows, LANES), BF16),
            jax.ShapeDtypeStruct((parts, 4, cap, LANES), BF16),
        ],
        scratch_shapes=[
            pltpu.VMEM((together, keys, LANES), BF16),
            pltpu.VMEM((together, keys, LANES), BF16),
            pltpu.VMEM((rows, 4 * LANES), BF16),
        ],
        compiler_params=params(60),
        cost_estimate=cost(12 * 10**9, 8 * 2**20, 2 * rows * keys),
        name="attention",
    )(near, asked, q, kv, halo, spot_row, lane_row, *after)


def place_kernel(spot_ref, x_ref, out_ref):
    dests, cap = out_ref.shape[0], out_ref.shape[1]
    step = 4

    @pl.loop(0, dests // step)
    def _(i):
        tile = step * cap
        spot = spot_ref[...]
        here = lax.broadcasted_iota(jnp.int32, (tile, spot.shape[1]), 0) + i * tile
        hot = jnp.where(here == spot, 1.0, 0.0).astype(BF16)
        placed = jnp.dot(hot, x_ref[...], preferred_element_type=F32).astype(BF16)
        for d in range(step):
            out_ref[i * step + d] = placed[d * cap : (d + 1) * cap, :]


def place_rows(spot_row, x, parts, cap):
    rows, width = x.shape
    return pl.pallas_call(
        place_kernel,
        in_specs=[VMEM, VMEM],
        out_specs=VMEM,
        out_shape=jax.ShapeDtypeStruct((parts, cap, width), BF16),
        compiler_params=params(60),
        cost_estimate=cost(2 * parts * cap * rows * width, 4 * 2**20),
        name="place_rows",
    )(spot_row, x)


def route_kernel(route_ref, *rest):
    rest[-1][...] = route_ref[...]


def hold_route(route, after):
    return pl.pallas_call(
        route_kernel,
        in_specs=[VMEM] + [ANY] * len(after),
        out_specs=VMEM,
        out_shape=jax.ShapeDtypeStruct(route.shape, route.dtype),
        compiler_params=params(60),
        cost_estimate=cost(2 * 10**10, 10**7),
        name="hold_route",
    )(route, *after)


def experts_kernel(me_ref, gain_ref, route_ref, h_ref, x_ref, w0_ref, w1_ref, w2_ref, w3_ref, *rest):
    out_ref, heads, features, project, quarters, results, sems = rest[-7:]
    me = me_ref[0]
    tiles, step, cap, width = features.shape
    tile = step * cap
    sources = (w0_ref, w1_ref, w2_ref, w3_ref)
    sizes = ((h_ref, heads), (x_ref, features))
    small = [
        pltpu.make_async_copy(
            w.at[pl.ds(3 * width, LANES)], project.at[pl.ds(k * LANES, LANES)], sems.at[k]
        )
        for k, w in enumerate(sources)
    ]
    large = [
        pltpu.make_async_copy(w.at[pl.ds(0, 3 * width)], quarters.at[k], sems.at[4 + k])
        for k, w in enumerate(sources)
    ]
    rows = [
        [
            pltpu.make_async_copy(source.at[pl.ds(t * step, step)], target.at[t], sems.at[8 + 2 * t + i])
            for i, (source, target) in enumerate(sizes)
        ]
        for t in range(tiles)
    ]
    outs = [
        pltpu.make_async_copy(
            results.at[t], out_ref.at[pl.ds(t * step, step)], sems.at[8 + 2 * tiles + t]
        )
        for t in range(tiles)
    ]
    for copy in rows[0] + small + large + [c for later in rows[1:] for c in later]:
        copy.start()
    for copy in small:
        copy.wait()
    for t in range(tiles):
        for copy in rows[t]:
            copy.wait()
        arrived = jnp.concatenate([heads[t, :, me ^ k].reshape(tile, LANES) for k in range(4)], axis=1)
        mixed = features[t].reshape(tile, width).astype(F32) + jnp.dot(
            arrived, project[...], preferred_element_type=F32
        )
        mean = jnp.mean(mixed * mixed, axis=1, keepdims=True)
        normed = (mixed * lax.rsqrt(mean + EPS) * gain_ref[...]).astype(BF16)
        logit = jnp.sum(normed.astype(F32) * route_ref[...], axis=1, keepdims=True)
        gate = 1.0 / (1.0 + jnp.exp(-logit))
        result = None
        for k in range(4):
            if t == 0:
                large[k].wait()
            left = jnp.dot(normed, quarters[k, :width, :], preferred_element_type=F32)
            right = jnp.dot(normed, quarters[k, width : 2 * width, :], preferred_element_type=F32)
            half = 0.5 * left
            hidden = ((half + half * jnp.tanh(half)) * right).astype(BF16)
            term = jnp.dot(hidden, quarters[k, 2 * width :, :], preferred_element_type=F32)
            result = term if result is None else result + term
        result = (gate * result).astype(BF16).reshape(step, cap, width)
        for m in range(4):
            results[t, :, m] = result[:, :, m * LANES : (m + 1) * LANES]
        outs[t].start()
    for copy in outs:
        copy.wait()


def experts(me, heads, x, gain, route, weights, after, tiles=2):
    parts, cap, width = x.shape
    step = parts // tiles
    return pl.pallas_call(
        experts_kernel,
        in_specs=[SMEM, VMEM, VMEM, HBM, HBM] + [ANY] * (4 + len(after)),
        out_specs=HBM,
        out_shape=jax.ShapeDtypeStruct((parts, 4, cap, LANES), BF16),
        scratch_shapes=[
            pltpu.VMEM((tiles, step, 4, cap, LANES), BF16),
            pltpu.VMEM((tiles, step, cap, width), BF16),
            pltpu.VMEM((width, width), BF16),
            pltpu.VMEM((4, 3 * width, width), BF16),
            pltpu.VMEM((tiles, step, 4, cap, LANES), BF16),
            pltpu.SemaphoreType.DMA((8 + 3 * tiles,)),
        ],
        compiler_params=params(58),
        cost_estimate=cost(2 * parts * cap * width * (12 * width + width), 12 * 2**20),
        name="experts",
    )(me, gain, route, heads, x, *weights, *after)


def columns_kernel(
    me_ref, h0_ref, h1_ref, h3_ref, top_ref, bottom_ref, w0_ref, w1_ref, w2_ref, w3_ref, x_ref, attn_ref, mixed_ref
):
    columns = pl.ds(pl.multiple_of(me_ref[0] * LANES, LANES), LANES)
    half = top_ref.shape[0]
    for start, h2_ref in ((0, top_ref), (half, bottom_ref)):
        rows = slice(start, start + half)
        pieces = [h0_ref[rows, :], h1_ref[rows, :], h2_ref[...], h3_ref[rows, :]]
        weights = [w[:, columns] for w in (w0_ref, w1_ref, w2_ref, w3_ref)]
        total = jnp.dot(
            jnp.concatenate(pieces, axis=1), jnp.concatenate(weights, axis=0), preferred_element_type=F32
        )
        attn_ref[rows, :] = total.astype(BF16)
        mixed_ref[rows, :] = x_ref[rows, columns].astype(F32) + total


def attention_columns(me, heads, by_one, by_three, relayed, weights, x):
    rows, width = x.shape
    last = weights[0].shape[0] // LANES - 1
    out = pl.BlockSpec((rows, LANES), lambda i: (0, 0))
    half = pl.BlockSpec((rows // 2, LANES), lambda i: (0, 0))
    return pl.pallas_call(
        columns_kernel,
        grid=(1,),
        in_specs=[SMEM]
        + [out] * 3
        + [half] * 2
        + [pl.BlockSpec((LANES, width), lambda i: (last, 0))] * 4
        + [pl.BlockSpec((rows, width), lambda i: (0, 0))],
        out_specs=[out, out],
        out_shape=[
            jax.ShapeDtypeStruct((rows, LANES), BF16),
            jax.ShapeDtypeStruct((rows, LANES), F32),
        ],
        compiler_params=params(60),
        cost_estimate=cost(2 * rows * width * LANES, 8 * 2**20),
        name="attention_columns",
    )(me, heads, by_one, by_three, *relayed, *weights, x)


def combine_kernel(spot_ref, lane_ref, mixed_hbm, back_ref, out_ref, slots, mixed_ref, sems):
    dests, cap, width = slots.shape
    rows = out_ref.shape[0]
    copies = [
        pltpu.make_async_copy(
            back_ref.at[:, m], slots.at[:, :, pl.ds(m * LANES, LANES)], sems.at[m]
        )
        for m in range(4)
    ]
    copies.append(pltpu.make_async_copy(mixed_hbm, mixed_ref, sems.at[4]))
    for copy in copies:
        copy.start()
    for copy in copies:
        copy.wait()
    tile = 256
    names = lax.broadcasted_iota(jnp.int32, (ROWS_BLK, dests * cap), 1).astype(F32)

    @pl.loop(0, rows // tile)
    def _(i):
        pieces = [
            pl.ds(pl.multiple_of(i * tile + t * ROWS_BLK, ROWS_BLK), ROWS_BLK) for t in range(tile // ROWS_BLK)
        ]
        hot = jnp.concatenate(
            [jnp.where(names == as_column(spot_ref[:, p]), 1.0, 0.0).astype(BF16) for p in pieces], axis=0
        )
        found = jnp.dot(hot, slots[...].reshape(dests * cap, width), preferred_element_type=F32)
        for t, p in enumerate(pieces):
            lane = as_column(lane_ref[:, p])
            total = mixed_ref[p, :]
            for m in range(4):
                part = found[t * ROWS_BLK : (t + 1) * ROWS_BLK, m * LANES : (m + 1) * LANES]
                total = total + jnp.where(lane == m, part, 0.0)
            out_ref[p, :] = total.astype(BF16)


def combine(spot_row, lane_row, back, mixed):
    rows = mixed.shape[0]
    slots = back.shape[0] * back.shape[2]
    return pl.pallas_call(
        combine_kernel,
        in_specs=[VMEM] * 2 + [HBM] * 2,
        out_specs=VMEM,
        out_shape=jax.ShapeDtypeStruct((rows, LANES), BF16),
        scratch_shapes=[
            pltpu.VMEM((back.shape[0], back.shape[2], 4 * LANES), BF16),
            pltpu.VMEM((rows, LANES), F32),
            pltpu.SemaphoreType.DMA((5,)),
        ],
        compiler_params=params(24),
        cost_estimate=cost(2 * rows * slots * 4 * LANES, 4 * 2**20),
        name="combine",
    )(spot_row, lane_row, mixed, back)


def swap(array, change):
    return lax.ppermute(array, "mp", [(i, i ^ change) for i in range(4)])


def exchange(array, axes):
    return lax.all_to_all(array, axes, split_axis=0, concat_axis=0, tiled=True)


def on_device(
    node_features,
    w_qkv,
    w_out,
    head_scale,
    norm_gain,
    router,
    w_gate,
    w_up,
    w_down,
    neighbor_blocks,
    expert_ids,
):
    parts = lax.axis_size("graph")
    part = lax.axis_index("graph")
    me = lax.axis_index("mp")
    rows, width = node_features.shape
    half_cap = CAP_E // 2

    requests = make_requests(neighbor_blocks, parts)
    incoming = exchange(requests.reshape(parts, 1, CAP_H), "graph")
    q, kv = qkv(node_features, w_qkv, head_scale)
    outgoing = pick_blocks(incoming, kv)
    halo = exchange(outgoing, "graph")

    which = me // 2
    me_ref = me[None].astype(jnp.int32)
    kept, given = split_weights(me_ref, w_gate, w_up, w_down, w_out, outgoing)
    weights = [kept, swap(kept, 1), swap(given, 2), swap(given, 3)]

    routed = expert_ids[:, 0]
    experts_all = router.shape[1]
    chosen = routed[:, None] == jnp.arange(experts_all, dtype=jnp.int32)[None, :]
    row_ids = jnp.arange(rows, dtype=jnp.int32)
    earlier = (row_ids[:, None] > row_ids[None, :]).astype(BF16)
    before = jnp.dot(earlier, chosen.astype(BF16), preferred_element_type=F32)
    rank = jnp.sum(jnp.where(chosen, before, 0.0), axis=1).astype(jnp.int32)
    second = (rank >= half_cap).astype(jnp.int32)
    lane = (routed % 2) * 2 + second
    spot = (routed // 2) * half_cap + rank - second * half_cap
    spot_row, lane_row = spot[None, :], lane[None, :]
    mine_row = jnp.where(lane == me, spot, -1)[None, :]
    x_there = exchange(place_rows(mine_row, node_features, parts, half_cap), "graph")

    route = lax.dynamic_index_in_dim(router, 2 * part + which, 1, keepdims=False).astype(F32)[None, :]
    heads, send = attention(
        neighbor_blocks, requests, q, kv, halo, spot_row, lane_row, weights[1:2], parts, half_cap
    )
    send, x_there = lax.optimization_barrier((send, x_there))
    heads_there = exchange(send.reshape(parts * 4, half_cap, LANES), ("graph", "mp"))
    route = hold_route(route, [send] + weights[2:])
    heads, heads_there, route = lax.optimization_barrier((heads, heads_there, route))
    by_one, by_three = swap(heads, 1), swap(heads, 3)
    produced = experts(
        me_ref,
        heads_there.reshape(parts, 4, half_cap, LANES),
        x_there,
        norm_gain[None, :],
        route,
        weights,
        (),
    )
    produced, by_one, by_three = lax.optimization_barrier((produced, by_one, by_three))
    middle = rows // 2
    relayed = [swap(by_three[:middle], 1), swap(by_one[middle:], 3)]
    attn_out, mixed = attention_columns(
        me_ref, heads, by_one, by_three, relayed, weights, node_features
    )
    back = exchange(produced.reshape(parts * 4, half_cap, LANES), ("graph", "mp"))
    layer_out = combine(spot_row, lane_row, back.reshape(parts, 4, half_cap, LANES), mixed)
    return (attn_out, layer_out)


def solution(mesh):
    placed = (
        P("graph", None),
        P(None, None, "mp"),
        P("mp", None),
        P("mp"),
        P(),
        P(),
        P("graph", None, "mp"),
        P("graph", None, "mp"),
        P("graph", "mp", None),
        P("graph", None),
        P("graph", None),
    )
    return jax.shard_map(
        on_device,
        mesh=mesh,
        in_specs=placed,
        out_specs=(P("graph", "mp"), P("graph", "mp")),
        check_vma=False,
    )
```

```python
import math

import jax
import jax.numpy as jnp
from jax import lax
from jax.experimental import pallas as pl
from jax.experimental.pallas import tpu as pltpu
from jax.sharding import PartitionSpec as P

HEAD_DIM = 64
ROWS_BLK = 128
LOCAL_REFS = 4
CAP_H = 2
CAP_E = 96
EPS = 1e-06
LANES = 128

VMEM = pl.BlockSpec(memory_space=pltpu.VMEM)
SMEM = pl.BlockSpec(memory_space=pltpu.SMEM)
ANY = pl.BlockSpec(memory_space=pl.ANY)
HBM = pl.BlockSpec(memory_space=pltpu.HBM)
F32 = jnp.float32
BF16 = jnp.bfloat16


def params(mebibytes):
    return pltpu.CompilerParams(vmem_limit_bytes=mebibytes * 2**20)


def cost(flops, moved, transcendentals=0):
    return pl.CostEstimate(flops=flops, bytes_accessed=moved, transcendentals=transcendentals)


def head_units(values):
    low = lax.broadcasted_iota(jnp.int32, values.shape, 1) < HEAD_DIM
    squares = values * values
    first = jnp.sum(jnp.where(low, squares, 0.0), axis=1, keepdims=True)
    second = jnp.sum(jnp.where(low, 0.0, squares), axis=1, keepdims=True)
    scale = lax.rsqrt(jnp.where(low, first, second) * (1.0 / HEAD_DIM) + EPS)
    return values * scale


def qkv_kernel(x_ref, w_ref, scale_ref, q_ref, kv_ref):
    x = x_ref[...]
    rows = x.shape[0]
    query = jnp.dot(x, w_ref[0], preferred_element_type=F32)
    low = lax.broadcasted_iota(jnp.int32, (1, LANES), 1) < HEAD_DIM
    scale = jnp.where(low, scale_ref[0], scale_ref[1]) * (1.0 / math.sqrt(HEAD_DIM))
    q_ref[...] = (head_units(query) * scale).astype(BF16)
    key = jnp.dot(x, w_ref[1], preferred_element_type=F32)
    value = jnp.dot(x, w_ref[2], preferred_element_type=F32)
    kv_ref[:, :, :LANES] = head_units(key).astype(BF16).reshape(rows // ROWS_BLK, ROWS_BLK, LANES)
    kv_ref[:, :, LANES:] = value.astype(BF16).reshape(rows // ROWS_BLK, ROWS_BLK, LANES)


def qkv(x, w, scale):
    rows, width = x.shape
    tile = 1024
    blocks = tile // ROWS_BLK
    return pl.pallas_call(
        qkv_kernel,
        grid=(rows // tile,),
        in_specs=[
            pl.BlockSpec((tile, width), lambda i: (i, 0)),
            pl.BlockSpec((3, width, LANES), lambda i: (0, 0, 0)),
            SMEM,
        ],
        out_specs=[
            pl.BlockSpec((tile, LANES), lambda i: (i, 0)),
            pl.BlockSpec((blocks, ROWS_BLK, 2 * LANES), lambda i: (i, 0, 0)),
        ],
        out_shape=[
            jax.ShapeDtypeStruct((rows, LANES), BF16),
            jax.ShapeDtypeStruct((rows // ROWS_BLK, ROWS_BLK, 2 * LANES), BF16),
        ],
        compiler_params=params(60),
        cost_estimate=cost(2 * rows * width * 3 * LANES, 2 * rows * (width + 3 * LANES)),
        name="qkv",
    )(x, w, scale)


def requests_kernel(near_ref, out_ref):
    parts = out_ref.shape[0]
    rows, listed = near_ref.shape
    shape = (parts, rows)
    inside = lax.broadcasted_iota(jnp.int32, shape, 1)
    names = lax.broadcasted_iota(jnp.int32, shape, 0) * rows + inside
    wanted = jnp.zeros(shape, jnp.int32)
    for i in range(rows):
        for j in range(LOCAL_REFS, listed):
            wanted = jnp.where(names == near_ref[i, j], 1, wanted)
    first = jnp.min(jnp.where(wanted == 1, inside, rows - 1), axis=1, keepdims=True)
    last = jnp.max(jnp.where(wanted == 1, inside, 0), axis=1, keepdims=True)
    lane = lax.broadcasted_iota(jnp.int32, (parts, CAP_H), 1)
    out_ref[...] = jnp.where(lane == 0, first, last)


def make_requests(neighbor_blocks, parts):
    return pl.pallas_call(
        requests_kernel,
        in_specs=[SMEM],
        out_specs=VMEM,
        out_shape=jax.ShapeDtypeStruct((parts, CAP_H), jnp.int32),
        compiler_params=params(60),
        name="make_requests",
    )(neighbor_blocks)


def split_kernel(me_ref, gate_ref, up_ref, down_ref, out_w_ref, _, kept_ref, given_ref, sems):
    which = me_ref[0] // 2
    width = gate_ref.shape[1]
    copies = []
    for target, index in ((kept_ref, which), (given_ref, 1 - which)):
        for i, source in enumerate((gate_ref, up_ref, down_ref)):
            copies.append((source.at[index], target.at[pl.ds(i * width, width)]))
        copies.append((out_w_ref, target.at[pl.ds(3 * width, LANES)]))
    copies = [pltpu.make_async_copy(a, b, sems.at[i]) for i, (a, b) in enumerate(copies)]
    for copy in copies:
        copy.start()
    for copy in copies:
        copy.wait()


def split_weights(me, gate, up, down, out_w, after):
    width = gate.shape[1]
    out = jax.ShapeDtypeStruct((3 * width + LANES, width), BF16)
    return pl.pallas_call(
        split_kernel,
        in_specs=[SMEM] + [VMEM] * 4 + [ANY],
        out_specs=[HBM, HBM],
        out_shape=[out, out],
        scratch_shapes=[pltpu.SemaphoreType.DMA((8,))],
        compiler_params=params(60),
        cost_estimate=cost(0, 4 * out.size * 2),
        name="split_weights",
    )(me, gate, up, down, out_w, after)


def pick_kernel(wanted_ref, kv_ref, out_ref, sems):
    count = out_ref.shape[0]
    copies = [
        pltpu.make_async_copy(
            kv_ref.at[wanted_ref[i // CAP_H, 0, i % CAP_H]], out_ref.at[i], sems.at[i]
        )
        for i in range(count)
    ]
    for copy in copies:
        copy.start()
    for copy in copies:
        copy.wait()


def pick_blocks(wanted, kv):
    count = wanted.size
    out = jax.ShapeDtypeStruct((count,) + kv.shape[1:], kv.dtype)
    return pl.pallas_call(
        pick_kernel,
        in_specs=[SMEM, VMEM],
        out_specs=HBM,
        out_shape=out,
        scratch_shapes=[pltpu.SemaphoreType.DMA((count,))],
        compiler_params=params(60),
        cost_estimate=cost(0, 2 * out.size * 2),
        name="pick_blocks",
    )(wanted, kv)


def as_column(row):
    count = row.shape[1]
    shape = (count, count)
    same = lax.broadcasted_iota(jnp.int32, shape, 0) == lax.broadcasted_iota(jnp.int32, shape, 1)
    return jnp.sum(jnp.where(same, row.astype(F32), 0.0), axis=1, keepdims=True)


def attention_kernel(
    near_ref, asked_ref, q_ref, kv_ref, halo_ref, spot_ref, lane_ref, *rest
):
    heads_ref, send_ref, keys, values, spread = rest[-5:]
    blocks = kv_ref.shape[0]
    together = keys.shape[0]
    listed = near_ref.shape[1]
    low = lax.broadcasted_iota(jnp.int32, (ROWS_BLK, LANES), 1) < HEAD_DIM

    @pl.loop(0, blocks // together)
    def _(i):
        at = [i * together + t for t in range(together)]
        at_rows = [pl.ds(pl.multiple_of(b * ROWS_BLK, ROWS_BLK), ROWS_BLK) for b in at]
        scores = []
        for t, (b, rows) in enumerate(zip(at, at_rows)):
            q = q_ref[rows, :].astype(F32)
            both = jnp.concatenate([jnp.where(low, q, 0.0), jnp.where(low, 0.0, q)], axis=0).astype(BF16)
            for j in range(listed):
                name = near_ref[b, j]
                owner = name // blocks
                inside = name - owner * blocks
                if j < LOCAL_REFS:
                    block = kv_ref[inside]
                else:
                    second = (inside != asked_ref[owner, 0]).astype(jnp.int32)
                    block = halo_ref[owner * CAP_H + second]
                keys[t, j * ROWS_BLK : (j + 1) * ROWS_BLK, :] = block[:, :LANES]
                values[t, j * ROWS_BLK : (j + 1) * ROWS_BLK, :] = block[:, LANES:]
            scores.append(
                lax.dot_general(both, keys[t], (((1,), (1,)), ((), ())), preferred_element_type=F32)
            )
        for t, rows in enumerate(at_rows):
            largest = jnp.max(scores[t], axis=1, keepdims=True)
            expo = jnp.exp(scores[t] - largest)
            total = jnp.sum(expo, axis=1, keepdims=True)
            out = jnp.dot(expo.astype(BF16), values[t], preferred_element_type=F32) / total
            heads = jnp.where(low, out[:ROWS_BLK], out[ROWS_BLK:])
            heads_ref[rows, :] = heads.astype(BF16)
            lane = as_column(lane_ref[:, rows])
            for m in range(4):
                spread[rows, m * LANES : (m + 1) * LANES] = jnp.where(lane == m, heads, 0.0).astype(BF16)

    dests, cap = send_ref.shape[0], send_ref.shape[2]
    step = 4

    @pl.loop(0, dests // step)
    def _(i):
        tile = step * cap
        spot = spot_ref[...]
        here = lax.broadcasted_iota(jnp.int32, (tile, spot.shape[1]), 0) + i * tile
        hot = jnp.where(here == spot, 1.0, 0.0).astype(BF16)
        placed = jnp.dot(hot, spread[...], preferred_element_type=F32).astype(BF16)
        for d in range(step):
            for m in range(4):
                send_ref[i * step + d, m] = placed[d * cap : (d + 1) * cap, m * LANES : (m + 1) * LANES]


def attention(near, asked, q, kv, halo, spot_row, lane_row, after, parts, cap, together=4):
    rows = q.shape[0]
    keys = near.shape[1] * ROWS_BLK
    return pl.pallas_call(
        attention_kernel,
        in_specs=[SMEM, SMEM, VMEM, VMEM, VMEM, VMEM, VMEM] + [ANY] * len(after),
        out_specs=[VMEM, VMEM],
        out_shape=[
            jax.ShapeDtypeStruct((rows, LANES), BF16),
            jax.ShapeDtypeStruct((parts, 4, cap, LANES), BF16),
        ],
        scratch_shapes=[
            pltpu.VMEM((together, keys, LANES), BF16),
            pltpu.VMEM((together, keys, LANES), BF16),
            pltpu.VMEM((rows, 4 * LANES), BF16),
        ],
        compiler_params=params(60),
        cost_estimate=cost(12 * 10**9, 8 * 2**20, 2 * rows * keys),
        name="attention",
    )(near, asked, q, kv, halo, spot_row, lane_row, *after)


def place_kernel(spot_ref, x_ref, out_ref):
    dests, cap = out_ref.shape[0], out_ref.shape[1]
    step = 4

    @pl.loop(0, dests // step)
    def _(i):
        tile = step * cap
        spot = spot_ref[...]
        here = lax.broadcasted_iota(jnp.int32, (tile, spot.shape[1]), 0) + i * tile
        hot = jnp.where(here == spot, 1.0, 0.0).astype(BF16)
        placed = jnp.dot(hot, x_ref[...], preferred_element_type=F32).astype(BF16)
        for d in range(step):
            out_ref[i * step + d] = placed[d * cap : (d + 1) * cap, :]


def place_rows(spot_row, x, parts, cap):
    rows, width = x.shape
    return pl.pallas_call(
        place_kernel,
        in_specs=[VMEM, VMEM],
        out_specs=VMEM,
        out_shape=jax.ShapeDtypeStruct((parts, cap, width), BF16),
        compiler_params=params(60),
        cost_estimate=cost(2 * parts * cap * rows * width, 4 * 2**20),
        name="place_rows",
    )(spot_row, x)


def route_kernel(route_ref, *rest):
    rest[-1][...] = route_ref[...]


def hold_route(route, after):
    return pl.pallas_call(
        route_kernel,
        in_specs=[VMEM] + [ANY] * len(after),
        out_specs=VMEM,
        out_shape=jax.ShapeDtypeStruct(route.shape, route.dtype),
        compiler_params=params(60),
        cost_estimate=cost(2 * 10**10, 10**7),
        name="hold_route",
    )(route, *after)


def experts_kernel(me_ref, gain_ref, route_ref, h_ref, x_ref, w0_ref, w1_ref, w2_ref, w3_ref, *rest):
    out_ref, heads, features, project, quarters, results, sems = rest[-7:]
    me = me_ref[0]
    tiles, step, cap, width = features.shape
    tile = step * cap
    sources = (w0_ref, w1_ref, w2_ref, w3_ref)
    sizes = ((h_ref, heads), (x_ref, features))
    small = [
        pltpu.make_async_copy(
            w.at[pl.ds(3 * width, LANES)], project.at[pl.ds(k * LANES, LANES)], sems.at[k]
        )
        for k, w in enumerate(sources)
    ]
    large = [
        pltpu.make_async_copy(w.at[pl.ds(0, 3 * width)], quarters.at[k], sems.at[4 + k])
        for k, w in enumerate(sources)
    ]
    rows = [
        [
            pltpu.make_async_copy(source.at[pl.ds(t * step, step)], target.at[t], sems.at[8 + 2 * t + i])
            for i, (source, target) in enumerate(sizes)
        ]
        for t in range(tiles)
    ]
    outs = [
        pltpu.make_async_copy(
            results.at[t], out_ref.at[pl.ds(t * step, step)], sems.at[8 + 2 * tiles + t]
        )
        for t in range(tiles)
    ]
    for copy in rows[0] + small + large + [c for later in rows[1:] for c in later]:
        copy.start()
    for copy in small:
        copy.wait()
    for t in range(tiles):
        for copy in rows[t]:
            copy.wait()
        arrived = jnp.concatenate([heads[t, :, me ^ k].reshape(tile, LANES) for k in range(4)], axis=1)
        mixed = features[t].reshape(tile, width).astype(F32) + jnp.dot(
            arrived, project[...], preferred_element_type=F32
        )
        mean = jnp.mean(mixed * mixed, axis=1, keepdims=True)
        normed = (mixed * lax.rsqrt(mean + EPS) * gain_ref[...]).astype(BF16)
        logit = jnp.sum(normed.astype(F32) * route_ref[...], axis=1, keepdims=True)
        gate = 1.0 / (1.0 + jnp.exp(-logit))
        result = None
        for k in range(4):
            if t == 0:
                large[k].wait()
            hidden = []
            for c in range(0, width, 256):
                left = jnp.dot(normed, quarters[k, :width, c : c + 256], preferred_element_type=F32)
                right = jnp.dot(
                    normed, quarters[k, width : 2 * width, c : c + 256], preferred_element_type=F32
                )
                half = 0.5 * left
                hidden.append(((half + half * jnp.tanh(half)) * right).astype(BF16))
            hidden = jnp.concatenate(hidden, axis=1)
            term = jnp.dot(hidden, quarters[k, 2 * width :, :], preferred_element_type=F32)
            result = term if result is None else result + term
        result = (gate * result).astype(BF16).reshape(step, cap, width)
        for m in range(4):
            results[t, :, m] = result[:, :, m * LANES : (m + 1) * LANES]
        outs[t].start()
    for copy in outs:
        copy.wait()


def experts(me, heads, x, gain, route, weights, after, tiles=2):
    parts, cap, width = x.shape
    step = parts // tiles
    return pl.pallas_call(
        experts_kernel,
        in_specs=[SMEM, VMEM, VMEM, HBM, HBM] + [ANY] * (4 + len(after)),
        out_specs=HBM,
        out_shape=jax.ShapeDtypeStruct((parts, 4, cap, LANES), BF16),
        scratch_shapes=[
            pltpu.VMEM((tiles, step, 4, cap, LANES), BF16),
            pltpu.VMEM((tiles, step, cap, width), BF16),
            pltpu.VMEM((width, width), BF16),
            pltpu.VMEM((4, 3 * width, width), BF16),
            pltpu.VMEM((tiles, step, 4, cap, LANES), BF16),
            pltpu.SemaphoreType.DMA((8 + 3 * tiles,)),
        ],
        compiler_params=params(58),
        cost_estimate=cost(2 * parts * cap * width * (12 * width + width), 12 * 2**20),
        name="experts",
    )(me, gain, route, heads, x, *weights, *after)


def columns_kernel(
    me_ref, h0_ref, h1_ref, h3_ref, w0_ref, w1_ref, w2_ref, w3_ref, x_ref, part_ref, kept_ref, last_ref, sem
):
    columns = pl.ds(pl.multiple_of(me_ref[0] * LANES, LANES), LANES)
    copy = pltpu.make_async_copy(x_ref.at[:, columns], kept_ref, sem)
    copy.start()
    pieces = [h[...] for h in (h0_ref, h1_ref, h3_ref)]
    weights = [w[:, columns] for w in (w0_ref, w1_ref, w3_ref)]
    part_ref[...] = jnp.dot(
        jnp.concatenate(pieces, axis=1), jnp.concatenate(weights, axis=0), preferred_element_type=F32
    )
    last_ref[...] = w2_ref[:, columns]
    copy.wait()


def attention_columns(me, heads, by_one, by_three, weights, x):
    rows, width = x.shape
    last = weights[0].shape[0] // LANES - 1
    out = pl.BlockSpec((rows, LANES), lambda i: (0, 0))
    return pl.pallas_call(
        columns_kernel,
        grid=(1,),
        in_specs=[SMEM]
        + [out] * 3
        + [pl.BlockSpec((LANES, width), lambda i: (last, 0))] * 4
        + [ANY],
        out_specs=[out, out, pl.BlockSpec((LANES, LANES), lambda i: (0, 0))],
        out_shape=[
            jax.ShapeDtypeStruct((rows, LANES), F32),
            jax.ShapeDtypeStruct((rows, LANES), BF16),
            jax.ShapeDtypeStruct((LANES, LANES), BF16),
        ],
        scratch_shapes=[pltpu.SemaphoreType.DMA],
        compiler_params=params(60),
        cost_estimate=cost(2 * rows * width * LANES, 8 * 2**20),
        name="attention_columns",
    )(me, heads, by_one, by_three, *weights, x)


def combine_kernel(
    spot_ref, lane_ref, last_ref, part_hbm, kept_hbm, top_hbm, bottom_hbm, back_ref, attn_ref, out_ref,
    slots, part_ref, kept_ref, h2_ref, sems
):
    dests, cap, width = slots.shape
    rows = out_ref.shape[0]
    copies = [
        pltpu.make_async_copy(
            back_ref.at[:, m], slots.at[:, :, pl.ds(m * LANES, LANES)], sems.at[m]
        )
        for m in range(4)
    ]
    half = rows // 2
    for source, target in (
        (part_hbm, part_ref),
        (kept_hbm, kept_ref),
        (top_hbm, h2_ref.at[pl.ds(0, half)]),
        (bottom_hbm, h2_ref.at[pl.ds(half, half)]),
    ):
        copies.append(pltpu.make_async_copy(source, target, sems.at[len(copies)]))
    for copy in copies:
        copy.start()
    tile = 256
    names = lax.broadcasted_iota(jnp.int32, (ROWS_BLK, dests * cap), 1).astype(F32)

    for i in range(rows // tile):
        pieces = [pl.ds(i * tile + t * ROWS_BLK, ROWS_BLK) for t in range(tile // ROWS_BLK)]
        hot = jnp.concatenate(
            [jnp.where(names == as_column(spot_ref[:, p]), 1.0, 0.0).astype(BF16) for p in pieces], axis=0
        )
        if i == 0:
            for copy in copies:
                copy.wait()
        found = jnp.dot(hot, slots[...].reshape(dests * cap, width), preferred_element_type=F32)
        for t, p in enumerate(pieces):
            lane = as_column(lane_ref[:, p])
            total = part_ref[p, :] + jnp.dot(h2_ref[p, :], last_ref[...], preferred_element_type=F32)
            attn_ref[p, :] = total.astype(BF16)
            total = kept_ref[p, :].astype(F32) + total
            for m in range(4):
                part = found[t * ROWS_BLK : (t + 1) * ROWS_BLK, m * LANES : (m + 1) * LANES]
                total = total + jnp.where(lane == m, part, 0.0)
            out_ref[p, :] = total.astype(BF16)


def combine(spot_row, lane_row, last, part, kept, relayed, back):
    rows = part.shape[0]
    slots = back.shape[0] * back.shape[2]
    out = jax.ShapeDtypeStruct((rows, LANES), BF16)
    return pl.pallas_call(
        combine_kernel,
        in_specs=[VMEM] * 3 + [HBM] * 5,
        out_specs=[VMEM, VMEM],
        out_shape=[out, out],
        scratch_shapes=[
            pltpu.VMEM((back.shape[0], back.shape[2], 4 * LANES), BF16),
            pltpu.VMEM((rows, LANES), F32),
            pltpu.VMEM((rows, LANES), BF16),
            pltpu.VMEM((rows, LANES), BF16),
            pltpu.SemaphoreType.DMA((8,)),
        ],
        compiler_params=params(60),
        cost_estimate=cost(2 * rows * slots * 4 * LANES, 4 * 2**20),
        name="combine",
    )(spot_row, lane_row, last, part, kept, *relayed, back)


def swap(array, change):
    return lax.ppermute(array, "mp", [(i, i ^ change) for i in range(4)])


def exchange(array, axes):
    return lax.all_to_all(array, axes, split_axis=0, concat_axis=0, tiled=True)


def on_device(
    node_features,
    w_qkv,
    w_out,
    head_scale,
    norm_gain,
    router,
    w_gate,
    w_up,
    w_down,
    neighbor_blocks,
    expert_ids,
):
    parts = lax.axis_size("graph")
    part = lax.axis_index("graph")
    me = lax.axis_index("mp")
    rows, width = node_features.shape
    half_cap = CAP_E // 2

    requests = make_requests(neighbor_blocks, parts)
    incoming = exchange(requests.reshape(parts, 1, CAP_H), "graph")
    q, kv = qkv(node_features, w_qkv, head_scale)
    outgoing = pick_blocks(incoming, kv)
    halo = exchange(outgoing, "graph")

    which = me // 2
    me_ref = me[None].astype(jnp.int32)
    kept, given = split_weights(me_ref, w_gate, w_up, w_down, w_out, outgoing)
    weights = [kept, swap(kept, 1), swap(given, 2), swap(given, 3)]

    routed = expert_ids[:, 0]
    experts_all = router.shape[1]
    chosen = routed[:, None] == jnp.arange(experts_all, dtype=jnp.int32)[None, :]
    row_ids = jnp.arange(rows, dtype=jnp.int32)
    earlier = (row_ids[:, None] > row_ids[None, :]).astype(BF16)
    before = jnp.dot(earlier, chosen.astype(BF16), preferred_element_type=F32)
    rank = jnp.sum(jnp.where(chosen, before, 0.0), axis=1).astype(jnp.int32)
    second = (rank >= half_cap).astype(jnp.int32)
    lane = (routed % 2) * 2 + second
    spot = (routed // 2) * half_cap + rank - second * half_cap
    spot_row, lane_row = spot[None, :], lane[None, :]
    mine_row = jnp.where(lane == me, spot, -1)[None, :]
    x_there = exchange(place_rows(mine_row, node_features, parts, half_cap), "graph")

    route = lax.dynamic_index_in_dim(router, 2 * part + which, 1, keepdims=False).astype(F32)[None, :]
    heads, send = attention(
        neighbor_blocks, requests, q, kv, halo, spot_row, lane_row, weights[1:2], parts, half_cap
    )
    send, x_there = lax.optimization_barrier((send, x_there))
    heads_there = exchange(send.reshape(parts * 4, half_cap, LANES), ("graph", "mp"))
    route = hold_route(route, [send] + weights[2:])
    heads, heads_there, route = lax.optimization_barrier((heads, heads_there, route))
    by_one, by_three = swap(heads, 1), swap(heads, 3)
    produced = experts(
        me_ref,
        heads_there.reshape(parts, 4, half_cap, LANES),
        x_there,
        norm_gain[None, :],
        route,
        weights,
        (),
    )
    produced, by_one, by_three = lax.optimization_barrier((produced, by_one, by_three))
    middle = rows // 2
    relayed = [swap(by_three[:middle], 1), swap(by_one[middle:], 3)]
    part, kept_columns, last = attention_columns(
        me_ref, heads, by_one, by_three, weights, node_features
    )
    back = exchange(produced.reshape(parts * 4, half_cap, LANES), ("graph", "mp"))
    attn_out, layer_out = combine(
        spot_row, lane_row, last, part, kept_columns, relayed, back.reshape(parts, 4, half_cap, LANES)
    )
    return (attn_out, layer_out)


def solution(mesh):
    placed = (
        P("graph", None),
        P(None, None, "mp"),
        P("mp", None),
        P("mp"),
        P(),
        P(),
        P("graph", None, "mp"),
        P("graph", None, "mp"),
        P("graph", "mp", None),
        P("graph", None),
        P("graph", None),
    )
    return jax.shard_map(
        on_device,
        mesh=mesh,
        in_specs=placed,
        out_specs=(P("graph", "mp"), P("graph", "mp")),
        check_vma=False,
    )
```

```python
import math

import jax
import jax.numpy as jnp
from jax import lax
from jax.experimental import pallas as pl
from jax.experimental.pallas import tpu as pltpu
from jax.sharding import PartitionSpec as P

HEAD_DIM = 64
ROWS_BLK = 128
LOCAL_REFS = 4
CAP_H = 2
CAP_E = 96
EPS = 1e-06
LANES = 128

VMEM = pl.BlockSpec(memory_space=pltpu.VMEM)
SMEM = pl.BlockSpec(memory_space=pltpu.SMEM)
ANY = pl.BlockSpec(memory_space=pl.ANY)
HBM = pl.BlockSpec(memory_space=pltpu.HBM)
F32 = jnp.float32
BF16 = jnp.bfloat16


def params(mebibytes):
    return pltpu.CompilerParams(vmem_limit_bytes=mebibytes * 2**20)


def cost(flops, moved, transcendentals=0):
    return pl.CostEstimate(flops=flops, bytes_accessed=moved, transcendentals=transcendentals)


def head_units(values):
    low = lax.broadcasted_iota(jnp.int32, values.shape, 1) < HEAD_DIM
    squares = values * values
    first = jnp.sum(jnp.where(low, squares, 0.0), axis=1, keepdims=True)
    second = jnp.sum(jnp.where(low, 0.0, squares), axis=1, keepdims=True)
    scale = lax.rsqrt(jnp.where(low, first, second) * (1.0 / HEAD_DIM) + EPS)
    return values * scale


def qkv_kernel(x_ref, w_ref, scale_ref, q_ref, kv_ref):
    x = x_ref[...]
    rows = x.shape[0]
    query = jnp.dot(x, w_ref[0], preferred_element_type=F32)
    low = lax.broadcasted_iota(jnp.int32, (1, LANES), 1) < HEAD_DIM
    scale = jnp.where(low, scale_ref[0], scale_ref[1]) * (1.0 / math.sqrt(HEAD_DIM))
    q_ref[...] = (head_units(query) * scale).astype(BF16)
    key = jnp.dot(x, w_ref[1], preferred_element_type=F32)
    value = jnp.dot(x, w_ref[2], preferred_element_type=F32)
    kv_ref[:, :, :LANES] = head_units(key).astype(BF16).reshape(rows // ROWS_BLK, ROWS_BLK, LANES)
    kv_ref[:, :, LANES:] = value.astype(BF16).reshape(rows // ROWS_BLK, ROWS_BLK, LANES)


def qkv(x, w, scale):
    rows, width = x.shape
    tile = 1024
    blocks = tile // ROWS_BLK
    return pl.pallas_call(
        qkv_kernel,
        grid=(rows // tile,),
        in_specs=[
            pl.BlockSpec((tile, width), lambda i: (i, 0)),
            pl.BlockSpec((3, width, LANES), lambda i: (0, 0, 0)),
            SMEM,
        ],
        out_specs=[
            pl.BlockSpec((tile, LANES), lambda i: (i, 0)),
            pl.BlockSpec((blocks, ROWS_BLK, 2 * LANES), lambda i: (i, 0, 0)),
        ],
        out_shape=[
            jax.ShapeDtypeStruct((rows, LANES), BF16),
            jax.ShapeDtypeStruct((rows // ROWS_BLK, ROWS_BLK, 2 * LANES), BF16),
        ],
        compiler_params=params(60),
        cost_estimate=cost(2 * rows * width * 3 * LANES, 2 * rows * (width + 3 * LANES)),
        name="qkv",
    )(x, w, scale)


def requests_kernel(near_ref, out_ref):
    parts = out_ref.shape[0]
    rows, listed = near_ref.shape
    shape = (parts, rows)
    inside = lax.broadcasted_iota(jnp.int32, shape, 1)
    names = lax.broadcasted_iota(jnp.int32, shape, 0) * rows + inside
    wanted = jnp.zeros(shape, jnp.int32)
    for i in range(rows):
        for j in range(LOCAL_REFS, listed):
            wanted = jnp.where(names == near_ref[i, j], 1, wanted)
    first = jnp.min(jnp.where(wanted == 1, inside, rows - 1), axis=1, keepdims=True)
    last = jnp.max(jnp.where(wanted == 1, inside, 0), axis=1, keepdims=True)
    lane = lax.broadcasted_iota(jnp.int32, (parts, CAP_H), 1)
    out_ref[...] = jnp.where(lane == 0, first, last)


def make_requests(neighbor_blocks, parts):
    return pl.pallas_call(
        requests_kernel,
        in_specs=[SMEM],
        out_specs=VMEM,
        out_shape=jax.ShapeDtypeStruct((parts, CAP_H), jnp.int32),
        compiler_params=params(60),
        name="make_requests",
    )(neighbor_blocks)


def split_kernel(me_ref, gate_ref, up_ref, down_ref, out_w_ref, _, kept_ref, given_ref, sems):
    which = me_ref[0] // 2
    width = gate_ref.shape[1]
    copies = []
    for target, index in ((kept_ref, which), (given_ref, 1 - which)):
        for i, source in enumerate((gate_ref, up_ref, down_ref)):
            copies.append((source.at[index], target.at[pl.ds(i * width, width)]))
        copies.append((out_w_ref, target.at[pl.ds(3 * width, LANES)]))
    copies = [pltpu.make_async_copy(a, b, sems.at[i]) for i, (a, b) in enumerate(copies)]
    for copy in copies:
        copy.start()
    for copy in copies:
        copy.wait()


def split_weights(me, gate, up, down, out_w, after):
    width = gate.shape[1]
    out = jax.ShapeDtypeStruct((3 * width + LANES, width), BF16)
    return pl.pallas_call(
        split_kernel,
        in_specs=[SMEM] + [VMEM] * 4 + [ANY],
        out_specs=[HBM, HBM],
        out_shape=[out, out],
        scratch_shapes=[pltpu.SemaphoreType.DMA((8,))],
        compiler_params=params(60),
        cost_estimate=cost(0, 4 * out.size * 2),
        name="split_weights",
    )(me, gate, up, down, out_w, after)


def pick_kernel(wanted_ref, kv_ref, out_ref, sems):
    count = out_ref.shape[0]
    copies = [
        pltpu.make_async_copy(
            kv_ref.at[wanted_ref[i // CAP_H, 0, i % CAP_H]], out_ref.at[i], sems.at[i]
        )
        for i in range(count)
    ]
    for copy in copies:
        copy.start()
    for copy in copies:
        copy.wait()


def pick_blocks(wanted, kv):
    count = wanted.size
    out = jax.ShapeDtypeStruct((count,) + kv.shape[1:], kv.dtype)
    return pl.pallas_call(
        pick_kernel,
        in_specs=[SMEM, VMEM],
        out_specs=HBM,
        out_shape=out,
        scratch_shapes=[pltpu.SemaphoreType.DMA((count,))],
        compiler_params=params(60),
        cost_estimate=cost(0, 2 * out.size * 2),
        name="pick_blocks",
    )(wanted, kv)


def as_column(row):
    count = row.shape[1]
    shape = (count, count)
    same = lax.broadcasted_iota(jnp.int32, shape, 0) == lax.broadcasted_iota(jnp.int32, shape, 1)
    return jnp.sum(jnp.where(same, row.astype(F32), 0.0), axis=1, keepdims=True)


def attention_kernel(
    near_ref, asked_ref, q_ref, kv_ref, halo_ref, spot_ref, lane_ref, *rest
):
    heads_ref, send_ref, keys, values, spread = rest[-5:]
    blocks = kv_ref.shape[0]
    together = keys.shape[0]
    listed = near_ref.shape[1]
    low = lax.broadcasted_iota(jnp.int32, (ROWS_BLK, LANES), 1) < HEAD_DIM

    @pl.loop(0, blocks // together)
    def _(i):
        at = [i * together + t for t in range(together)]
        at_rows = [pl.ds(pl.multiple_of(b * ROWS_BLK, ROWS_BLK), ROWS_BLK) for b in at]
        scores = []
        for t, (b, rows) in enumerate(zip(at, at_rows)):
            q = q_ref[rows, :].astype(F32)
            both = jnp.concatenate([jnp.where(low, q, 0.0), jnp.where(low, 0.0, q)], axis=0).astype(BF16)
            for j in range(listed):
                name = near_ref[b, j]
                owner = name // blocks
                inside = name - owner * blocks
                if j < LOCAL_REFS:
                    block = kv_ref[inside]
                else:
                    second = (inside != asked_ref[owner, 0]).astype(jnp.int32)
                    block = halo_ref[owner * CAP_H + second]
                keys[t, j * ROWS_BLK : (j + 1) * ROWS_BLK, :] = block[:, :LANES]
                values[t, j * ROWS_BLK : (j + 1) * ROWS_BLK, :] = block[:, LANES:]
            scores.append(
                lax.dot_general(both, keys[t], (((1,), (1,)), ((), ())), preferred_element_type=F32)
            )
        for t, rows in enumerate(at_rows):
            largest = jnp.max(scores[t], axis=1, keepdims=True)
            expo = jnp.exp(scores[t] - largest)
            total = jnp.sum(expo, axis=1, keepdims=True)
            out = jnp.dot(expo.astype(BF16), values[t], preferred_element_type=F32) / total
            heads = jnp.where(low, out[:ROWS_BLK], out[ROWS_BLK:])
            heads_ref[rows, :] = heads.astype(BF16)
            lane = as_column(lane_ref[:, rows])
            for m in range(4):
                spread[rows, m * LANES : (m + 1) * LANES] = jnp.where(lane == m, heads, 0.0).astype(BF16)

    dests, cap = send_ref.shape[0], send_ref.shape[2]
    step = 4

    @pl.loop(0, dests // step)
    def _(i):
        tile = step * cap
        spot = spot_ref[...]
        here = lax.broadcasted_iota(jnp.int32, (tile, spot.shape[1]), 0) + i * tile
        hot = jnp.where(here == spot, 1.0, 0.0).astype(BF16)
        placed = jnp.dot(hot, spread[...], preferred_element_type=F32).astype(BF16)
        for d in range(step):
            for m in range(4):
                send_ref[i * step + d, m] = placed[d * cap : (d + 1) * cap, m * LANES : (m + 1) * LANES]


def attention(near, asked, q, kv, halo, spot_row, lane_row, after, parts, cap, together=4):
    rows = q.shape[0]
    keys = near.shape[1] * ROWS_BLK
    return pl.pallas_call(
        attention_kernel,
        in_specs=[SMEM, SMEM, VMEM, VMEM, VMEM, VMEM, VMEM] + [ANY] * len(after),
        out_specs=[VMEM, VMEM],
        out_shape=[
            jax.ShapeDtypeStruct((rows, LANES), BF16),
            jax.ShapeDtypeStruct((parts, 4, cap, LANES), BF16),
        ],
        scratch_shapes=[
            pltpu.VMEM((together, keys, LANES), BF16),
            pltpu.VMEM((together, keys, LANES), BF16),
            pltpu.VMEM((rows, 4 * LANES), BF16),
        ],
        compiler_params=params(60),
        cost_estimate=cost(12 * 10**9, 8 * 2**20, 2 * rows * keys),
        name="attention",
    )(near, asked, q, kv, halo, spot_row, lane_row, *after)


def place_kernel(spot_ref, x_ref, out_ref):
    dests, cap = out_ref.shape[0], out_ref.shape[1]
    step = 4

    @pl.loop(0, dests // step)
    def _(i):
        tile = step * cap
        spot = spot_ref[...]
        here = lax.broadcasted_iota(jnp.int32, (tile, spot.shape[1]), 0) + i * tile
        hot = jnp.where(here == spot, 1.0, 0.0).astype(BF16)
        placed = jnp.dot(hot, x_ref[...], preferred_element_type=F32).astype(BF16)
        for d in range(step):
            out_ref[i * step + d] = placed[d * cap : (d + 1) * cap, :]


def place_rows(spot_row, x, parts, cap):
    rows, width = x.shape
    return pl.pallas_call(
        place_kernel,
        in_specs=[VMEM, VMEM],
        out_specs=VMEM,
        out_shape=jax.ShapeDtypeStruct((parts, cap, width), BF16),
        compiler_params=params(60),
        cost_estimate=cost(2 * parts * cap * rows * width, 4 * 2**20),
        name="place_rows",
    )(spot_row, x)


def route_kernel(route_ref, *rest):
    rest[-1][...] = route_ref[...]


def hold_route(route, after):
    return pl.pallas_call(
        route_kernel,
        in_specs=[VMEM] + [ANY] * len(after),
        out_specs=VMEM,
        out_shape=jax.ShapeDtypeStruct(route.shape, route.dtype),
        compiler_params=params(60),
        cost_estimate=cost(2 * 10**10, 10**7),
        name="hold_route",
    )(route, *after)


def experts_kernel(me_ref, gain_ref, route_ref, h_ref, x_ref, w0_ref, w1_ref, w2_ref, w3_ref, *rest):
    out_ref, heads, features, project, quarters, results, sems = rest[-7:]
    me = me_ref[0]
    tiles, step, cap, width = features.shape
    tile = step * cap
    sources = (w0_ref, w1_ref, w2_ref, w3_ref)
    sizes = ((h_ref, heads), (x_ref, features))
    small = [
        pltpu.make_async_copy(
            w.at[pl.ds(3 * width, LANES)], project.at[pl.ds(k * LANES, LANES)], sems.at[k]
        )
        for k, w in enumerate(sources)
    ]
    large = [
        pltpu.make_async_copy(w.at[pl.ds(0, 3 * width)], quarters.at[k], sems.at[4 + k])
        for k, w in enumerate(sources)
    ]
    rows = [
        [
            pltpu.make_async_copy(source.at[pl.ds(t * step, step)], target.at[t], sems.at[8 + 2 * t + i])
            for i, (source, target) in enumerate(sizes)
        ]
        for t in range(tiles)
    ]
    outs = [
        pltpu.make_async_copy(
            results.at[t], out_ref.at[pl.ds(t * step, step)], sems.at[8 + 2 * tiles + t]
        )
        for t in range(tiles)
    ]
    for copy in rows[0] + small + large + [c for later in rows[1:] for c in later]:
        copy.start()
    for copy in small:
        copy.wait()
    for t in range(tiles):
        for copy in rows[t]:
            copy.wait()
        arrived = jnp.concatenate([heads[t, :, me ^ k].reshape(tile, LANES) for k in range(4)], axis=1)
        mixed = features[t].reshape(tile, width).astype(F32) + jnp.dot(
            arrived, project[...], preferred_element_type=F32
        )
        mean = jnp.mean(mixed * mixed, axis=1, keepdims=True)
        normed = (mixed * lax.rsqrt(mean + EPS) * gain_ref[...]).astype(BF16)
        logit = jnp.sum(normed.astype(F32) * route_ref[...], axis=1, keepdims=True)
        gate = 1.0 / (1.0 + jnp.exp(-logit))
        result = None
        for k in range(4):
            if t == 0:
                large[k].wait()
            hidden = []
            for c in range(0, width, 256):
                left = jnp.dot(normed, quarters[k, :width, c : c + 256], preferred_element_type=F32)
                right = jnp.dot(
                    normed, quarters[k, width : 2 * width, c : c + 256], preferred_element_type=F32
                )
                half = 0.5 * left
                hidden.append(((half + half * jnp.tanh(half)) * right).astype(BF16))
            hidden = jnp.concatenate(hidden, axis=1)
            term = jnp.dot(hidden, quarters[k, 2 * width :, :], preferred_element_type=F32)
            result = term if result is None else result + term
        result = (gate * result).astype(BF16).reshape(step, cap, width)
        for m in range(4):
            results[t, :, m] = result[:, :, m * LANES : (m + 1) * LANES]
        outs[t].start()
    for copy in outs:
        copy.wait()


def experts(me, heads, x, gain, route, weights, after, tiles=2):
    parts, cap, width = x.shape
    step = parts // tiles
    return pl.pallas_call(
        experts_kernel,
        in_specs=[SMEM, VMEM, VMEM, HBM, HBM] + [ANY] * (4 + len(after)),
        out_specs=HBM,
        out_shape=jax.ShapeDtypeStruct((parts, 4, cap, LANES), BF16),
        scratch_shapes=[
            pltpu.VMEM((tiles, step, 4, cap, LANES), BF16),
            pltpu.VMEM((tiles, step, cap, width), BF16),
            pltpu.VMEM((width, width), BF16),
            pltpu.VMEM((4, 3 * width, width), BF16),
            pltpu.VMEM((tiles, step, 4, cap, LANES), BF16),
            pltpu.SemaphoreType.DMA((8 + 3 * tiles,)),
        ],
        compiler_params=params(58),
        cost_estimate=cost(2 * parts * cap * width * (12 * width + width), 12 * 2**20),
        name="experts",
    )(me, gain, route, heads, x, *weights, *after)


def columns_kernel(
    me_ref, h0_ref, h1_ref, h3_ref, w0_ref, w1_ref, w2_ref, w3_ref, x_ref, part_ref, kept_ref, last_ref, sem
):
    columns = pl.ds(pl.multiple_of(me_ref[0] * LANES, LANES), LANES)
    copy = pltpu.make_async_copy(x_ref.at[:, columns], kept_ref, sem)
    copy.start()
    pieces = [h[...] for h in (h0_ref, h1_ref, h3_ref)]
    weights = [w[:, columns] for w in (w0_ref, w1_ref, w3_ref)]
    part_ref[...] = jnp.dot(
        jnp.concatenate(pieces, axis=1), jnp.concatenate(weights, axis=0), preferred_element_type=F32
    )
    last_ref[...] = w2_ref[:, columns]
    copy.wait()


def attention_columns(me, heads, by_one, by_three, weights, x):
    rows, width = x.shape
    last = weights[0].shape[0] // LANES - 1
    out = pl.BlockSpec((rows, LANES), lambda i: (0, 0))
    return pl.pallas_call(
        columns_kernel,
        grid=(1,),
        in_specs=[SMEM]
        + [out] * 3
        + [pl.BlockSpec((LANES, width), lambda i: (last, 0))] * 4
        + [ANY],
        out_specs=[out, out, pl.BlockSpec((LANES, LANES), lambda i: (0, 0))],
        out_shape=[
            jax.ShapeDtypeStruct((rows, LANES), F32),
            jax.ShapeDtypeStruct((rows, LANES), BF16),
            jax.ShapeDtypeStruct((LANES, LANES), BF16),
        ],
        scratch_shapes=[pltpu.SemaphoreType.DMA],
        compiler_params=params(60),
        cost_estimate=cost(2 * rows * width * LANES, 8 * 2**20),
        name="attention_columns",
    )(me, heads, by_one, by_three, *weights, x)


def combine_kernel(
    spot_ref, lane_ref, last_ref, part_hbm, kept_hbm, top_hbm, bottom_hbm, back_ref, attn_hbm, out_hbm,
    slots, part_ref, kept_ref, h2_ref, attn_ref, out_ref, sems
):
    dests, cap, width = slots.shape
    rows = out_ref.shape[0]
    copies = [
        pltpu.make_async_copy(
            back_ref.at[:, m], slots.at[:, :, pl.ds(m * LANES, LANES)], sems.at[m]
        )
        for m in range(4)
    ]
    half = rows // 2
    for source, target in (
        (part_hbm, part_ref),
        (kept_hbm, kept_ref),
        (top_hbm, h2_ref.at[pl.ds(0, half)]),
        (bottom_hbm, h2_ref.at[pl.ds(half, half)]),
    ):
        copies.append(pltpu.make_async_copy(source, target, sems.at[len(copies)]))
    for copy in copies:
        copy.start()
    tile = 256
    outs = []
    names = lax.broadcasted_iota(jnp.int32, (ROWS_BLK, dests * cap), 1).astype(F32)

    for i in range(rows // tile):
        pieces = [pl.ds(i * tile + t * ROWS_BLK, ROWS_BLK) for t in range(tile // ROWS_BLK)]
        hot = jnp.concatenate(
            [jnp.where(names == as_column(spot_ref[:, p]), 1.0, 0.0).astype(BF16) for p in pieces], axis=0
        )
        if i == 0:
            for copy in copies[:4]:
                copy.wait()
        found = jnp.dot(hot, slots[...].reshape(dests * cap, width), preferred_element_type=F32)
        if i == 0:
            for copy in copies[4:]:
                copy.wait()
        whole = slice(i * tile, (i + 1) * tile)
        added = jnp.dot(h2_ref[whole, :], last_ref[...], preferred_element_type=F32)
        for t, p in enumerate(pieces):
            lane = as_column(lane_ref[:, p])
            total = part_ref[p, :] + added[t * ROWS_BLK : (t + 1) * ROWS_BLK]
            attn_ref[p, :] = total.astype(BF16)
            total = kept_ref[p, :].astype(F32) + total
            for m in range(4):
                part = found[t * ROWS_BLK : (t + 1) * ROWS_BLK, m * LANES : (m + 1) * LANES]
                total = total + jnp.where(lane == m, part, 0.0)
            out_ref[p, :] = total.astype(BF16)
        for source, target in ((attn_ref, attn_hbm), (out_ref, out_hbm)):
            here = pl.ds(i * tile, tile)
            outs.append(pltpu.make_async_copy(source.at[here], target.at[here], sems.at[8 + len(outs)]))
            outs[-1].start()
    for copy in outs:
        copy.wait()


def combine(spot_row, lane_row, last, part, kept, relayed, back):
    rows = part.shape[0]
    slots = back.shape[0] * back.shape[2]
    out = jax.ShapeDtypeStruct((rows, LANES), BF16)
    return pl.pallas_call(
        combine_kernel,
        in_specs=[VMEM] * 3 + [HBM] * 5,
        out_specs=[HBM, HBM],
        out_shape=[out, out],
        scratch_shapes=[
            pltpu.VMEM((back.shape[0], back.shape[2], 4 * LANES), BF16),
            pltpu.VMEM((rows, LANES), F32),
            pltpu.VMEM((rows, LANES), BF16),
            pltpu.VMEM((rows, LANES), BF16),
            pltpu.VMEM((rows, LANES), BF16),
            pltpu.VMEM((rows, LANES), BF16),
            pltpu.SemaphoreType.DMA((8 + 2 * (rows // 256),)),
        ],
        compiler_params=params(60),
        cost_estimate=cost(2 * rows * slots * 4 * LANES, 4 * 2**20),
        name="combine",
    )(spot_row, lane_row, last, part, kept, *relayed, back)


def swap(array, change):
    return lax.ppermute(array, "mp", [(i, i ^ change) for i in range(4)])


def exchange(array, axes):
    return lax.all_to_all(array, axes, split_axis=0, concat_axis=0, tiled=True)


def on_device(
    node_features,
    w_qkv,
    w_out,
    head_scale,
    norm_gain,
    router,
    w_gate,
    w_up,
    w_down,
    neighbor_blocks,
    expert_ids,
):
    parts = lax.axis_size("graph")
    part = lax.axis_index("graph")
    me = lax.axis_index("mp")
    rows, width = node_features.shape
    half_cap = CAP_E // 2

    requests = make_requests(neighbor_blocks, parts)
    incoming = exchange(requests.reshape(parts, 1, CAP_H), "graph")
    q, kv = qkv(node_features, w_qkv, head_scale)
    outgoing = pick_blocks(incoming, kv)
    halo = exchange(outgoing, "graph")

    which = me // 2
    me_ref = me[None].astype(jnp.int32)
    kept, given = split_weights(me_ref, w_gate, w_up, w_down, w_out, outgoing)
    weights = [kept, swap(kept, 1), swap(given, 2), swap(given, 3)]

    routed = expert_ids[:, 0]
    experts_all = router.shape[1]
    chosen = routed[:, None] == jnp.arange(experts_all, dtype=jnp.int32)[None, :]
    row_ids = jnp.arange(rows, dtype=jnp.int32)
    earlier = (row_ids[:, None] > row_ids[None, :]).astype(BF16)
    before = jnp.dot(earlier, chosen.astype(BF16), preferred_element_type=F32)
    rank = jnp.sum(jnp.where(chosen, before, 0.0), axis=1).astype(jnp.int32)
    second = (rank >= half_cap).astype(jnp.int32)
    lane = (routed % 2) * 2 + second
    spot = (routed // 2) * half_cap + rank - second * half_cap
    spot_row, lane_row = spot[None, :], lane[None, :]
    mine_row = jnp.where(lane == me, spot, -1)[None, :]
    x_there = exchange(place_rows(mine_row, node_features, parts, half_cap), "graph")

    route = lax.dynamic_index_in_dim(router, 2 * part + which, 1, keepdims=False).astype(F32)[None, :]
    heads, send = attention(
        neighbor_blocks, requests, q, kv, halo, spot_row, lane_row, weights[1:2], parts, half_cap
    )
    send, x_there = lax.optimization_barrier((send, x_there))
    heads_there = exchange(send.reshape(parts * 4, half_cap, LANES), ("graph", "mp"))
    route = hold_route(route, [send] + weights[2:])
    heads, heads_there, route = lax.optimization_barrier((heads, heads_there, route))
    by_one, by_three = swap(heads, 1), swap(heads, 3)
    produced = experts(
        me_ref,
        heads_there.reshape(parts, 4, half_cap, LANES),
        x_there,
        norm_gain[None, :],
        route,
        weights,
        (),
    )
    produced, by_one, by_three = lax.optimization_barrier((produced, by_one, by_three))
    middle = rows // 2
    relayed = [swap(by_three[:middle], 1), swap(by_one[middle:], 3)]
    part, kept_columns, last = attention_columns(
        me_ref, heads, by_one, by_three, weights, node_features
    )
    back = exchange(produced.reshape(parts * 4, half_cap, LANES), ("graph", "mp"))
    attn_out, layer_out = combine(
        spot_row, lane_row, last, part, kept_columns, relayed, back.reshape(parts, 4, half_cap, LANES)
    )
    return (attn_out, layer_out)


def solution(mesh):
    placed = (
        P("graph", None),
        P(None, None, "mp"),
        P("mp", None),
        P("mp"),
        P(),
        P(),
        P("graph", None, "mp"),
        P("graph", None, "mp"),
        P("graph", "mp", None),
        P("graph", None),
        P("graph", None),
    )
    return jax.shard_map(
        on_device,
        mesh=mesh,
        in_specs=placed,
        out_specs=(P("graph", "mp"), P("graph", "mp")),
        check_vma=False,
    )
```

```python
import math

import jax
import jax.numpy as jnp
from jax import lax
from jax.experimental import pallas as pl
from jax.experimental.pallas import tpu as pltpu
from jax.sharding import PartitionSpec as P

HEAD_DIM = 64
ROWS_BLK = 128
LOCAL_REFS = 4
CAP_H = 2
CAP_E = 96
EPS = 1e-06
LANES = 128

VMEM = pl.BlockSpec(memory_space=pltpu.VMEM)
SMEM = pl.BlockSpec(memory_space=pltpu.SMEM)
ANY = pl.BlockSpec(memory_space=pl.ANY)
HBM = pl.BlockSpec(memory_space=pltpu.HBM)
F32 = jnp.float32
BF16 = jnp.bfloat16


def params(mebibytes):
    return pltpu.CompilerParams(vmem_limit_bytes=mebibytes * 2**20)


def cost(flops, moved, transcendentals=0):
    return pl.CostEstimate(flops=flops, bytes_accessed=moved, transcendentals=transcendentals)


def head_units(values):
    low = lax.broadcasted_iota(jnp.int32, values.shape, 1) < HEAD_DIM
    squares = values * values
    first = jnp.sum(jnp.where(low, squares, 0.0), axis=1, keepdims=True)
    second = jnp.sum(jnp.where(low, 0.0, squares), axis=1, keepdims=True)
    scale = lax.rsqrt(jnp.where(low, first, second) * (1.0 / HEAD_DIM) + EPS)
    return values * scale


def qkv_kernel(x_ref, w_ref, scale_ref, q_ref, kv_ref):
    x = x_ref[...]
    rows = x.shape[0]
    query = jnp.dot(x, w_ref[0], preferred_element_type=F32)
    low = lax.broadcasted_iota(jnp.int32, (1, LANES), 1) < HEAD_DIM
    scale = jnp.where(low, scale_ref[0], scale_ref[1]) * (1.0 / math.sqrt(HEAD_DIM))
    q_ref[...] = (head_units(query) * scale).astype(BF16)
    key = jnp.dot(x, w_ref[1], preferred_element_type=F32)
    value = jnp.dot(x, w_ref[2], preferred_element_type=F32)
    kv_ref[:, :, :LANES] = head_units(key).astype(BF16).reshape(rows // ROWS_BLK, ROWS_BLK, LANES)
    kv_ref[:, :, LANES:] = value.astype(BF16).reshape(rows // ROWS_BLK, ROWS_BLK, LANES)


def qkv(x, w, scale):
    rows, width = x.shape
    tile = 1024
    blocks = tile // ROWS_BLK
    return pl.pallas_call(
        qkv_kernel,
        grid=(rows // tile,),
        in_specs=[
            pl.BlockSpec((tile, width), lambda i: (i, 0)),
            pl.BlockSpec((3, width, LANES), lambda i: (0, 0, 0)),
            SMEM,
        ],
        out_specs=[
            pl.BlockSpec((tile, LANES), lambda i: (i, 0)),
            pl.BlockSpec((blocks, ROWS_BLK, 2 * LANES), lambda i: (i, 0, 0)),
        ],
        out_shape=[
            jax.ShapeDtypeStruct((rows, LANES), BF16),
            jax.ShapeDtypeStruct((rows // ROWS_BLK, ROWS_BLK, 2 * LANES), BF16),
        ],
        compiler_params=params(60),
        cost_estimate=cost(2 * rows * width * 3 * LANES, 2 * rows * (width + 3 * LANES)),
        name="qkv",
    )(x, w, scale)


def requests_kernel(near_ref, out_ref):
    parts = out_ref.shape[0]
    rows, listed = near_ref.shape
    shape = (parts, rows)
    inside = lax.broadcasted_iota(jnp.int32, shape, 1)
    names = lax.broadcasted_iota(jnp.int32, shape, 0) * rows + inside
    wanted = jnp.zeros(shape, jnp.int32)
    for i in range(rows):
        for j in range(LOCAL_REFS, listed):
            wanted = jnp.where(names == near_ref[i, j], 1, wanted)
    first = jnp.min(jnp.where(wanted == 1, inside, rows - 1), axis=1, keepdims=True)
    last = jnp.max(jnp.where(wanted == 1, inside, 0), axis=1, keepdims=True)
    lane = lax.broadcasted_iota(jnp.int32, (parts, CAP_H), 1)
    out_ref[...] = jnp.where(lane == 0, first, last)


def make_requests(neighbor_blocks, parts):
    return pl.pallas_call(
        requests_kernel,
        in_specs=[SMEM],
        out_specs=VMEM,
        out_shape=jax.ShapeDtypeStruct((parts, CAP_H), jnp.int32),
        compiler_params=params(60),
        name="make_requests",
    )(neighbor_blocks)


def split_kernel(me_ref, gate_ref, up_ref, down_ref, out_w_ref, _, kept_ref, given_ref, sems):
    which = me_ref[0] // 2
    width = gate_ref.shape[1]
    copies = []
    for target, index in ((kept_ref, which), (given_ref, 1 - which)):
        for i, source in enumerate((gate_ref, up_ref, down_ref)):
            copies.append((source.at[index], target.at[pl.ds(i * width, width)]))
        copies.append((out_w_ref, target.at[pl.ds(3 * width, LANES)]))
    copies = [pltpu.make_async_copy(a, b, sems.at[i]) for i, (a, b) in enumerate(copies)]
    for copy in copies:
        copy.start()
    for copy in copies:
        copy.wait()


def split_weights(me, gate, up, down, out_w, after):
    width = gate.shape[1]
    out = jax.ShapeDtypeStruct((3 * width + LANES, width), BF16)
    return pl.pallas_call(
        split_kernel,
        in_specs=[SMEM] + [VMEM] * 4 + [ANY],
        out_specs=[HBM, HBM],
        out_shape=[out, out],
        scratch_shapes=[pltpu.SemaphoreType.DMA((8,))],
        compiler_params=params(60),
        cost_estimate=cost(0, 4 * out.size * 2),
        name="split_weights",
    )(me, gate, up, down, out_w, after)


def pick_kernel(wanted_ref, kv_ref, out_ref, sems):
    count = out_ref.shape[0]
    copies = [
        pltpu.make_async_copy(
            kv_ref.at[wanted_ref[i // CAP_H, 0, i % CAP_H]], out_ref.at[i], sems.at[i]
        )
        for i in range(count)
    ]
    for copy in copies:
        copy.start()
    for copy in copies:
        copy.wait()


def pick_blocks(wanted, kv):
    count = wanted.size
    out = jax.ShapeDtypeStruct((count,) + kv.shape[1:], kv.dtype)
    return pl.pallas_call(
        pick_kernel,
        in_specs=[SMEM, VMEM],
        out_specs=HBM,
        out_shape=out,
        scratch_shapes=[pltpu.SemaphoreType.DMA((count,))],
        compiler_params=params(60),
        cost_estimate=cost(0, 2 * out.size * 2),
        name="pick_blocks",
    )(wanted, kv)


def as_column(row):
    count = row.shape[1]
    shape = (count, count)
    same = lax.broadcasted_iota(jnp.int32, shape, 0) == lax.broadcasted_iota(jnp.int32, shape, 1)
    return jnp.sum(jnp.where(same, row.astype(F32), 0.0), axis=1, keepdims=True)


def attention_kernel(
    near_ref, asked_ref, q_ref, kv_ref, halo_ref, spot_ref, lane_ref, *rest
):
    heads_ref, send_ref, keys, values, spread = rest[-5:]
    blocks = kv_ref.shape[0]
    together = keys.shape[0]
    listed = near_ref.shape[1]
    low = lax.broadcasted_iota(jnp.int32, (ROWS_BLK, LANES), 1) < HEAD_DIM

    @pl.loop(0, blocks // together)
    def _(i):
        at = [i * together + t for t in range(together)]
        at_rows = [pl.ds(pl.multiple_of(b * ROWS_BLK, ROWS_BLK), ROWS_BLK) for b in at]
        scores = []
        for t, (b, rows) in enumerate(zip(at, at_rows)):
            q = q_ref[rows, :].astype(F32)
            both = jnp.concatenate([jnp.where(low, q, 0.0), jnp.where(low, 0.0, q)], axis=0).astype(BF16)
            for j in range(listed):
                name = near_ref[b, j]
                owner = name // blocks
                inside = name - owner * blocks
                if j < LOCAL_REFS:
                    block = kv_ref[inside]
                else:
                    second = (inside != asked_ref[owner, 0]).astype(jnp.int32)
                    block = halo_ref[owner * CAP_H + second]
                keys[t, j * ROWS_BLK : (j + 1) * ROWS_BLK, :] = block[:, :LANES]
                values[t, j * ROWS_BLK : (j + 1) * ROWS_BLK, :] = block[:, LANES:]
            scores.append(
                lax.dot_general(both, keys[t], (((1,), (1,)), ((), ())), preferred_element_type=F32)
            )
        for t, rows in enumerate(at_rows):
            largest = jnp.max(scores[t], axis=1, keepdims=True)
            expo = jnp.exp(scores[t] - largest)
            total = jnp.sum(expo, axis=1, keepdims=True)
            out = jnp.dot(expo.astype(BF16), values[t], preferred_element_type=F32) / total
            heads = jnp.where(low, out[:ROWS_BLK], out[ROWS_BLK:])
            heads_ref[rows, :] = heads.astype(BF16)
            lane = as_column(lane_ref[:, rows])
            for m in range(4):
                spread[rows, m * LANES : (m + 1) * LANES] = jnp.where(lane == m, heads, 0.0).astype(BF16)

    dests, cap = send_ref.shape[0], send_ref.shape[2]
    step = 4

    @pl.loop(0, dests // step)
    def _(i):
        tile = step * cap
        spot = spot_ref[...]
        here = lax.broadcasted_iota(jnp.int32, (tile, spot.shape[1]), 0) + i * tile
        hot = jnp.where(here == spot, 1.0, 0.0).astype(BF16)
        placed = jnp.dot(hot, spread[...], preferred_element_type=F32).astype(BF16)
        for d in range(step):
            for m in range(4):
                send_ref[i * step + d, m] = placed[d * cap : (d + 1) * cap, m * LANES : (m + 1) * LANES]


def attention(near, asked, q, kv, halo, spot_row, lane_row, after, parts, cap, together=4):
    rows = q.shape[0]
    keys = near.shape[1] * ROWS_BLK
    return pl.pallas_call(
        attention_kernel,
        in_specs=[SMEM, SMEM, VMEM, VMEM, VMEM, VMEM, VMEM] + [ANY] * len(after),
        out_specs=[VMEM, VMEM],
        out_shape=[
            jax.ShapeDtypeStruct((rows, LANES), BF16),
            jax.ShapeDtypeStruct((parts, 4, cap, LANES), BF16),
        ],
        scratch_shapes=[
            pltpu.VMEM((together, keys, LANES), BF16),
            pltpu.VMEM((together, keys, LANES), BF16),
            pltpu.VMEM((rows, 4 * LANES), BF16),
        ],
        compiler_params=params(60),
        cost_estimate=cost(12 * 10**9, 8 * 2**20, 2 * rows * keys),
        name="attention",
    )(near, asked, q, kv, halo, spot_row, lane_row, *after)


def place_kernel(spot_ref, x_ref, out_ref):
    dests, cap = out_ref.shape[0], out_ref.shape[1]
    step = 4

    @pl.loop(0, dests // step)
    def _(i):
        tile = step * cap
        spot = spot_ref[...]
        here = lax.broadcasted_iota(jnp.int32, (tile, spot.shape[1]), 0) + i * tile
        hot = jnp.where(here == spot, 1.0, 0.0).astype(BF16)
        placed = jnp.dot(hot, x_ref[...], preferred_element_type=F32).astype(BF16)
        for d in range(step):
            out_ref[i * step + d] = placed[d * cap : (d + 1) * cap, :]


def place_rows(spot_row, x, parts, cap):
    rows, width = x.shape
    return pl.pallas_call(
        place_kernel,
        in_specs=[VMEM, VMEM],
        out_specs=VMEM,
        out_shape=jax.ShapeDtypeStruct((parts, cap, width), BF16),
        compiler_params=params(60),
        cost_estimate=cost(2 * parts * cap * rows * width, 4 * 2**20),
        name="place_rows",
    )(spot_row, x)


def route_kernel(route_ref, *rest):
    rest[-1][...] = route_ref[...]


def hold_route(route, after):
    return pl.pallas_call(
        route_kernel,
        in_specs=[VMEM] + [ANY] * len(after),
        out_specs=VMEM,
        out_shape=jax.ShapeDtypeStruct(route.shape, route.dtype),
        compiler_params=params(60),
        cost_estimate=cost(2 * 10**10, 10**7),
        name="hold_route",
    )(route, *after)


def experts_kernel(me_ref, gain_ref, route_ref, h_ref, x_ref, w0_ref, w1_ref, w2_ref, w3_ref, *rest):
    out_ref, heads, features, project, quarters, results, sems = rest[-7:]
    me = me_ref[0]
    tiles, step, cap, width = features.shape
    tile = step * cap
    sources = (w0_ref, w1_ref, w2_ref, w3_ref)
    sizes = ((h_ref, heads), (x_ref, features))
    small = [
        pltpu.make_async_copy(
            w.at[pl.ds(3 * width, LANES)], project.at[pl.ds(k * LANES, LANES)], sems.at[k]
        )
        for k, w in enumerate(sources)
    ]
    large = [
        pltpu.make_async_copy(w.at[pl.ds(0, 3 * width)], quarters.at[k], sems.at[4 + k])
        for k, w in enumerate(sources)
    ]
    rows = [
        [
            pltpu.make_async_copy(source.at[pl.ds(t * step, step)], target.at[t], sems.at[8 + 2 * t + i])
            for i, (source, target) in enumerate(sizes)
        ]
        for t in range(tiles)
    ]
    outs = [
        pltpu.make_async_copy(
            results.at[t], out_ref.at[pl.ds(t * step, step)], sems.at[8 + 2 * tiles + t]
        )
        for t in range(tiles)
    ]
    for copy in rows[0] + small + large + [c for later in rows[1:] for c in later]:
        copy.start()
    for copy in small:
        copy.wait()
    for t in range(tiles):
        for copy in rows[t]:
            copy.wait()
        arrived = jnp.concatenate([heads[t, :, me ^ k].reshape(tile, LANES) for k in range(4)], axis=1)
        mixed = features[t].reshape(tile, width).astype(F32) + jnp.dot(
            arrived, project[...], preferred_element_type=F32
        )
        mean = jnp.mean(mixed * mixed, axis=1, keepdims=True)
        normed = (mixed * lax.rsqrt(mean + EPS) * gain_ref[...]).astype(BF16)
        logit = jnp.sum(normed.astype(F32) * route_ref[...], axis=1, keepdims=True)
        gate = 1.0 / (1.0 + jnp.exp(-logit))
        result = None
        for k in range(4):
            if t == 0:
                large[k].wait()
            hidden = []
            for c in range(0, width, 256):
                left = jnp.dot(normed, quarters[k, :width, c : c + 256], preferred_element_type=F32)
                right = jnp.dot(
                    normed, quarters[k, width : 2 * width, c : c + 256], preferred_element_type=F32
                )
                half = 0.5 * left
                hidden.append(((half + half * jnp.tanh(half)) * right).astype(BF16))
            hidden = jnp.concatenate(hidden, axis=1)
            term = jnp.dot(hidden, quarters[k, 2 * width :, :], preferred_element_type=F32)
            result = term if result is None else result + term
        result = (gate * result).astype(BF16).reshape(step, cap, width)
        for m in range(4):
            results[t, :, m] = result[:, :, m * LANES : (m + 1) * LANES]
        outs[t].start()
    for copy in outs:
        copy.wait()


def experts(me, heads, x, gain, route, weights, after, tiles=2):
    parts, cap, width = x.shape
    step = parts // tiles
    return pl.pallas_call(
        experts_kernel,
        in_specs=[SMEM, VMEM, VMEM, HBM, HBM] + [ANY] * (4 + len(after)),
        out_specs=HBM,
        out_shape=jax.ShapeDtypeStruct((parts, 4, cap, LANES), BF16),
        scratch_shapes=[
            pltpu.VMEM((tiles, step, 4, cap, LANES), BF16),
            pltpu.VMEM((tiles, step, cap, width), BF16),
            pltpu.VMEM((width, width), BF16),
            pltpu.VMEM((4, 3 * width, width), BF16),
            pltpu.VMEM((tiles, step, 4, cap, LANES), BF16),
            pltpu.SemaphoreType.DMA((8 + 3 * tiles,)),
        ],
        compiler_params=params(58),
        cost_estimate=cost(2 * parts * cap * width * (12 * width + width), 12 * 2**20),
        name="experts",
    )(me, gain, route, heads, x, *weights, *after)


def columns_kernel(
    me_ref, h0_ref, h1_ref, h3_ref, w0_ref, w1_ref, w2_ref, w3_ref, x_ref, part_ref, kept_ref, last_ref, sem
):
    columns = pl.ds(pl.multiple_of(me_ref[0] * LANES, LANES), LANES)
    copy = pltpu.make_async_copy(x_ref.at[:, columns], kept_ref, sem)
    copy.start()
    pieces = [h[...] for h in (h0_ref, h1_ref, h3_ref)]
    weights = [w[:, columns] for w in (w0_ref, w1_ref, w3_ref)]
    part_ref[...] = jnp.dot(
        jnp.concatenate(pieces, axis=1), jnp.concatenate(weights, axis=0), preferred_element_type=F32
    )
    last_ref[...] = w2_ref[:, columns]
    copy.wait()


def attention_columns(me, heads, by_one, by_three, weights, x):
    rows, width = x.shape
    last = weights[0].shape[0] // LANES - 1
    out = pl.BlockSpec((rows, LANES), lambda i: (0, 0))
    return pl.pallas_call(
        columns_kernel,
        grid=(1,),
        in_specs=[SMEM]
        + [out] * 3
        + [pl.BlockSpec((LANES, width), lambda i: (last, 0))] * 4
        + [ANY],
        out_specs=[out, out, pl.BlockSpec((LANES, LANES), lambda i: (0, 0))],
        out_shape=[
            jax.ShapeDtypeStruct((rows, LANES), F32),
            jax.ShapeDtypeStruct((rows, LANES), BF16),
            jax.ShapeDtypeStruct((LANES, LANES), BF16),
        ],
        scratch_shapes=[pltpu.SemaphoreType.DMA],
        compiler_params=params(60),
        cost_estimate=cost(2 * rows * width * LANES, 8 * 2**20),
        name="attention_columns",
    )(me, heads, by_one, by_three, *weights, x)


def combine_kernel(
    spot_ref, lane_ref, last_ref, part_hbm, kept_hbm, h2_hbm, back_ref, attn_hbm, out_hbm,
    slots, part_ref, kept_ref, h2_ref, attn_ref, out_ref, sems
):
    dests, cap, width = slots.shape
    rows = out_ref.shape[0]
    copies = [
        pltpu.make_async_copy(
            back_ref.at[:, m], slots.at[:, :, pl.ds(m * LANES, LANES)], sems.at[m]
        )
        for m in range(4)
    ]
    for source, target in (
        (part_hbm, part_ref),
        (kept_hbm, kept_ref),
        (h2_hbm, h2_ref),
    ):
        copies.append(pltpu.make_async_copy(source, target, sems.at[len(copies)]))
    for copy in copies:
        copy.start()
    tile = 256
    outs = []
    names = lax.broadcasted_iota(jnp.int32, (ROWS_BLK, dests * cap), 1).astype(F32)

    for i in range(rows // tile):
        pieces = [pl.ds(i * tile + t * ROWS_BLK, ROWS_BLK) for t in range(tile // ROWS_BLK)]
        hot = jnp.concatenate(
            [jnp.where(names == as_column(spot_ref[:, p]), 1.0, 0.0).astype(BF16) for p in pieces], axis=0
        )
        if i == 0:
            for copy in copies[:4]:
                copy.wait()
        found = jnp.dot(hot, slots[...].reshape(dests * cap, width), preferred_element_type=F32)
        if i == 0:
            for copy in copies[4:]:
                copy.wait()
        whole = slice(i * tile, (i + 1) * tile)
        added = jnp.dot(h2_ref[whole, :], last_ref[...], preferred_element_type=F32)
        for t, p in enumerate(pieces):
            lane = as_column(lane_ref[:, p])
            total = part_ref[p, :] + added[t * ROWS_BLK : (t + 1) * ROWS_BLK]
            attn_ref[p, :] = total.astype(BF16)
            total = kept_ref[p, :].astype(F32) + total
            for m in range(4):
                part = found[t * ROWS_BLK : (t + 1) * ROWS_BLK, m * LANES : (m + 1) * LANES]
                total = total + jnp.where(lane == m, part, 0.0)
            out_ref[p, :] = total.astype(BF16)
        for source, target in ((attn_ref, attn_hbm), (out_ref, out_hbm)):
            here = pl.ds(i * tile, tile)
            outs.append(pltpu.make_async_copy(source.at[here], target.at[here], sems.at[8 + len(outs)]))
            outs[-1].start()
    for copy in outs:
        copy.wait()


def combine(spot_row, lane_row, last, part, kept, relayed, back):
    rows = part.shape[0]
    slots = back.shape[0] * back.shape[2]
    out = jax.ShapeDtypeStruct((rows, LANES), BF16)
    return pl.pallas_call(
        combine_kernel,
        in_specs=[VMEM] * 3 + [HBM] * 4,
        out_specs=[HBM, HBM],
        out_shape=[out, out],
        scratch_shapes=[
            pltpu.VMEM((back.shape[0], back.shape[2], 4 * LANES), BF16),
            pltpu.VMEM((rows, LANES), F32),
            pltpu.VMEM((rows, LANES), BF16),
            pltpu.VMEM((rows, LANES), BF16),
            pltpu.VMEM((rows, LANES), BF16),
            pltpu.VMEM((rows, LANES), BF16),
            pltpu.SemaphoreType.DMA((8 + 2 * (rows // 256),)),
        ],
        compiler_params=params(60),
        cost_estimate=cost(2 * rows * slots * 4 * LANES, 4 * 2**20),
        name="combine",
    )(spot_row, lane_row, last, part, kept, relayed, back)


def swap(array, change):
    return lax.ppermute(array, "mp", [(i, i ^ change) for i in range(4)])


def exchange(array, axes):
    return lax.all_to_all(array, axes, split_axis=0, concat_axis=0, tiled=True)


def on_device(
    node_features,
    w_qkv,
    w_out,
    head_scale,
    norm_gain,
    router,
    w_gate,
    w_up,
    w_down,
    neighbor_blocks,
    expert_ids,
):
    parts = lax.axis_size("graph")
    part = lax.axis_index("graph")
    me = lax.axis_index("mp")
    rows, width = node_features.shape
    half_cap = CAP_E // 2

    requests = make_requests(neighbor_blocks, parts)
    incoming = exchange(requests.reshape(parts, 1, CAP_H), "graph")
    q, kv = qkv(node_features, w_qkv, head_scale)
    outgoing = pick_blocks(incoming, kv)
    halo = exchange(outgoing, "graph")

    which = me // 2
    me_ref = me[None].astype(jnp.int32)
    kept, given = split_weights(me_ref, w_gate, w_up, w_down, w_out, outgoing)
    weights = [kept, swap(kept, 1), swap(given, 2), swap(given, 3)]

    routed = expert_ids[:, 0]
    experts_all = router.shape[1]
    chosen = routed[:, None] == jnp.arange(experts_all, dtype=jnp.int32)[None, :]
    row_ids = jnp.arange(rows, dtype=jnp.int32)
    earlier = (row_ids[:, None] > row_ids[None, :]).astype(BF16)
    before = jnp.dot(earlier, chosen.astype(BF16), preferred_element_type=F32)
    rank = jnp.sum(jnp.where(chosen, before, 0.0), axis=1).astype(jnp.int32)
    second = (rank >= half_cap).astype(jnp.int32)
    lane = (routed % 2) * 2 + second
    spot = (routed // 2) * half_cap + rank - second * half_cap
    spot_row, lane_row = spot[None, :], lane[None, :]
    mine_row = jnp.where(lane == me, spot, -1)[None, :]
    x_there = exchange(place_rows(mine_row, node_features, parts, half_cap), "graph")

    route = lax.dynamic_index_in_dim(router, 2 * part + which, 1, keepdims=False).astype(F32)[None, :]
    heads, send = attention(
        neighbor_blocks, requests, q, kv, halo, spot_row, lane_row, weights[1:2], parts, half_cap
    )
    send, x_there = lax.optimization_barrier((send, x_there))
    heads_there = exchange(send.reshape(parts * 4, half_cap, LANES), ("graph", "mp"))
    route = hold_route(route, [send] + weights[2:])
    heads, heads_there, route = lax.optimization_barrier((heads, heads_there, route))
    by_one, by_three = swap(heads, 1), swap(heads, 3)
    produced = experts(
        me_ref,
        heads_there.reshape(parts, 4, half_cap, LANES),
        x_there,
        norm_gain[None, :],
        route,
        weights,
        (),
    )
    produced, by_one, by_three = lax.optimization_barrier((produced, by_one, by_three))
    relayed = swap(by_three, 1)
    part, kept_columns, last = attention_columns(
        me_ref, heads, by_one, by_three, weights, node_features
    )
    back = exchange(produced.reshape(parts * 4, half_cap, LANES), ("graph", "mp"))
    attn_out, layer_out = combine(
        spot_row, lane_row, last, part, kept_columns, relayed, back.reshape(parts, 4, half_cap, LANES)
    )
    return (attn_out, layer_out)


def solution(mesh):
    placed = (
        P("graph", None),
        P(None, None, "mp"),
        P("mp", None),
        P("mp"),
        P(),
        P(),
        P("graph", None, "mp"),
        P("graph", None, "mp"),
        P("graph", "mp", None),
        P("graph", None),
        P("graph", None),
    )
    return jax.shard_map(
        on_device,
        mesh=mesh,
        in_specs=placed,
        out_specs=(P("graph", "mp"), P("graph", "mp")),
        check_vma=False,
    )
```
